256 devices in a mesh: gx: 32 (over x, z), gy: 8 (over y, core).
Axes of the slice: x: 4, y: 4, z: 8, core: 2. Of those that a mesh axis runs over, the one named last changes fastest.
Arguments:
- classes: int32 [8192, 16384], P('gy', 'gx'), may hold values from 0 to 7
- exponents: int32 [64, 128], P('gy', 'gx'), may hold values from -1 to 1
- gain_field: bfloat16 [8192, 16384], P('gy', 'gx'), may hold values from 0.5 to 2
- level_table: float32 [8], replicated, may hold values from 0.3 to 1.2
- level_weights: float32 [3], replicated, may hold values from 0.2 to 0.8
Outputs:
- new_dose: float32 [8192, 16384], P('gy', 'gx')
The draws below stay inside these ranges and needn't reach their ends.
All inputs are finite; a program needn't handle non-finite values.
Results may differ from the reference program's by a relative error of at most 0.0003.
The reference program's roundings to bfloat16 on the way count: a program that leaves them out, or rounds other values in their place, can miss the bound.
Values may be sent and summed in bfloat16 or wider, within the bound.
No kernel may reach another device: no remote copies, remote signals or barrier semaphores. Data moves between devices by JAX's collectives and lax.ppermute only.
A program may use at most 64 MiB of HBM per device.

```python
import math
import jax
import jax.numpy as jnp
from jax import lax

HW = 4
CLASSES = 8
SB = 128
ITERS = 4
NR = 8192
NC = 16384


def draw_gain_field(key, part):
    values = jnp.exp(jax.random.uniform(key, (NR, NC), jnp.float32, -0.6931, 0.6931))
    return values.astype(jnp.bfloat16)


def set_ends(array, key, low, largest):
    spot = [jax.random.randint(jax.random.fold_in(key, axis), (), 0, length) for axis, length in enumerate(array.shape)]
    longest = array.shape.index(max(array.shape))
    next_to = spot[:longest] + [(spot[longest] + 1) % array.shape[longest]] + spot[longest + 1:]
    return array.at[tuple(spot)].set(low).at[tuple(next_to)].set(largest)


def setup_inputs(seed: int = 0) -> dict:
    splits = jax.random.split(jax.random.key(seed), 6)
    classes = set_ends(jax.random.randint(splits[0], (NR, NC), 0, CLASSES), jax.random.fold_in(splits[0], 1), 0, CLASSES - 1).astype(jnp.int32)
    exponents = set_ends(jax.random.randint(splits[1], (NR // SB, NC // SB), -1, 2), jax.random.fold_in(splits[1], 1), -1, 1).astype(jnp.int32)
    gain_field = draw_gain_field(jax.random.fold_in(splits[5], 71), 0)
    level_table = jnp.clip(jnp.exp(jax.random.uniform(splits[3], (CLASSES,), jnp.float32, math.log(0.3), math.log(1.2))), 0.3, 1.2)
    level_weights = jnp.clip(jax.random.uniform(splits[4], (3,), jnp.float32, 0.2, 0.8), 0.2, 0.8)
    return dict(classes=classes, exponents=exponents, gain_field=gain_field, level_table=level_table, level_weights=level_weights)


def gauss_taps():
    offsets = jnp.arange(-HW, HW + 1).astype(jnp.float32)
    weights = jnp.exp(-(offsets * offsets) / float(HW * HW))
    return weights / jnp.sum(weights)


def blur_along(values, kernel, axis):
    length = values.shape[axis]
    widths = [(0, 0), (0, 0)]
    widths[axis] = (HW, HW)
    padded = jnp.pad(values, widths)
    summed = jnp.zeros(values.shape, jnp.float32)
    for shift in range(2 * HW + 1):
        summed = summed + kernel[shift] * lax.slice_in_dim(padded, shift, shift + length, axis=axis)
    return summed


def blur_level(values, kernel):
    return blur_along(blur_along(values, kernel, 1), kernel, 0)


def pool_level(values, factor):
    height, breadth = values.shape
    blocks = values.reshape(height // factor, factor, breadth // factor, factor)
    return jnp.sum(blocks, axis=(1, 3)) / float(factor * factor)


def upsample_along(values, factor, axis):
    length = values.shape[axis]
    target = jnp.arange(length * factor, dtype=jnp.int32)
    lower = (target - factor // 2) // factor
    fraction = ((target - factor // 2 - factor * lower).astype(jnp.float32) + 0.5) / factor
    low_vals = jnp.take(values, jnp.clip(lower, 0, length - 1).astype(jnp.int32), axis=axis)
    high_vals = jnp.take(values, jnp.clip(lower + 1, 0, length - 1).astype(jnp.int32), axis=axis)
    shape = [1, 1]
    shape[axis] = length * factor
    fraction = fraction.reshape(shape)
    return (1.0 - fraction) * low_vals + fraction * high_vals


def upsample(values, factor):
    return upsample_along(upsample_along(values, factor, 0), factor, 1)


def reference(classes, exponents, gain_field, level_table, level_weights):
    level = jnp.zeros((NR, NC), jnp.float32)
    for class_id in range(1, CLASSES):
        level = jnp.where(classes == class_id, level_table[class_id], level)
    scale = jnp.exp2(exponents.astype(jnp.float32))
    scaled = (level.reshape(NR // SB, SB, NC // SB, SB) * scale[:, None, :, None]).reshape(NR, NC)
    dose = (scaled * gain_field.astype(jnp.float32)).astype(jnp.bfloat16)
    kernel = gauss_taps()
    kernel_fine = kernel.astype(jnp.bfloat16).astype(jnp.float32)
    updated = jnp.zeros((NR, NC), jnp.float32)
    for sweep in range(ITERS):
        dose_values = dose.astype(jnp.float32)
        half = blur_along(dose_values, kernel_fine, 1).astype(jnp.bfloat16)
        short_range = blur_along(half.astype(jnp.float32), kernel_fine, 0)
        second = pool_level(dose_values, 16)
        third = pool_level(second, 4)
        fourth = pool_level(third, 4)
        fog = jnp.mean(fourth)
        fourth_term = level_weights[2] * (blur_level(fourth, kernel) + fog)
        third_term = level_weights[1] * blur_level(third, kernel) + upsample(fourth_term, 4)
        second_term = level_weights[0] * blur_level(second, kernel) + upsample(third_term, 4)
        backscatter = upsample(second_term, 16)
        updated = dose_values * 2.0 / (1.0 + (short_range + backscatter))
        dose = updated.astype(jnp.bfloat16)
    return updated
```

```python
import functools

import jax
import jax.numpy as jnp
import ml_dtypes
import numpy as np
from jax import lax
from jax.experimental import pallas as pl
from jax.experimental.pallas import tpu as pltpu
from jax.sharding import PartitionSpec as P

HW = 4
CLASSES = 8
SB = 128
ITERS = 4
NX, NY = 32, 8
TR, TC = 1024, 512
HALO = HW * ITERS
ER = TR + 2 * HALO
EC = TC + 128
BLK = 176
NB = ER // BLK
QC, QR = 36, 68
F32, BF16 = jnp.float32, jnp.bfloat16
EXACT = lax.Precision.HIGHEST


def gauss_taps():
    offsets = np.arange(-HW, HW + 1).astype(np.float32)
    weights = np.exp(-(offsets * offsets) / np.float32(HW * HW)).astype(np.float32)
    return weights / weights.sum(dtype=np.float32)


def blur_operator(n):
    taps = gauss_taps().astype(np.float64)
    out = np.zeros((n, n))
    for k in range(-HW, HW + 1):
        out += taps[k + HW] * np.eye(n, k=k)
    return out


def up_operator(n, factor):
    target = np.arange(n * factor)
    lower = (target - factor // 2) // factor
    t = (target - factor // 2 - factor * lower + 0.5) / factor
    out = np.zeros((n * factor, n))
    np.add.at(out, (target, np.clip(lower, 0, n - 1)), 1 - t)
    np.add.at(out, (target, np.clip(lower + 1, 0, n - 1)), t)
    return out


def level_operators(n_second):
    third, fourth = n_second // 4, n_second // 16
    return (
        blur_operator(n_second),
        up_operator(third, 4) @ blur_operator(third),
        up_operator(third, 4) @ up_operator(fourth, 4) @ blur_operator(fourth),
    )


@functools.cache
def column_matrices():
    second, third, fourth = level_operators(NX * 32)
    got = np.zeros((NX, 128, 256), np.float32)
    own = np.zeros((NX, 128, 32), np.float32)
    for px in range(NX):
        for q in range(QC):
            g = min(max(32 * px + q - 2, 0), NX * 32 - 1)
            for s in np.nonzero(second[g])[0]:
                p, j = divmod(int(s), 32)
                if p == px:
                    own[px, q, j] = second[g, s]
                else:
                    assert j >= 24 if p < px else j < 8
                    got[px, q, p * 8 + j % 8] = second[g, s]
            got[px, 40 + q] = third[g]
            for j in range(2):
                got[px, 80 + q, j::8] = fourth[g, j::2]
        got[px, 120, 0::8] = 1
        got[px, 120, 1::8] = 1
    return got, own


def row_matrices(groups, first, step, length):
    second, third, fourth = level_operators(NY * 64)
    m = 16 * groups
    out = np.zeros((NY, 3 * m + 8, 192), np.float32)
    for py in range(NY):
        for b in range(groups):
            for k in range(length):
                row, q = b * 16 + k, first + step * b + k
                g = min(max(64 * py + q - 2, 0), NY * 64 - 1)
                for s in np.nonzero(second[g])[0]:
                    p, j = divmod(int(s), 64)
                    assert p == py or (j >= 56 if p < py else j < 8)
                    out[py, row, 64 + j if p == py else p * 8 + j % 8] = second[g, s]
                for s in np.nonzero(third[g])[0]:
                    p, j = divmod(int(s), 16)
                    assert p == py or (j >= 8 if p < py else j < 8)
                    out[py, m + row, 128 + j if p == py else p * 8 + j % 8] = third[g, s]
                for s in np.nonzero(fourth[g])[0]:
                    p, j = divmod(int(s), 4)
                    out[py, 2 * m + row, p * 8 + j] = fourth[g, s]
        out[py, 3 * m, 4:64:8] = 1
    return out


@functools.cache
def column_spread():
    out = np.zeros((128, EC), np.float32)
    for lane in range(EC):
        cell = lane if lane < TC + HALO else lane - EC
        if cell < -HALO:
            continue
        lower = (cell - 8) // 16
        t = (cell - 8 - 16 * lower + 0.5) / 16
        for level in range(3):
            out[40 * level + lower + 2, lane] += 1 - t
            out[40 * level + lower + 3, lane] += t
        out[120, lane] = 1
    return out


@functools.cache
def column_pool(lanes):
    out = np.zeros((lanes, 128), np.float32)
    cell = np.arange(TC)
    out[cell, cell // 16] = 1
    out[cell, 32 + cell // 64] = 1
    out[cell, 40 + cell // 256] = 1
    return out.astype(ml_dtypes.bfloat16)


@functools.cache
def row_pool(groups, stride, real, first):
    out = np.zeros((128, groups * stride), np.float32)
    for b in range(groups):
        for k in range(real):
            s = b * real + k - first
            if 0 <= s < TR // 16:
                at = b * stride + k
                out[s, at] = 2.0**-8
                out[64 + s // 4, at] = 2.0**-12
                out[80 + s // 16, at] = 2.0**-16
                out[84, at] = 1.0 / (TR * NY * TC * NX)
    return out


def fine_taps():
    return gauss_taps().astype(ml_dtypes.bfloat16)


@functools.cache
def fine_columns():
    out = np.zeros((EC, EC), ml_dtypes.bfloat16)
    taps, lane = fine_taps(), np.arange(EC)
    for k in range(-HW, HW + 1):
        out[(lane + k) % EC, lane] = taps[k + HW]
    return out


@functools.cache
def fine_rows():
    out = np.zeros((3, BLK, BLK + 32), ml_dtypes.bfloat16)
    taps = fine_taps()
    for which in range(3):
        for r in range(BLK):
            for k in range(-HW, HW + 1):
                c = r + 16 * which + k
                if 0 <= c < BLK + 32:
                    out[which, r, c] = taps[k + HW]
    return out


def params(mib=24):
    return pltpu.CompilerParams(vmem_limit_bytes=mib * 2**20)


def dot(a, b, **kw):
    return jnp.dot(a, b, preferred_element_type=F32, **kw)


def pooled_out(sums, row_pool_ref, px, send_ref, own_ref):
    pooled = dot(row_pool_ref[...], sums, precision=EXACT).T
    own_ref[...] = pooled
    lane = lax.broadcasted_iota(jnp.int32, (8, 128), 1)
    coarse = jnp.where(lane < 80, pooled[32:40], pooled[40:48])
    left = jnp.where(lane < 64, pooled[0:8], coarse)
    right = jnp.where(lane < 64, pooled[24:32], coarse)
    for p in range(NX):
        send_ref[p] = jnp.where(p < px, left, right)


def start_kernel(place, table, exps, classes, gain, cpool, rpool, dose, lo, hi, send, own, sums):
    i = pl.program_id(0)
    for n in range(TC // SB):
        e = exps[i, n]
        scale = jnp.where(e > 0, 2.0, jnp.where(e < 0, 0.5, 1.0)).astype(F32)
        at = slice(n * SB, (n + 1) * SB)
        c = classes[:, at]
        level = jnp.zeros((SB, SB), F32)
        for k in range(1, CLASSES):
            level = jnp.where(c == k, table[k] * scale, level)
        value = (level * gain[:, at].astype(F32)).astype(BF16)
        dose[:, at] = value
        if n == 0:
            lo[...] = value.astype(F32).T[:HALO].astype(BF16)
        if n == TC // SB - 1:
            hi[...] = value.astype(F32).T[SB - HALO :].astype(BF16)
    across = dot(dose[...], cpool[...])
    sums[i] = jnp.sum(across.reshape(8, 16, 128), axis=1)

    @pl.when(i == TR // SB - 1)
    def _():
        pooled_out(sums[...].reshape(64, 128), rpool, place[0], send, own)


def start(place, table, exps, classes, gain):
    steps = TR // SB
    whole = lambda *shape: pl.BlockSpec(shape, lambda i, s: (0,) * len(shape))
    strip = pl.BlockSpec((HALO, SB), lambda i, s: (0, i))
    return pl.pallas_call(
        start_kernel,
        grid_spec=pltpu.PrefetchScalarGridSpec(
            num_scalar_prefetch=1,
            grid=(steps,),
            in_specs=[
                pl.BlockSpec(memory_space=pltpu.SMEM),
                pl.BlockSpec(memory_space=pltpu.SMEM),
                pl.BlockSpec((SB, TC), lambda i, s: (i, 0)),
                pl.BlockSpec((SB, TC), lambda i, s: (i, 0)),
                whole(TC, 128),
                whole(128, 64),
            ],
            out_specs=[
                pl.BlockSpec((SB, TC), lambda i, s: (i, 0)),
                strip,
                strip,
                whole(NX, 8, 128),
                whole(128, 128),
            ],
            scratch_shapes=[pltpu.VMEM((steps, 8, 128), F32)],
        ),
        out_shape=[
            jax.ShapeDtypeStruct((TR, TC), BF16),
            jax.ShapeDtypeStruct((HALO, TR), BF16),
            jax.ShapeDtypeStruct((HALO, TR), BF16),
            jax.ShapeDtypeStruct((NX, 8, 128), F32),
            jax.ShapeDtypeStruct((128, 128), F32),
        ],
        compiler_params=params(),
        name="start",
    )(place, table, exps, classes, gain, column_pool(TC), row_pool(8, 8, 8, 0))


def across_kernel(place, got, own, mgot, mown, send, part):
    z = dot(mgot[0], got[...], precision=EXACT) + dot(mown[0], own[:32], precision=EXACT)
    z = z.T
    part[...] = z
    lane = lax.broadcasted_iota(jnp.int32, (8, 128), 1)
    coarse = z[80:88]
    up = jnp.where(lane < 40, z[0:8], jnp.where(lane < 80, z[64:72], coarse))
    down = jnp.where(lane < 40, z[56:64], jnp.where(lane < 80, z[72:80], coarse))
    for p in range(NY):
        send[p] = jnp.where(p < place[1], up, down)


def across(place, got, own):
    mgot, mown = column_matrices()
    whole = lambda *shape: pl.BlockSpec(shape, lambda i, s: (0,) * len(shape))
    mine = lambda *shape: pl.BlockSpec((1, *shape), lambda i, s: (s[0],) + (0,) * len(shape))
    return pl.pallas_call(
        across_kernel,
        grid_spec=pltpu.PrefetchScalarGridSpec(
            num_scalar_prefetch=1,
            grid=(1,),
            in_specs=[whole(256, 128), whole(128, 128), mine(128, 256), mine(128, 32)],
            out_specs=[whole(NY, 8, 128), whole(128, 128)],
        ),
        out_shape=[
            jax.ShapeDtypeStruct((NY, 8, 128), F32),
            jax.ShapeDtypeStruct((128, 128), F32),
        ],
        compiler_params=params(),
        name="across",
    )(place, got.reshape(NX * 8, 128), own, mgot, mown)


def side(strip_lo, strip_hi):
    rows = strip_lo.shape[1]
    empty = jnp.zeros((rows, 128 - 2 * HALO), F32)
    return jnp.concatenate([strip_hi.astype(F32).T, empty, strip_lo.astype(F32).T], axis=1).astype(BF16)


def edges_kernel(dose_top, dose_bottom, lo_top, hi_top, lo_bottom, hi_bottom, top, bottom):
    top[:, :TC] = dose_top[...]
    top[:, TC:] = side(lo_top[...], hi_top[...])[:HALO]
    bottom[:, :TC] = dose_bottom[...]
    bottom[:, TC:] = side(lo_bottom[...], hi_bottom[...])[128 - HALO :]


def edges(dose, lo, hi):
    first, last = TR // HALO - 1, TR // 128 - 1
    return pl.pallas_call(
        edges_kernel,
        grid=(1,),
        in_specs=[
            pl.BlockSpec((HALO, TC), lambda i: (0, 0)),
            pl.BlockSpec((HALO, TC), lambda i: (first, 0)),
            pl.BlockSpec((HALO, 128), lambda i: (0, 0)),
            pl.BlockSpec((HALO, 128), lambda i: (0, 0)),
            pl.BlockSpec((HALO, 128), lambda i: (0, last)),
            pl.BlockSpec((HALO, 128), lambda i: (0, last)),
        ],
        out_specs=[pl.BlockSpec((HALO, EC), lambda i: (0, 0))] * 2,
        out_shape=[jax.ShapeDtypeStruct((HALO, EC), BF16)] * 2,
        compiler_params=params(),
        name="edges",
    )(dose, dose, lo, hi, lo, hi)


def assemble_kernel(dose, lo, hi, above, below, out):
    out[:HALO] = above[...]
    out[HALO + TR :] = below[...]
    out[HALO : HALO + TR, :TC] = dose[...]
    for n in range(TR // 128):
        at = slice(n * 128, (n + 1) * 128)
        out[HALO + n * 128 : HALO + (n + 1) * 128, TC:] = side(lo[:, at], hi[:, at])


def assemble(dose, lo, hi, above, below):
    return pl.pallas_call(
        assemble_kernel,
        out_shape=jax.ShapeDtypeStruct((ER, EC), BF16),
        compiler_params=params(),
        name="assemble",
    )(dose, lo, hi, above, below)


def fine_kernel(last, dose, cols, rows, *refs):
    out, half = refs[0], refs[-1]
    for b in range(NB):
        at = slice(b * BLK, (b + 1) * BLK)
        half[at] = dot(dose[at], cols[...]).astype(BF16)
    for b in range(NB):
        first = min(max(b * BLK - 16, 0), ER - BLK - 32)
        which = (b * BLK - first) // 16
        values = half[first : first + BLK + 32]
        if last:
            got = dot(rows[which], values[:, :TC])
            begin, end = max(b * BLK, HALO), min((b + 1) * BLK, HALO + TR)
            out[begin - HALO : end - HALO] = got[begin - b * BLK : end - b * BLK]
        else:
            out[b * BLK : (b + 1) * BLK] = dot(rows[which], values)
    if last:
        refs[1][...] = dose[HALO : HALO + TR, :TC]


def fine(dose, last):
    if last:
        shapes = [jax.ShapeDtypeStruct((TR, TC), F32), jax.ShapeDtypeStruct((TR, TC), BF16)]
    else:
        shapes = [jax.ShapeDtypeStruct((ER, EC), F32)]
    return pl.pallas_call(
        functools.partial(fine_kernel, last),
        out_shape=shapes,
        scratch_shapes=[pltpu.VMEM((ER, EC), BF16)],
        compiler_params=params(),
        cost_estimate=pl.CostEstimate(flops=2 * ER * EC * (EC + 208), bytes_accessed=6 * ER * EC, transcendentals=0),
        name="fine",
    )(dose, fine_columns(), fine_rows())


def spread(weights, got, part, matrix, cols, grid, groups):
    m = 16 * groups
    stacked = jnp.concatenate([got[...], part[...]], axis=0)
    y = dot(matrix[0], stacked, precision=EXACT)
    lane = lax.broadcasted_iota(jnp.int32, (m, 128), 1)
    fourth = jnp.where(lane < 120, y[2 * m : 3 * m], jnp.where(lane == 120, y[3 * m : 3 * m + 1], 0.0))
    terms = jnp.where(
        lane < 40,
        weights[0] * y[:m],
        jnp.where(lane < 80, weights[1] * y[m : 2 * m], weights[2] * fourth),
    )
    grid[...] = dot(terms, cols[...], precision=EXACT).reshape(grid.shape)


def update(b, rows, dose, short, grid, out):
    lanes = dose.shape[1]
    t = (lax.broadcasted_iota(jnp.int32, (8, lanes), 0).astype(F32) + 0.5) / 16.0
    for n in range(rows // 16):
        at = slice(16 * n, 16 * n + 16)
        a, m, c = (grid[b, n + k : n + k + 1] for k in range(3))
        back = jnp.concatenate([a + (t + 0.5) * (m - a), m + t * (c - m)], axis=0)
        out[at] = (dose[at].astype(F32) * 2.0 / (1.0 + (short[at] + back))).astype(out.dtype)


def step_kernel(place, weights, got, part, matrix, cols, dose, short, cpool, rpool, out, send, own, grid, sums):
    b = pl.program_id(0)

    @pl.when(b == 0)
    def _():
        spread(weights, got, part, matrix, cols, grid, NB)

    update(b, BLK, dose, short, grid, out)
    pooled = dot(out[...], cpool[...])
    pooled = jnp.sum(pooled.reshape(BLK // 16, 16, 128), axis=1)
    sums[b] = jnp.concatenate([pooled, jnp.zeros((16 - BLK // 16, 128), F32)], axis=0)

    @pl.when(b == NB - 1)
    def _():
        pooled_out(sums[...].reshape(NB * 16, 128), rpool, place[0], send, own)


def step(place, weights, got, part, dose, short):
    whole = lambda *shape: pl.BlockSpec(shape, lambda i, s: (0,) * len(shape))
    block = pl.BlockSpec((BLK, EC), lambda i, s: (i, 0))
    m = 3 * 16 * NB + 8
    return pl.pallas_call(
        step_kernel,
        grid_spec=pltpu.PrefetchScalarGridSpec(
            num_scalar_prefetch=1,
            grid=(NB,),
            in_specs=[
                pl.BlockSpec(memory_space=pltpu.SMEM),
                whole(NY * 8, 128),
                whole(128, 128),
                pl.BlockSpec((1, m, 192), lambda i, s: (s[1], 0, 0)),
                whole(128, EC),
                block,
                block,
                whole(EC, 128),
                whole(128, NB * 16),
            ],
            out_specs=[block, whole(NX, 8, 128), whole(128, 128)],
            scratch_shapes=[pltpu.VMEM((NB, 16, EC), F32), pltpu.VMEM((NB, 16, 128), F32)],
        ),
        out_shape=[
            jax.ShapeDtypeStruct((ER, EC), BF16),
            jax.ShapeDtypeStruct((NX, 8, 128), F32),
            jax.ShapeDtypeStruct((128, 128), F32),
        ],
        compiler_params=params(),
        name="step",
    )(
        place, weights, got.reshape(NY * 8, 128), part, row_matrices(NB, 0, BLK // 16, BLK // 16 + 2),
        column_spread(), dose, short, column_pool(EC), row_pool(NB, 16, BLK // 16, 1),
    )


def finish_kernel(place, weights, got, part, matrix, cols, dose, short, out, grid):
    b = pl.program_id(0)

    @pl.when(b == 0)
    def _():
        spread(weights, got, part, matrix, cols, grid, TR // SB)

    update(b, SB, dose, short, grid, out)


def finish(place, weights, got, part, dose, short):
    whole = lambda *shape: pl.BlockSpec(shape, lambda i, s: (0,) * len(shape))
    block = pl.BlockSpec((SB, TC), lambda i, s: (i, 0))
    groups = TR // SB
    return pl.pallas_call(
        finish_kernel,
        grid_spec=pltpu.PrefetchScalarGridSpec(
            num_scalar_prefetch=1,
            grid=(groups,),
            in_specs=[
                pl.BlockSpec(memory_space=pltpu.SMEM),
                whole(NY * 8, 128),
                whole(128, 128),
                pl.BlockSpec((1, 3 * 16 * groups + 8, 192), lambda i, s: (s[1], 0, 0)),
                whole(128, TC),
                block,
                block,
            ],
            out_specs=block,
            scratch_shapes=[pltpu.VMEM((groups, 16, TC), F32)],
        ),
        out_shape=jax.ShapeDtypeStruct((TR, TC), F32),
        compiler_params=params(),
        name="finish",
    )(
        place, weights, got.reshape(NY * 8, 128), part, row_matrices(groups, 1, SB // 16, SB // 16 + 2),
        column_spread()[:, :TC], dose, short,
    )


def shifted(x, axis, by):
    n = lax.axis_size(axis)
    return lax.ppermute(x, axis, [(i, i + by) for i in range(n) if 0 <= i + by < n])


def exchanged(x, axis):
    return lax.all_to_all(x, axis, 0, 0, tiled=True)


def local(classes, exponents, gain_field, level_table, level_weights):
    place = jnp.stack([lax.axis_index("gx"), lax.axis_index("gy")]).astype(jnp.int32)
    tile, lo, hi, send, own = start(place, level_table, exponents, classes, gain_field)
    left, right = shifted(hi, "gx", 1), shifted(lo, "gx", -1)
    got = exchanged(send, "gx")
    top, bottom = edges(tile, left, right)
    above, below = shifted(bottom, "gy", 1), shifted(top, "gy", -1)
    send, part = across(place, got, own)
    got = exchanged(send, "gy")
    dose = assemble(tile, left, right, above, below)
    (short,) = fine(dose, False)
    for sweep in range(1, ITERS):
        dose, send, own = step(place, level_weights, got, part, dose, short)
        got = exchanged(send, "gx")
        last = sweep == ITERS - 1
        blurred = fine(dose, last)
        short = blurred[0]
        if last:
            dose = blurred[1]
        send, part = across(place, got, own)
        got = exchanged(send, "gy")
    return finish(place, level_weights, got, part, dose, short)


def solution(mesh):
    in_specs = (P("gy", "gx"), P("gy", "gx"), P("gy", "gx"), P(), P())
    return jax.shard_map(local, mesh=mesh, in_specs=in_specs, out_specs=P("gy", "gx"), check_vma=False)
```

```python
import functools

import jax
import jax.numpy as jnp
import ml_dtypes
import numpy as np
from jax import lax
from jax.experimental import pallas as pl
from jax.experimental.pallas import tpu as pltpu
from jax.sharding import PartitionSpec as P

HW = 4
CLASSES = 8
SB = 128
ITERS = 4
NX, NY = 32, 8
TR, TC = 1024, 512
HALO = HW * ITERS
ER = TR + 2 * HALO
EC = TC + 128
BLK = 176
NB = ER // BLK
QC, QR = 36, 68
F32, BF16 = jnp.float32, jnp.bfloat16
EXACT = lax.Precision.HIGHEST


def gauss_taps():
    offsets = np.arange(-HW, HW + 1).astype(np.float32)
    weights = np.exp(-(offsets * offsets) / np.float32(HW * HW)).astype(np.float32)
    return weights / weights.sum(dtype=np.float32)


def blur_operator(n):
    taps = gauss_taps().astype(np.float64)
    out = np.zeros((n, n))
    for k in range(-HW, HW + 1):
        out += taps[k + HW] * np.eye(n, k=k)
    return out


def up_operator(n, factor):
    target = np.arange(n * factor)
    lower = (target - factor // 2) // factor
    t = (target - factor // 2 - factor * lower + 0.5) / factor
    out = np.zeros((n * factor, n))
    np.add.at(out, (target, np.clip(lower, 0, n - 1)), 1 - t)
    np.add.at(out, (target, np.clip(lower + 1, 0, n - 1)), t)
    return out


def level_operators(n_second):
    third, fourth = n_second // 4, n_second // 16
    return (
        blur_operator(n_second),
        up_operator(third, 4) @ blur_operator(third),
        up_operator(third, 4) @ up_operator(fourth, 4) @ blur_operator(fourth),
    )


@functools.cache
def column_matrices():
    second, third, fourth = level_operators(NX * 32)
    got = np.zeros((NX, 128, 256), np.float32)
    own = np.zeros((NX, 128, 32), np.float32)
    for px in range(NX):
        for q in range(QC):
            g = min(max(32 * px + q - 2, 0), NX * 32 - 1)
            for s in np.nonzero(second[g])[0]:
                p, j = divmod(int(s), 32)
                if p == px:
                    own[px, q, j] = second[g, s]
                else:
                    assert j >= 24 if p < px else j < 8
                    got[px, q, p * 8 + j % 8] = second[g, s]
            got[px, 40 + q] = third[g]
            for j in range(2):
                got[px, 80 + q, j::8] = fourth[g, j::2]
        got[px, 120, 0::8] = 1
        got[px, 120, 1::8] = 1
    return got, own


def row_matrices(groups, first, step, length):
    second, third, fourth = level_operators(NY * 64)
    m = 16 * groups
    out = np.zeros((NY, 3 * m + 8, 192), np.float32)
    for py in range(NY):
        for b in range(groups):
            for k in range(length):
                row, q = b * 16 + k, first + step * b + k
                g = min(max(64 * py + q - 2, 0), NY * 64 - 1)
                for s in np.nonzero(second[g])[0]:
                    p, j = divmod(int(s), 64)
                    assert p == py or (j >= 56 if p < py else j < 8)
                    out[py, row, 64 + j if p == py else p * 8 + j % 8] = second[g, s]
                for s in np.nonzero(third[g])[0]:
                    p, j = divmod(int(s), 16)
                    assert p == py or (j >= 8 if p < py else j < 8)
                    out[py, m + row, 128 + j if p == py else p * 8 + j % 8] = third[g, s]
                for s in np.nonzero(fourth[g])[0]:
                    p, j = divmod(int(s), 4)
                    out[py, 2 * m + row, p * 8 + j] = fourth[g, s]
        out[py, 3 * m, 4:64:8] = 1
    return out


@functools.cache
def column_spread():
    out = np.zeros((128, EC), np.float32)
    for lane in range(EC):
        cell = lane if lane < TC + HALO else lane - EC
        if cell < -HALO:
            continue
        lower = (cell - 8) // 16
        t = (cell - 8 - 16 * lower + 0.5) / 16
        for level in range(3):
            out[40 * level + lower + 2, lane] += 1 - t
            out[40 * level + lower + 3, lane] += t
        out[120, lane] = 1
    return out.astype(ml_dtypes.bfloat16)


@functools.cache
def column_pool(lanes):
    out = np.zeros((lanes, 128), np.float32)
    cell = np.arange(TC)
    out[cell, cell // 16] = 1
    out[cell, 32 + cell // 64] = 1
    out[cell, 40 + cell // 256] = 1
    return out.astype(ml_dtypes.bfloat16)


@functools.cache
def row_pool(groups, stride, real, first):
    out = np.zeros((128, groups * stride), np.float32)
    for b in range(groups):
        for k in range(real):
            s = b * real + k - first
            if 0 <= s < TR // 16:
                at = b * stride + k
                out[s, at] = 2.0**-8
                out[64 + s // 4, at] = 2.0**-12
                out[80 + s // 16, at] = 2.0**-16
                out[84, at] = 1.0 / (TR * NY * TC * NX)
    return out.astype(ml_dtypes.bfloat16)


def fine_taps():
    return gauss_taps().astype(ml_dtypes.bfloat16)


@functools.cache
def fine_columns():
    out = np.zeros((512, 256), ml_dtypes.bfloat16)
    taps, lane = fine_taps(), np.arange(256)
    for k in range(-HW, HW + 1):
        out[lane + 128 + k, lane] = taps[k + HW]
    return out


@functools.cache
def fine_rows():
    out = np.zeros((3, BLK, BLK + 32), ml_dtypes.bfloat16)
    taps = fine_taps()
    for which in range(3):
        for r in range(BLK):
            for k in range(-HW, HW + 1):
                c = r + 16 * which + k
                if 0 <= c < BLK + 32:
                    out[which, r, c] = taps[k + HW]
    return out


VMEM = pl.BlockSpec(memory_space=pltpu.VMEM)
SMEM = pl.BlockSpec(memory_space=pltpu.SMEM)
HBM = pl.BlockSpec(memory_space=pl.ANY)
DMA = pltpu.SemaphoreType.DMA


def params(mib=24):
    return pltpu.CompilerParams(vmem_limit_bytes=mib * 2**20)


def near(x):
    return pltpu.with_memory_space_constraint(x, pltpu.VMEM)


def far(x):
    return pltpu.with_memory_space_constraint(x, pltpu.HBM)


def dot(a, b, **kw):
    return jnp.dot(a, b, preferred_element_type=F32, **kw)


def pieces(x):
    first = x.astype(BF16)
    rest = x - first.astype(F32)
    second = rest.astype(BF16)
    return first, second, (rest - second.astype(F32)).astype(BF16)


def pooled_out(sums, row_pool_ref, px, send_ref, own_ref):
    a, b, c = pieces(sums)
    rows = row_pool_ref[...]
    pooled = (dot(rows, a) + dot(rows, b) + dot(rows, c)).T
    own_ref[...] = pooled
    lane = lax.broadcasted_iota(jnp.int32, (8, 128), 1)
    coarse = jnp.where(lane < 80, pooled[32:40], pooled[40:48])
    left = jnp.where(lane < 64, pooled[0:8], coarse)
    right = jnp.where(lane < 64, pooled[24:32], coarse)
    for p in range(NX):
        send_ref[p] = jnp.where(p < px, left, right)


def operators():
    mgot, mown = column_matrices()
    return [
        (row_matrices(NB, 0, BLK // 16, BLK // 16 + 2), 1),
        (row_matrices(TR // SB, 1, SB // 16, SB // 16 + 2), 1),
        (mgot, 0),
        (mown, 0),
        (column_spread(), None),
        (column_pool(EC), None),
        (row_pool(NB, 16, BLK // 16, 1), None),
        (fine_columns(), None),
        (fine_rows(), None),
    ]


def start_kernel(picks, weights, table, exps, classes, gain, cpool, rpool, *refs):
    n, steps = len(picks), TR // SB
    tables, outs = refs[:n], refs[n + 7 : 2 * n + 7]
    dose, top, bottom, lo, hi, send, own = refs[n : n + 7]
    cbuf, gbuf, made, sums, csem, gsem, tsem, dsem = refs[2 * n + 7 :]
    place = lax.axis_index("gx"), lax.axis_index("gy")
    loads = []
    for i in range(steps):
        rows = pl.ds(i * SB, SB)
        loads.append(
            (
                pltpu.make_async_copy(classes.at[rows], cbuf.at[rows], csem.at[i]),
                pltpu.make_async_copy(gain.at[rows], gbuf.at[rows], gsem.at[i]),
            )
        )
        for copy in loads[-1]:
            copy.start()
    copies = []
    for i, pick in enumerate(picks):
        source = tables[i] if pick is None else tables[i].at[place[pick]]
        copies.append(pltpu.make_async_copy(source, outs[i], tsem.at[i]))
        copies[-1].start()
    stores = []
    for i in range(steps):
        for copy in loads[i]:
            copy.wait()
        rows = slice(i * SB, (i + 1) * SB)
        for k in range(TC // SB):
            e = exps[i, k]
            scale = jnp.where(e > 0, 2.0, jnp.where(e < 0, 0.5, 1.0)).astype(F32)
            at = slice(k * SB, (k + 1) * SB)
            c = cbuf[rows, at]
            level = jnp.zeros((SB, SB), F32)
            for j in range(1, CLASSES):
                level = jnp.where(c == j, table[j] * scale, level)
            value = (level * gbuf[rows, at].astype(F32)).astype(BF16)
            made[rows, at] = value
            if k == 0:
                lo[:, rows] = value.astype(F32).T[:HALO].astype(BF16)
            if k == TC // SB - 1:
                hi[:, rows] = value.astype(F32).T[SB - HALO :].astype(BF16)
        stores.append(pltpu.make_async_copy(made.at[rows], dose.at[rows], dsem.at[i]))
        stores[-1].start()
        across = dot(made[rows], cpool[...])
        sums[8 * i : 8 * i + 8] = jnp.sum(across.reshape(8, 16, 128), axis=1)
    top[...] = made[:HALO]
    bottom[...] = made[TR - HALO :]
    pooled_out(sums[...], rpool, place[0], send, own)
    for copy in copies:
        copy.wait()
    for ref, m in ((outs[0], 16 * NB), (outs[1], TR // SB * 16)):
        for level in range(3):
            at = slice(m * level, m * (level + 1))
            ref[at] = ref[at] * weights[level]
        ref[3 * m :] = ref[3 * m :] * weights[2]
    for copy in stores:
        copy.wait()


def start(weights, table, exps, classes, gain):
    made = operators()
    picks = [pick for _, pick in made]
    outs = [pltpu.VMEM(t.shape if pick is None else t.shape[1:], t.dtype) for t, pick in made]
    steps = TR // SB
    got = pl.pallas_call(
        functools.partial(start_kernel, picks),
        in_specs=[SMEM, SMEM, SMEM, HBM, HBM, VMEM, VMEM] + [HBM] * len(made),
        out_specs=[HBM] + [VMEM] * (6 + len(made)),
        out_shape=[
            pltpu.HBM((TR, TC), BF16),
            pltpu.VMEM((HALO, TC), BF16),
            pltpu.VMEM((HALO, TC), BF16),
            pltpu.VMEM((HALO, TR), BF16),
            pltpu.VMEM((HALO, TR), BF16),
            pltpu.VMEM((NX, 8, 128), F32),
            pltpu.VMEM((128, 128), F32),
            *outs,
        ],
        scratch_shapes=[
            pltpu.VMEM((TR, TC), jnp.int32),
            pltpu.VMEM((TR, TC), BF16),
            pltpu.VMEM((TR, TC), BF16),
            pltpu.VMEM((TR // 16, 128), F32),
            DMA((steps,)),
            DMA((steps,)),
            DMA((len(made),)),
            DMA((steps,)),
        ],
        compiler_params=params(),
        name="start",
    )(
        weights, table, exps, far(classes), far(gain), column_pool(TC), row_pool(8, 8, 8, 0),
        *[far(jnp.asarray(t)) for t, _ in made],
    )
    return got[:7], got[7:]


def across_kernel(got, own, mgot, mown, send, part):
    received = got[...].reshape(NX * 8, 128)
    z = dot(mgot[...], received, precision=EXACT) + dot(mown[...], own[:32], precision=EXACT)
    z = z.T
    part[...] = z
    lane = lax.broadcasted_iota(jnp.int32, (8, 128), 1)
    coarse = z[80:88]
    up = jnp.where(lane < 40, z[0:8], jnp.where(lane < 80, z[64:72], coarse))
    down = jnp.where(lane < 40, z[56:64], jnp.where(lane < 80, z[72:80], coarse))
    py = lax.axis_index("gy")
    for p in range(NY):
        send[p] = jnp.where(p < py, up, down)


def across(got, own, ops):
    return pl.pallas_call(
        across_kernel,
        in_specs=[VMEM] * 4,
        out_specs=[VMEM] * 2,
        out_shape=[pltpu.VMEM((NY, 8, 128), F32), pltpu.VMEM((128, 128), F32)],
        compiler_params=params(),
        name="across",
    )(near(got), near(own), near(ops[2]), near(ops[3]))


def side(strip_lo, strip_hi):
    rows = strip_lo.shape[1]
    empty = jnp.zeros((rows, 128 - 2 * HALO), F32)
    return jnp.concatenate([strip_hi.astype(F32).T, empty, strip_lo.astype(F32).T], axis=1).astype(BF16)


def edges_kernel(first, final, lo, hi, top, bottom):
    top[:, :TC] = first[...]
    top[:, TC:] = side(lo[:, :128], hi[:, :128])[:HALO]
    bottom[:, :TC] = final[...]
    bottom[:, TC:] = side(lo[:, TR - 128 :], hi[:, TR - 128 :])[128 - HALO :]


def edges(first, final, lo, hi):
    return pl.pallas_call(
        edges_kernel,
        in_specs=[VMEM] * 4,
        out_specs=[VMEM] * 2,
        out_shape=[pltpu.VMEM((HALO, EC), BF16)] * 2,
        compiler_params=params(),
        name="edges",
    )(near(first), near(final), near(lo), near(hi))


def fine_blocks(last, wait, values, cols, rows, half, out_ref, store):
    def across_block(b):
        wait(b)
        block = values[b * BLK : (b + 1) * BLK]
        tile = [block[:, 128 * n : 128 * (n + 1)] for n in range(5)]
        join = lambda *which: jnp.concatenate([tile[n] for n in which], axis=1)
        at = slice(b * BLK, (b + 1) * BLK)
        half[at, :256] = dot(join(4, 0, 1, 2), cols[...]).astype(BF16)
        half[at, 256:512] = dot(join(1, 2, 3, 4), cols[...]).astype(BF16)
        if not last:
            half[at, 512:] = dot(join(3, 4, 0), cols[:384, :128]).astype(BF16)

    across_block(0)
    for b in range(NB):
        if b + 1 < NB:
            across_block(b + 1)
        first = min(max(b * BLK - 16, 0), ER - BLK - 32)
        which = (b * BLK - first) // 16
        got = dot(rows[which], half[first : first + BLK + 32]) + 1.0
        if last:
            begin, end = max(b * BLK, HALO), min((b + 1) * BLK, HALO + TR)
            out_ref[begin - HALO : end - HALO] = got[begin - b * BLK : end - b * BLK]
            store(b, begin - HALO, end - begin)
        else:
            out_ref[b * BLK : (b + 1) * BLK] = got
            store(b, b * BLK, BLK)


def fine_kernel(last, dose, cols, rows, out, buf, half, made, lsem, ssem):
    loads, stores = [], []
    for b in range(NB):
        at = pl.ds(b * BLK, BLK)
        loads.append(pltpu.make_async_copy(dose.at[at], buf.at[at], lsem.at[b]))
        loads[-1].start()

    def store(b, begin, count):
        at = pl.ds(begin, count)
        stores.append(pltpu.make_async_copy(made.at[at], out.at[at], ssem.at[b]))
        stores[-1].start()

    fine_blocks(last, lambda b: loads[b].wait(), buf, cols, rows, half, made, store)
    for copy in stores:
        copy.wait()


def fine_cost():
    return pl.CostEstimate(flops=2 * ER * EC * (EC + 208), bytes_accessed=6 * ER * EC, transcendentals=0)


def fine(dose, ops, last):
    shape = (TR, TC) if last else (ER, EC)
    return pl.pallas_call(
        functools.partial(fine_kernel, last),
        in_specs=[HBM, VMEM, VMEM],
        out_specs=HBM,
        out_shape=pltpu.HBM(shape, F32),
        scratch_shapes=[
            pltpu.VMEM((ER, EC), BF16),
            pltpu.VMEM((ER, shape[1]), BF16),
            pltpu.VMEM(shape, F32),
            DMA((NB,)),
            DMA((NB,)),
        ],
        compiler_params=params(),
        cost_estimate=fine_cost(),
        name="fine",
    )(far(dose), near(ops[7]), near(ops[8]))


def first_kernel(dose, lo, hi, above, below, cols, rows, out, whole, buf, half, made, lsem, ssem, wsem):
    load = pltpu.make_async_copy(dose, buf.at[pl.ds(HALO, TR), pl.ds(0, TC)], lsem)
    load.start()
    buf[:HALO] = above[...]
    buf[HALO + TR :] = below[...]
    for n in range(TR // 128):
        at = slice(n * 128, (n + 1) * 128)
        buf[HALO + n * 128 : HALO + (n + 1) * 128, TC:] = side(lo[:, at], hi[:, at])
    load.wait()
    keep = pltpu.make_async_copy(buf, whole, wsem)
    keep.start()
    stores = []

    def store(b, begin, count):
        at = pl.ds(begin, count)
        stores.append(pltpu.make_async_copy(made.at[at], out.at[at], ssem.at[b]))
        stores[-1].start()

    fine_blocks(False, lambda b: None, buf, cols, rows, half, made, store)
    for copy in stores:
        copy.wait()
    keep.wait()


def first_fine(dose, lo, hi, above, below, ops):
    return pl.pallas_call(
        first_kernel,
        in_specs=[HBM] + [VMEM] * 6,
        out_specs=[HBM, HBM],
        out_shape=[pltpu.HBM((ER, EC), F32), pltpu.HBM((ER, EC), BF16)],
        scratch_shapes=[
            pltpu.VMEM((ER, EC), BF16),
            pltpu.VMEM((ER, EC), BF16),
            pltpu.VMEM((ER, EC), F32),
            DMA,
            DMA((NB,)),
            DMA,
        ],
        compiler_params=params(),
        cost_estimate=fine_cost(),
        name="first_fine",
    )(far(dose), near(lo), near(hi), near(above), near(below), near(ops[7]), near(ops[8]))


def spread(got, part, matrix, cols, groups):
    m = 16 * groups
    stacked = jnp.concatenate([got[...].reshape(NY * 8, 128), part[...]], axis=0)
    y = dot(matrix[...], stacked, precision=EXACT)
    lane = lax.broadcasted_iota(jnp.int32, (m, 128), 1)
    fourth = jnp.where(lane < 120, y[2 * m : 3 * m], jnp.where(lane == 120, y[3 * m : 3 * m + 1], 0.0))
    a, b, c = pieces(jnp.where(lane < 40, y[:m], jnp.where(lane < 80, y[m : 2 * m], fourth)))
    return dot(a, cols) + dot(b, cols) + dot(c, cols)


def update(b, rows, skip, dose, short, grid, out):
    lanes = out.shape[1]
    t = (lax.broadcasted_iota(jnp.int32, (8, lanes), 0).astype(F32) + 0.5) / 16.0
    for n in range(rows // 16):
        row = b * rows + 16 * n
        at = slice(row, row + 16)
        a, m, c = (grid[16 * b + n + k : 16 * b + n + k + 1] for k in range(3))
        back = jnp.concatenate([a + (t + 0.5) * (m - a), m + t * (c - m)], axis=0)
        old = dose[skip + row : skip + row + 16].astype(F32)
        out[at] = (old * 2.0 / (short[at] + back)).astype(out.dtype)


def fetch(dose, short, dbuf, sbuf, blocks, rows, skip, sems):
    loads = []
    for b in range(blocks):
        at, lanes = pl.ds(b * rows, rows), pl.ds(0, dbuf.shape[1])
        loads.append(
            (
                pltpu.make_async_copy(
                    dose.at[pl.ds(b * rows + skip, rows), lanes], dbuf.at[at], sems.at[0, b]
                ),
                pltpu.make_async_copy(short.at[at], sbuf.at[at], sems.at[1, b]),
            )
        )
        for copy in loads[-1]:
            copy.start()
    return loads


def step_kernel(got, part, matrix, cols, dose, short, cpool, rpool, out, send, own, dbuf, sbuf, made, grid, sums, lsem, ssem):
    loads = fetch(dose, short, dbuf, sbuf, NB, BLK, 0, lsem)
    grid[...] = spread(got, part, matrix, cols[...], NB)
    stores = []
    for b in range(NB):
        for copy in loads[b]:
            copy.wait()
        update(b, BLK, 0, dbuf, sbuf, grid, made)
        at = pl.ds(b * BLK, BLK)
        stores.append(pltpu.make_async_copy(made.at[at], out.at[at], ssem.at[b]))
        stores[-1].start()
        pooled = dot(made[b * BLK : (b + 1) * BLK], cpool[...])
        pooled = jnp.sum(pooled.reshape(BLK // 16, 16, 128), axis=1)
        sums[16 * b : 16 * b + 16] = jnp.concatenate([pooled, jnp.zeros((16 - BLK // 16, 128), F32)], axis=0)
    pooled_out(sums[...], rpool, lax.axis_index("gx"), send, own)
    for copy in stores:
        copy.wait()


def step(got, part, dose, short, ops):
    return pl.pallas_call(
        step_kernel,
        in_specs=[VMEM] * 4 + [HBM] * 2 + [VMEM] * 2,
        out_specs=[HBM, VMEM, VMEM],
        out_shape=[
            pltpu.HBM((ER, EC), BF16),
            pltpu.VMEM((NX, 8, 128), F32),
            pltpu.VMEM((128, 128), F32),
        ],
        scratch_shapes=[
            pltpu.VMEM((ER, EC), BF16),
            pltpu.VMEM((ER, EC), F32),
            pltpu.VMEM((ER, EC), BF16),
            pltpu.VMEM((NB * 16, EC), F32),
            pltpu.VMEM((NB * 16, 128), F32),
            DMA((2, NB)),
            DMA((NB,)),
        ],
        compiler_params=params(),
        name="step",
    )(near(got), near(part), near(ops[0]), near(ops[4]), far(dose), far(short), near(ops[5]), near(ops[6]))


def finish_kernel(got, part, matrix, cols, dose, short, out, dbuf, sbuf, made, grid, lsem, ssem):
    groups = TR // SB
    loads = fetch(dose, short, dbuf, sbuf, groups, SB, HALO, lsem)
    grid[...] = spread(got, part, matrix, cols[:, :TC], groups)
    stores = []
    for b in range(groups):
        for copy in loads[b]:
            copy.wait()
        update(b, SB, 0, dbuf, sbuf, grid, made)
        at = pl.ds(b * SB, SB)
        stores.append(pltpu.make_async_copy(made.at[at], out.at[at], ssem.at[b]))
        stores[-1].start()
    for copy in stores:
        copy.wait()


def finish(got, part, dose, short, ops):
    groups = TR // SB
    return pl.pallas_call(
        finish_kernel,
        in_specs=[VMEM] * 4 + [HBM] * 2,
        out_specs=HBM,
        out_shape=pltpu.HBM((TR, TC), F32),
        scratch_shapes=[
            pltpu.VMEM((TR, TC), BF16),
            pltpu.VMEM((TR, TC), F32),
            pltpu.VMEM((TR, TC), F32),
            pltpu.VMEM((groups * 16, TC), F32),
            DMA((2, groups)),
            DMA((groups,)),
        ],
        compiler_params=params(),
        name="finish",
    )(near(got), near(part), near(ops[1]), near(ops[4]), far(dose), far(short))


def shifted(x, axis, by):
    n = lax.axis_size(axis)
    return lax.ppermute(x, axis, [(i, i + by) for i in range(n) if 0 <= i + by < n])


def exchanged(x, axis):
    return lax.all_to_all(x, axis, 0, 0, tiled=True)


def local(classes, exponents, gain_field, level_table, level_weights):
    (tile, first, final, lo, hi, send, own), ops = start(
        level_weights, level_table, exponents, classes, gain_field
    )
    left, right = shifted(hi, "gx", 1), shifted(lo, "gx", -1)
    got = exchanged(send, "gx")
    top, bottom = edges(first, final, left, right)
    above, below = shifted(bottom, "gy", 1), shifted(top, "gy", -1)
    send, part = across(got, own, ops)
    got = exchanged(send, "gy")
    short, dose = first_fine(tile, left, right, above, below, ops)
    for sweep in range(1, ITERS):
        dose, send, own = step(got, part, dose, short, ops)
        got = exchanged(send, "gx")
        short = fine(dose, ops, sweep == ITERS - 1)
        send, part = across(got, own, ops)
        got = exchanged(send, "gy")
    return finish(got, part, dose, short, ops)


def solution(mesh):
    in_specs = (P("gy", "gx"), P("gy", "gx"), P("gy", "gx"), P(), P())
    return jax.shard_map(local, mesh=mesh, in_specs=in_specs, out_specs=P("gy", "gx"), check_vma=False)
```

```python
import functools

import jax
import jax.numpy as jnp
import ml_dtypes
import numpy as np
from jax import lax
from jax.experimental import pallas as pl
from jax.experimental.pallas import tpu as pltpu
from jax.sharding import PartitionSpec as P

HW = 4
CLASSES = 8
SB = 128
ITERS = 4
NX, NY = 32, 8
TR, TC = 1024, 512
HALO = HW * ITERS
ER = TR + 2 * HALO
EC = TC + 128
BLK = 176
NB = ER // BLK
QC, QR = 36, 68
F32, BF16 = jnp.float32, jnp.bfloat16
EXACT = lax.Precision.HIGHEST


def gauss_taps():
    offsets = np.arange(-HW, HW + 1).astype(np.float32)
    weights = np.exp(-(offsets * offsets) / np.float32(HW * HW)).astype(np.float32)
    return weights / weights.sum(dtype=np.float32)


def blur_operator(n):
    taps = gauss_taps().astype(np.float64)
    out = np.zeros((n, n))
    for k in range(-HW, HW + 1):
        out += taps[k + HW] * np.eye(n, k=k)
    return out


def up_operator(n, factor):
    target = np.arange(n * factor)
    lower = (target - factor // 2) // factor
    t = (target - factor // 2 - factor * lower + 0.5) / factor
    out = np.zeros((n * factor, n))
    np.add.at(out, (target, np.clip(lower, 0, n - 1)), 1 - t)
    np.add.at(out, (target, np.clip(lower + 1, 0, n - 1)), t)
    return out


def level_operators(n_second):
    third, fourth = n_second // 4, n_second // 16
    return (
        blur_operator(n_second),
        up_operator(third, 4) @ blur_operator(third),
        up_operator(third, 4) @ up_operator(fourth, 4) @ blur_operator(fourth),
    )


@functools.cache
def column_matrices():
    second, third, fourth = level_operators(NX * 32)
    got = np.zeros((NX, 128, 256), np.float32)
    own = np.zeros((NX, 128, 32), np.float32)
    for px in range(NX):
        for q in range(QC):
            g = min(max(32 * px + q - 2, 0), NX * 32 - 1)
            for s in np.nonzero(second[g])[0]:
                p, j = divmod(int(s), 32)
                if p == px:
                    own[px, q, j] = second[g, s]
                else:
                    assert j >= 24 if p < px else j < 8
                    got[px, q, p * 8 + j % 8] = second[g, s]
            got[px, 40 + q] = third[g]
            for j in range(2):
                got[px, 80 + q, j::8] = fourth[g, j::2]
        got[px, 120, 0::8] = 1
        got[px, 120, 1::8] = 1
    return got, own


def row_matrices(groups, first, step, length):
    second, third, fourth = level_operators(NY * 64)
    m = 16 * groups
    out = np.zeros((NY, 3 * m + 8, 192), np.float32)
    for py in range(NY):
        for b in range(groups):
            for k in range(length):
                row, q = b * 16 + k, first + step * b + k
                g = min(max(64 * py + q - 2, 0), NY * 64 - 1)
                for s in np.nonzero(second[g])[0]:
                    p, j = divmod(int(s), 64)
                    assert p == py or (j >= 56 if p < py else j < 8)
                    out[py, row, 64 + j if p == py else p * 8 + j % 8] = second[g, s]
                for s in np.nonzero(third[g])[0]:
                    p, j = divmod(int(s), 16)
                    assert p == py or (j >= 8 if p < py else j < 8)
                    out[py, m + row, 128 + j if p == py else p * 8 + j % 8] = third[g, s]
                for s in np.nonzero(fourth[g])[0]:
                    p, j = divmod(int(s), 4)
                    out[py, 2 * m + row, p * 8 + j] = fourth[g, s]
        out[py, 3 * m, 4:64:8] = 1
    return out


@functools.cache
def column_spread():
    out = np.zeros((128, EC), np.float32)
    for lane in range(EC):
        cell = lane if lane < TC + HALO else lane - EC
        if cell < -HALO:
            continue
        lower = (cell - 8) // 16
        t = (cell - 8 - 16 * lower + 0.5) / 16
        for level in range(3):
            out[40 * level + lower + 2, lane] += 1 - t
            out[40 * level + lower + 3, lane] += t
        out[120, lane] = 1
    return out.astype(ml_dtypes.bfloat16)


@functools.cache
def column_pool(lanes):
    out = np.zeros((lanes, 128), np.float32)
    cell = np.arange(TC)
    out[cell, cell // 16] = 1
    out[cell, 32 + cell // 64] = 1
    out[cell, 40 + cell // 256] = 1
    return out.astype(ml_dtypes.bfloat16)


@functools.cache
def row_pool(groups, stride, real, first):
    out = np.zeros((128, groups * stride), np.float32)
    for b in range(groups):
        for k in range(real):
            s = b * real + k - first
            if 0 <= s < TR // 16:
                at = b * stride + k
                out[s, at] = 2.0**-8
                out[64 + s // 4, at] = 2.0**-12
                out[80 + s // 16, at] = 2.0**-16
                out[84, at] = 1.0 / (TR * NY * TC * NX)
    return out.astype(ml_dtypes.bfloat16)


def fine_taps():
    return gauss_taps().astype(ml_dtypes.bfloat16)


@functools.cache
def fine_columns():
    out = np.zeros((512, 256), ml_dtypes.bfloat16)
    taps, lane = fine_taps(), np.arange(256)
    for k in range(-HW, HW + 1):
        out[lane + 128 + k, lane] = taps[k + HW]
    return out


@functools.cache
def fine_rows():
    out = np.zeros((3, BLK, BLK + 32), ml_dtypes.bfloat16)
    taps = fine_taps()
    for which in range(3):
        for r in range(BLK):
            for k in range(-HW, HW + 1):
                c = r + 16 * which + k
                if 0 <= c < BLK + 32:
                    out[which, r, c] = taps[k + HW]
    return out


VMEM = pl.BlockSpec(memory_space=pltpu.VMEM)
SMEM = pl.BlockSpec(memory_space=pltpu.SMEM)
HBM = pl.BlockSpec(memory_space=pl.ANY)
DMA = pltpu.SemaphoreType.DMA


def params(mib=24):
    return pltpu.CompilerParams(vmem_limit_bytes=mib * 2**20)


def near(x):
    return pltpu.with_memory_space_constraint(x, pltpu.VMEM)


def far(x):
    return pltpu.with_memory_space_constraint(x, pltpu.HBM)


def dot(a, b, **kw):
    return jnp.dot(a, b, preferred_element_type=F32, **kw)


def pieces(x):
    first = x.astype(BF16)
    rest = x - first.astype(F32)
    second = rest.astype(BF16)
    return first, second, (rest - second.astype(F32)).astype(BF16)


def pooled_out(sums, row_pool_ref, px, send_ref, own_ref):
    a, b, c = pieces(sums)
    rows = row_pool_ref[...]
    pooled = (dot(rows, a) + dot(rows, b) + dot(rows, c)).T
    own_ref[...] = pooled
    lane = lax.broadcasted_iota(jnp.int32, (8, 128), 1)
    coarse = jnp.where(lane < 80, pooled[32:40], pooled[40:48])
    left = jnp.where(lane < 64, pooled[0:8], coarse)
    right = jnp.where(lane < 64, pooled[24:32], coarse)
    for p in range(NX):
        send_ref[p] = jnp.where(p < px, left, right)


def start_kernel(table, exps, classes, gain, cpool_far, rpool_far, dose, lo, hi, send, own, *scratch):
    cbuf, gbuf, cpool, rpool, sums, csem, gsem, tsem = scratch
    steps = TR // SB
    loads = []
    for i in range(steps):
        rows = pl.ds(i * SB, SB)
        loads.append(
            (
                pltpu.make_async_copy(classes.at[rows], cbuf.at[rows], csem.at[i]),
                pltpu.make_async_copy(gain.at[rows], gbuf.at[rows], gsem.at[i]),
            )
        )
        for copy in loads[-1]:
            copy.start()
    tables = (
        pltpu.make_async_copy(cpool_far, cpool, tsem.at[0]),
        pltpu.make_async_copy(rpool_far, rpool, tsem.at[1]),
    )
    for copy in tables:
        copy.start()
    for i in range(steps):
        for copy in loads[i]:
            copy.wait()
        rows = slice(i * SB, (i + 1) * SB)
        for k in range(TC // SB):
            e = exps[i, k]
            scale = jnp.where(e > 0, 2.0, jnp.where(e < 0, 0.5, 1.0)).astype(F32)
            at = slice(k * SB, (k + 1) * SB)
            c = cbuf[rows, at]
            level = jnp.zeros((SB, SB), F32)
            for j in range(1, CLASSES):
                level = jnp.where(c == j, table[j] * scale, level)
            value = (level * gbuf[rows, at].astype(F32)).astype(BF16)
            dose[rows, at] = value
            if k == 0:
                lo[:, rows] = value.astype(F32).T[:HALO].astype(BF16)
            if k == TC // SB - 1:
                hi[:, rows] = value.astype(F32).T[SB - HALO :].astype(BF16)
        if i == 0:
            for copy in tables:
                copy.wait()
        across = dot(dose[rows], cpool[...])
        sums[8 * i : 8 * i + 8] = jnp.sum(across.reshape(8, 16, 128), axis=1)
    pooled_out(sums[...], rpool, lax.axis_index("gx"), send, own)


def start(table, exps, classes, gain):
    steps = TR // SB
    return pl.pallas_call(
        start_kernel,
        in_specs=[SMEM, SMEM] + [HBM] * 4,
        out_specs=[VMEM] * 5,
        out_shape=[
            pltpu.VMEM((TR, TC), BF16),
            pltpu.VMEM((HALO, TR), BF16),
            pltpu.VMEM((HALO, TR), BF16),
            pltpu.VMEM((NX, 8, 128), F32),
            pltpu.VMEM((128, 128), F32),
        ],
        scratch_shapes=[
            pltpu.VMEM((TR, TC), jnp.int32),
            pltpu.VMEM((TR, TC), BF16),
            pltpu.VMEM((TC, 128), BF16),
            pltpu.VMEM((128, TR // 16), BF16),
            pltpu.VMEM((TR // 16, 128), F32),
            DMA((steps,)),
            DMA((steps,)),
            DMA((2,)),
        ],
        compiler_params=params(),
        name="start",
    )(far(table), far(exps), far(classes), far(gain), far(jnp.asarray(column_pool(TC))), far(jnp.asarray(row_pool(8, 8, 8, 0))))


def operators():
    mgot, mown = column_matrices()
    return [
        (row_matrices(NB, 0, BLK // 16, BLK // 16 + 2), 1),
        (mgot, 0),
        (mown, 0),
        (column_spread(), None),
        (column_pool(EC), None),
        (row_pool(NB, 16, BLK // 16, 1), None),
        (fine_rows(), None),
    ]


def weighted(ref, weights, m):
    for level in range(3):
        at = slice(m * level, m * (level + 1))
        ref[at] = ref[at] * weights[level]
    ref[3 * m :] = ref[3 * m :] * weights[2]


def pick_kernel(picks, after, weights, *refs):
    n = len(picks)
    tables, outs, sems = refs[:n], refs[n : 2 * n], refs[-1]
    place = lax.axis_index("gx"), lax.axis_index("gy")
    copies = []
    for i, pick in enumerate(picks):
        source = tables[i] if pick is None else tables[i].at[place[pick]]
        copies.append(pltpu.make_async_copy(source, outs[i], sems.at[i]))
        copies[-1].start()
    for copy in copies:
        copy.wait()
    weighted(outs[0], weights, 16 * NB)


def pick(after, weights):
    made = operators()
    picks = [at for _, at in made]
    outs = [pltpu.VMEM(t.shape if at is None else t.shape[1:], t.dtype) for t, at in made]
    return pl.pallas_call(
        functools.partial(pick_kernel, picks),
        in_specs=[HBM, SMEM] + [HBM] * len(made),
        out_specs=[VMEM] * len(made),
        out_shape=outs,
        scratch_shapes=[DMA((len(made),))],
        compiler_params=params(),
        name="pick",
    )(near(after), far(weights), *[far(jnp.asarray(t)) for t, _ in made])


def side(strip_lo, strip_hi):
    rows = strip_lo.shape[1]
    empty = jnp.zeros((rows, 128 - 2 * HALO), F32)
    return jnp.concatenate([strip_hi.astype(F32).T, empty, strip_lo.astype(F32).T], axis=1)


def across_kernel(first, *refs):
    if first:
        tile, lo, hi, got, own, mgot, mown, send, part = refs
    else:
        _, got, own, mgot, mown, send, part = refs
    received = got[...].reshape(NX * 8, 128)
    z = dot(mgot[...], received, precision=EXACT) + dot(mown[...], own[:32], precision=EXACT)
    z = z.T
    part[...] = z
    lane = lax.broadcasted_iota(jnp.int32, (8, 128), 1)
    coarse = z[80:88]
    up = jnp.where(lane < 40, z[0:8], jnp.where(lane < 80, z[64:72], coarse))
    down = jnp.where(lane < 40, z[56:64], jnp.where(lane < 80, z[72:80], coarse))
    py = lax.axis_index("gy")
    for p in range(NY):
        send[p, :8] = jnp.where(p < py, up, down)
    if first:
        for n in range(EC // 128):
            lanes = slice(128 * n, 128 * n + 128)
            if n < TC // 128:
                top, bottom = tile[:HALO, lanes].astype(F32), tile[TR - HALO :, lanes].astype(F32)
            else:
                top = side(lo[:, :128], hi[:, :128])[:HALO]
                bottom = side(lo[:, TR - 128 :], hi[:, TR - 128 :])[128 - HALO :]
            for p in range(NY):
                send[p, 8 + HALO * n : 8 + HALO * (n + 1)] = jnp.where(p < py, top, bottom)


def across(first, extra, got, own, ops):
    count = 8 + HALO * (EC // 128) if first else 8
    specs = [VMEM] * 3 if first else [HBM]
    return pl.pallas_call(
        functools.partial(across_kernel, first),
        in_specs=specs + [VMEM] * 4,
        out_specs=[VMEM] * 2,
        out_shape=[pltpu.VMEM((NY, count, 128), F32), pltpu.VMEM((128, 128), F32)],
        compiler_params=params(),
        name="across",
    )(*([near(x) for x in extra] if first else [far(x) for x in extra]), near(got), near(own), near(ops[1]), near(ops[2]))


def column_pass(block, cols, half, at):
    tile = [block[:, 128 * n : 128 * (n + 1)] for n in range(EC // 128)]
    join = lambda *which: jnp.concatenate([tile[n] for n in which], axis=1)
    half[at, :256] = dot(join(4, 0, 1, 2), cols[...]).astype(BF16)
    half[at, 256:512] = dot(join(1, 2, 3, 4), cols[...]).astype(BF16)
    if half.shape[1] > TC:
        half[at, 512:] = dot(join(3, 4, 0), cols[:384, :128]).astype(BF16)


def first_half_kernel(tile, lo, hi, cols_far, half_far, dose_far, half, dose, cols, sems, csem):
    load = pltpu.make_async_copy(cols_far, cols, csem)
    load.start()
    stores = []
    for n in range(TR // SB):
        rows, begin = slice(n * SB, (n + 1) * SB), HALO + n * SB
        dose[begin : begin + SB, :TC] = tile[rows]
        dose[begin : begin + SB, TC:] = side(lo[:, rows], hi[:, rows]).astype(BF16)
        if n == 0:
            load.wait()
        column_pass(dose[begin : begin + SB], cols, half, slice(begin, begin + SB))
        at = pl.ds(begin, SB)
        stores.append(pltpu.make_async_copy(half.at[at], half_far.at[at], sems.at[0, n]))
        stores[-1].start()
        stores.append(pltpu.make_async_copy(dose.at[at], dose_far.at[at], sems.at[1, n]))
        stores[-1].start()
    for copy in stores:
        copy.wait()


def half_cost():
    return pl.CostEstimate(flops=4 * ER * EC * EC, bytes_accessed=6 * ER * EC, transcendentals=0)


def first_half(tile, lo, hi):
    return pl.pallas_call(
        first_half_kernel,
        in_specs=[VMEM] * 3 + [HBM],
        out_specs=[HBM, HBM],
        out_shape=[pltpu.HBM((ER, EC), BF16)] * 2,
        scratch_shapes=[
            pltpu.VMEM((ER, EC), BF16),
            pltpu.VMEM((ER, EC), BF16),
            pltpu.VMEM((512, 256), BF16),
            DMA((2, TR // SB)),
            DMA,
        ],
        compiler_params=params(),
        cost_estimate=half_cost(),
        name="first_half",
    )(near(tile), near(lo), near(hi), far(jnp.asarray(fine_columns())))


def half_kernel(dose, cols_far, half_far, half, cols, sems, csem):
    load = pltpu.make_async_copy(cols_far, cols, csem)
    load.start()
    load.wait()
    stores = []
    for b in range(NB):
        column_pass(dose[b * BLK : (b + 1) * BLK], cols, half, slice(b * BLK, (b + 1) * BLK))
        at = pl.ds(b * BLK, BLK)
        stores.append(pltpu.make_async_copy(half.at[at], half_far.at[at], sems.at[b]))
        stores[-1].start()
    for copy in stores:
        copy.wait()


def half_of(dose, lanes):
    return pl.pallas_call(
        half_kernel,
        in_specs=[VMEM, HBM],
        out_specs=HBM,
        out_shape=pltpu.HBM((ER, lanes), BF16),
        scratch_shapes=[pltpu.VMEM((ER, lanes), BF16), pltpu.VMEM((512, 256), BF16), DMA((NB,)), DMA],
        compiler_params=params(),
        cost_estimate=half_cost(),
        name="half",
    )(near(dose), far(jnp.asarray(fine_columns())))


def spread(received, part, matrix, cols, groups):
    m = 16 * groups
    y = dot(matrix[...], jnp.concatenate([received, part[...]], axis=0), precision=EXACT)
    lane = lax.broadcasted_iota(jnp.int32, (m, 128), 1)
    fourth = jnp.where(lane < 120, y[2 * m : 3 * m], jnp.where(lane == 120, y[3 * m : 3 * m + 1], 0.0))
    a, b, c = pieces(jnp.where(lane < 40, y[:m], jnp.where(lane < 80, y[m : 2 * m], fourth)))
    return dot(a, cols) + dot(b, cols) + dot(c, cols)


def short_range(b, rows, half):
    begin = min(max(b * BLK - 16, 0), ER - BLK - 32)
    return dot(rows[(b * BLK - begin) // 16], half[begin : begin + BLK + 32])


def update(b, old_rows, short, grid, out, skip):
    count, lanes = out.shape
    t = (lax.broadcasted_iota(jnp.int32, (8, lanes), 0).astype(F32) + 0.5) / 16.0
    for n in range(BLK // 16):
        row = b * BLK + 16 * n
        if not skip <= row < skip + count:
            continue
        a, m, c = (grid[16 * b + n + k : 16 * b + n + k + 1] for k in range(3))
        back = jnp.concatenate([a + (t + 0.5) * (m - a), m + t * (c - m)], axis=0)
        full = 1.0 + (short[16 * n : 16 * n + 16] + back)
        out[row - skip : row - skip + 16] = (old_rows(row).astype(F32) * 2.0 / full).astype(out.dtype)


def step_kernel(first, got, part, matrix, cols, dose, half, rows, cpool, rpool, *refs):
    if first:
        fcols_far, out, send, own, hbuf, grid, sums, lsem, dbuf, fcols, dsem, fsem = refs
        fetch = pltpu.make_async_copy(fcols_far, fcols, fsem)
        fetch.start()
    else:
        out, send, own, hbuf, grid, sums, lsem = refs
        dbuf = dose
    loads = []
    for b in range(NB):
        begin, end = b * BLK, (b + 1) * BLK
        if first:
            begin, end = max(begin, HALO), min(end, ER - HALO)
        at = pl.ds(begin, end - begin)
        loads.append([pltpu.make_async_copy(half.at[at], hbuf.at[at], lsem.at[b])])
        if first:
            loads[-1].append(pltpu.make_async_copy(dose.at[at], dbuf.at[at], dsem.at[b]))
        for copy in loads[-1]:
            copy.start()
    received = got[:, :8].reshape(NY * 8, 128)
    grid[...] = spread(received, part, matrix, cols[...], NB)
    if first:
        py = lax.axis_index("gy")
        fetch.wait()
        for row, p, real in ((0, jnp.maximum(py - 1, 0), py > 0), (ER - HALO, jnp.minimum(py + 1, NY - 1), py < NY - 1)):
            tiles = [got[p, 8 + HALO * n : 8 + HALO * (n + 1)] for n in range(EC // 128)]
            values = jnp.where(real, jnp.concatenate(tiles, axis=1), 0.0).astype(BF16)
            dbuf[row : row + HALO] = values
            column_pass(values, fcols, hbuf, slice(row, row + HALO))

    def ready(b):
        for copy in loads[b]:
            copy.wait()

    ready(0)
    for b in range(NB):
        if b + 1 < NB:
            ready(b + 1)
        update(b, lambda row: dbuf[row : row + 16], short_range(b, rows, hbuf), grid, out, 0)
        pooled = dot(out[b * BLK : (b + 1) * BLK], cpool[...])
        pooled = jnp.sum(pooled.reshape(BLK // 16, 16, 128), axis=1)
        sums[16 * b : 16 * b + 16] = jnp.concatenate([pooled, jnp.zeros((16 - BLK // 16, 128), F32)], axis=0)
    pooled_out(sums[...], rpool, lax.axis_index("gx"), send, own)


def step(first, got, part, dose, half, ops):
    scratch = [
        pltpu.VMEM((ER, EC), BF16),
        pltpu.VMEM((NB * 16, EC), F32),
        pltpu.VMEM((NB * 16, 128), F32),
        DMA((NB,)),
    ]
    more = [pltpu.VMEM((ER, EC), BF16), pltpu.VMEM((512, 256), BF16), DMA((NB,)), DMA] if first else []
    return pl.pallas_call(
        functools.partial(step_kernel, first),
        in_specs=[VMEM] * 4 + [HBM if first else VMEM, HBM] + [VMEM] * 3 + ([HBM] if first else []),
        out_specs=[VMEM] * 3,
        out_shape=[
            pltpu.VMEM((ER, EC), BF16),
            pltpu.VMEM((NX, 8, 128), F32),
            pltpu.VMEM((128, 128), F32),
        ],
        scratch_shapes=scratch + more,
        input_output_aliases={} if first else {4: 0},
        compiler_params=params(),
        name="first_step" if first else "step",
    )(
        near(got), near(part), near(ops[0]), near(ops[3]), far(dose) if first else near(dose), far(half),
        near(ops[6]), near(ops[4]), near(ops[5]), *([far(jnp.asarray(fine_columns()))] if first else []),
    )


def finish_kernel(got, part, matrix, cols, dose, half, rows, out, hbuf, made, grid, lsem, ssem):
    loads = []
    for b in range(NB):
        at = pl.ds(b * BLK, BLK)
        loads.append(pltpu.make_async_copy(half.at[at], hbuf.at[at], lsem.at[b]))
        loads[-1].start()
    grid[...] = spread(got[...].reshape(NY * 8, 128), part, matrix, cols[:, :TC], NB)
    stores = []
    loads[0].wait()
    for b in range(NB):
        if b + 1 < NB:
            loads[b + 1].wait()
        update(b, lambda row: dose[row : row + 16, :TC], short_range(b, rows, hbuf), grid, made, HALO)
        begin, end = max(b * BLK - HALO, 0), min((b + 1) * BLK - HALO, TR)
        at = pl.ds(begin, end - begin)
        stores.append(pltpu.make_async_copy(made.at[at], out.at[at], ssem.at[b]))
        stores[-1].start()
    for copy in stores:
        copy.wait()


def finish(got, part, dose, half, ops):
    return pl.pallas_call(
        finish_kernel,
        in_specs=[VMEM] * 5 + [HBM, VMEM],
        out_specs=HBM,
        out_shape=pltpu.HBM((TR, TC), F32),
        scratch_shapes=[
            pltpu.VMEM((ER, TC), BF16),
            pltpu.VMEM((TR, TC), F32),
            pltpu.VMEM((NB * 16, TC), F32),
            DMA((NB,)),
            DMA((NB,)),
        ],
        compiler_params=params(),
        name="finish",
    )(near(got), near(part), near(ops[0]), near(ops[3]), near(dose), far(half), near(ops[6]))


def shifted(x, axis, by):
    n = lax.axis_size(axis)
    return lax.ppermute(x, axis, [(i, i + by) for i in range(n) if 0 <= i + by < n])


def exchanged(x, axis):
    return lax.all_to_all(x, axis, 0, 0, tiled=True)


def local(classes, exponents, gain_field, level_table, level_weights):
    tile, lo, hi, send, own = start(level_table, exponents, classes, gain_field)
    left, right = shifted(hi, "gx", 1), shifted(lo, "gx", -1)
    got = exchanged(send, "gx")
    ops = pick(left, level_weights)
    send, part = across(True, (tile, left, right), got, own, ops)
    got = exchanged(send, "gy")
    half, dose = first_half(tile, left, right)
    dose, send, own = step(True, got, part, dose, half, ops)
    for sweep in range(2, ITERS + 1):
        got = exchanged(send, "gx")
        half = half_of(dose, EC if sweep < ITERS else TC)
        send, part = across(False, (half,), got, own, ops)
        got = exchanged(send, "gy")
        if sweep < ITERS:
            dose, send, own = step(False, got, part, dose, half, ops)
    return finish(got, part, dose, half, ops)


def solution(mesh):
    in_specs = (P("gy", "gx"), P("gy", "gx"), P("gy", "gx"), P(), P())
    return jax.shard_map(local, mesh=mesh, in_specs=in_specs, out_specs=P("gy", "gx"), check_vma=False)
```

```python
import functools

import jax
import jax.numpy as jnp
import ml_dtypes
import numpy as np
from jax import lax
from jax.experimental import pallas as pl
from jax.experimental.pallas import tpu as pltpu
from jax.sharding import PartitionSpec as P

HW = 4
CLASSES = 8
SB = 128
ITERS = 4
NX, NY = 32, 8
TR, TC = 1024, 512
HALO = HW * ITERS
ER = TR + 2 * HALO
EC = TC + 128
BLK = 176
NB = ER // BLK
QC, QR = 36, 68
F32, BF16 = jnp.float32, jnp.bfloat16
EXACT = lax.Precision.HIGHEST


def gauss_taps():
    offsets = np.arange(-HW, HW + 1).astype(np.float32)
    weights = np.exp(-(offsets * offsets) / np.float32(HW * HW)).astype(np.float32)
    return weights / weights.sum(dtype=np.float32)


def blur_operator(n):
    taps = gauss_taps().astype(np.float64)
    out = np.zeros((n, n))
    for k in range(-HW, HW + 1):
        out += taps[k + HW] * np.eye(n, k=k)
    return out


def up_operator(n, factor):
    target = np.arange(n * factor)
    lower = (target - factor // 2) // factor
    t = (target - factor // 2 - factor * lower + 0.5) / factor
    out = np.zeros((n * factor, n))
    np.add.at(out, (target, np.clip(lower, 0, n - 1)), 1 - t)
    np.add.at(out, (target, np.clip(lower + 1, 0, n - 1)), t)
    return out


def level_operators(n_second):
    third, fourth = n_second // 4, n_second // 16
    return (
        blur_operator(n_second),
        up_operator(third, 4) @ blur_operator(third),
        up_operator(third, 4) @ up_operator(fourth, 4) @ blur_operator(fourth),
    )


@functools.cache
def column_matrices():
    second, third, fourth = level_operators(NX * 32)
    got = np.zeros((NX, 128, 256), np.float32)
    own = np.zeros((NX, 40, 32), np.float32)
    for px in range(NX):
        for q in range(QC):
            g = min(max(32 * px + q - 2, 0), NX * 32 - 1)
            for s in np.nonzero(second[g])[0]:
                p, j = divmod(int(s), 32)
                if p == px:
                    own[px, q, j] = second[g, s]
                else:
                    assert j >= 24 if p < px else j < 8
                    got[px, q, p * 8 + j % 8] = second[g, s]
            got[px, 40 + q] = third[g]
            for j in range(2):
                got[px, 80 + q, j::8] = fourth[g, j::2]
        got[px, 120, 0::8] = 1
        got[px, 120, 1::8] = 1
    return got, own


def row_matrices(groups, first, step, length):
    second, third, fourth = level_operators(NY * 64)
    m = 16 * groups
    out = np.zeros((NY, 3 * m + 16, 144), np.float32)
    for py in range(NY):
        for b in range(groups):
            for k in range(length):
                row, q = b * 16 + k, first + step * b + k
                g = min(max(64 * py + q - 2, 0), NY * 64 - 1)
                for s in np.nonzero(second[g])[0]:
                    p, j = divmod(int(s), 64)
                    assert p == py or (j >= 56 if p < py else j < 8)
                    out[py, row, 64 + j if p == py else p * 8 + j % 8] = second[g, s]
                for s in np.nonzero(third[g])[0]:
                    p, j = divmod(int(s), 16)
                    assert p == py or (j >= 8 if p < py else j < 8)
                    out[py, m + row, 128 + j if p == py else p * 8 + j % 8] = third[g, s]
                for s in np.nonzero(fourth[g])[0]:
                    p, j = divmod(int(s), 4)
                    out[py, 2 * m + row, p * 8 + j] = fourth[g, s]
        out[py, 3 * m, 4:64:8] = 1
    return out


@functools.cache
def column_spread():
    out = np.zeros((128, EC), np.float32)
    for lane in range(EC):
        cell = lane if lane < TC + HALO else lane - EC
        if cell < -HALO:
            continue
        lower = (cell - 8) // 16
        t = (cell - 8 - 16 * lower + 0.5) / 16
        for level in range(3):
            out[40 * level + lower + 2, lane] += 1 - t
            out[40 * level + lower + 3, lane] += t
        out[120, lane] = 1
    return out.astype(ml_dtypes.bfloat16)


@functools.cache
def row_pool(groups, stride, real, first):
    out = np.zeros((128, groups * stride), np.float32)
    for b in range(groups):
        for k in range(real):
            s = b * real + k - first
            if 0 <= s < TR // 16:
                at = b * stride + k
                out[s, at] = 2.0**-8
                out[64 + s // 4, at] = 2.0**-12
                out[80 + s // 16, at] = 2.0**-16
                out[84, at] = 1.0 / (TR * NY * TC * NX)
    return out.astype(ml_dtypes.bfloat16)


def fine_taps():
    return gauss_taps().astype(ml_dtypes.bfloat16)


@functools.cache
def fine_columns():
    out = np.zeros((512, 256), ml_dtypes.bfloat16)
    taps, lane = fine_taps(), np.arange(256)
    for k in range(-HW, HW + 1):
        out[lane + 128 + k, lane] = taps[k + HW]
    return out


VMEM = pl.BlockSpec(memory_space=pltpu.VMEM)
SMEM = pl.BlockSpec(memory_space=pltpu.SMEM)
HBM = pl.BlockSpec(memory_space=pl.ANY)
DMA = pltpu.SemaphoreType.DMA


def params(mib=24):
    return pltpu.CompilerParams(vmem_limit_bytes=mib * 2**20)


def near(x):
    return pltpu.with_memory_space_constraint(x, pltpu.VMEM)


def far(x):
    return pltpu.with_memory_space_constraint(x, pltpu.HBM)


def dot(a, b, **kw):
    return jnp.dot(a, b, preferred_element_type=F32, **kw)


def pieces(x):
    first = x.astype(BF16)
    rest = x - first.astype(F32)
    second = rest.astype(BF16)
    return first, second, (rest - second.astype(F32)).astype(BF16)


def fill_rows(rows):
    shape = (BLK, BLK + 32)
    shift = lax.broadcasted_iota(jnp.int32, shape, 1) - lax.broadcasted_iota(jnp.int32, shape, 0)
    for which in range(3):
        band = jnp.zeros(shape, F32)
        for k in range(-HW, HW + 1):
            band = jnp.where(shift == 16 * which + k, float(fine_taps()[k + HW]), band)
        rows[which] = band.astype(BF16)


def fill_pool(cpool):
    col = lax.broadcasted_iota(jnp.int32, cpool.shape, 0)
    lane = lax.broadcasted_iota(jnp.int32, cpool.shape, 1)
    group = jnp.where(lane < 32, col >> 4, jnp.where(lane < 40, 32 + (col >> 6), 40 + (col >> 8)))
    cpool[...] = jnp.where((group == lane) & (col < TC), 1.0, 0.0).astype(BF16)


def pooled_out(sums, row_pool_ref, px, send_ref, own_ref):
    a, b, c = pieces(sums)
    rows = row_pool_ref[...]
    pooled = (dot(rows, a) + dot(rows, b) + dot(rows, c)).T
    own_ref[...] = pooled[:32]
    lane = lax.broadcasted_iota(jnp.int32, (8, 128), 1)
    coarse = jnp.where(lane < 80, pooled[32:40], pooled[40:48])
    left = jnp.where(lane < 64, pooled[0:8], coarse)
    right = jnp.where(lane < 64, pooled[24:32], coarse)
    for p in range(NX):
        send_ref[p] = jnp.where(p < px, left, right)


def start_kernel(table, exps, classes, gain, rpool_far, mgot_far, mown_far, dose, lo, hi, send, own, mgot, mown, *scratch):
    cbuf, gbuf, cpool, rpool, sums, csem, gsem, tsem = scratch
    px = lax.axis_index("gx")
    steps = TR // SB
    loads = []
    for i in range(steps):
        rows = pl.ds(i * SB, SB)
        loads.append(
            (
                pltpu.make_async_copy(classes.at[rows], cbuf.at[rows], csem.at[i]),
                pltpu.make_async_copy(gain.at[rows], gbuf.at[rows], gsem.at[i]),
            )
        )
        for copy in loads[-1]:
            copy.start()
    tables = (
        pltpu.make_async_copy(rpool_far, rpool, tsem.at[0]),
        pltpu.make_async_copy(mgot_far.at[px], mgot, tsem.at[1]),
        pltpu.make_async_copy(mown_far.at[px], mown, tsem.at[2]),
    )
    for copy in tables:
        copy.start()
    fill_pool(cpool)
    for i in range(steps):
        for copy in loads[i]:
            copy.wait()
        rows = slice(i * SB, (i + 1) * SB)
        for k in range(TC // SB):
            e = exps[k, i]
            scale = jnp.where(e > 0, 2.0, jnp.where(e < 0, 0.5, 1.0)).astype(F32)
            at = slice(k * SB, (k + 1) * SB)
            c = cbuf[rows, at]
            level = jnp.zeros((SB, SB), F32)
            for j in range(1, CLASSES):
                level = jnp.where(c == j, table[j] * scale, level)
            value = (level * gbuf[rows, at].astype(F32)).astype(BF16)
            dose[rows, at] = value
            if k == 0:
                lo[:, rows] = value.astype(F32).T[:HALO].astype(BF16)
            if k == TC // SB - 1:
                hi[:, rows] = value.astype(F32).T[SB - HALO :].astype(BF16)
        across = dot(dose[rows], cpool[...])
        sums[8 * i : 8 * i + 8] = jnp.sum(across.reshape(8, 16, 128), axis=1)
    for copy in tables:
        copy.wait()
    pooled_out(sums[...], rpool, px, send, own)


def start(table, exps, classes, gain):
    steps = TR // SB
    mgot, mown = column_matrices()
    return pl.pallas_call(
        start_kernel,
        in_specs=[SMEM, SMEM] + [HBM] * 5,
        out_specs=[VMEM] * 7,
        out_shape=[
            pltpu.VMEM((TR, TC), BF16),
            pltpu.VMEM((HALO, TR), BF16),
            pltpu.VMEM((HALO, TR), BF16),
            pltpu.HBM((NX, 8, 128), F32),
            pltpu.VMEM((32, 128), F32),
            pltpu.VMEM(mgot.shape[1:], F32),
            pltpu.VMEM(mown.shape[1:], F32),
        ],
        scratch_shapes=[
            pltpu.VMEM((TR, TC), jnp.int32),
            pltpu.VMEM((TR, TC), BF16),
            pltpu.VMEM((TC, 128), BF16),
            pltpu.VMEM((128, TR // 16), BF16),
            pltpu.VMEM((TR // 16, 128), F32),
            DMA((steps,)),
            DMA((steps,)),
            DMA((3,)),
        ],
        compiler_params=params(),
        name="start",
    )(
        far(table), far(exps.T), far(classes), far(gain), far(jnp.asarray(row_pool(8, 8, 8, 0))),
        far(jnp.asarray(mgot)), far(jnp.asarray(mown)),
    )


def pick_kernel(after, weights, matrix_far, spread_far, rpool_far, matrix, spread_near, rpool, buf, sems):
    copies = (
        pltpu.make_async_copy(matrix_far.at[lax.axis_index("gy")], buf, sems.at[0]),
        pltpu.make_async_copy(spread_far, spread_near, sems.at[1]),
        pltpu.make_async_copy(rpool_far, rpool, sems.at[2]),
    )
    for copy in copies:
        copy.start()
    for copy in copies:
        copy.wait()
    m, count = 16 * NB, buf.shape[0]
    for level in range(3):
        at = slice(m * level, m * (level + 1) if level < 2 else count)
        scaled = buf[at] * weights[level]
        first = scaled.astype(BF16)
        matrix[at] = first
        low = slice(count + at.start, count + at.stop)
        matrix[low] = (scaled - first.astype(F32)).astype(BF16)


def pick(after, weights):
    table = row_matrices(NB, 0, BLK // 16, BLK // 16 + 2)
    count, width = table.shape[1:]
    more = [column_spread(), row_pool(NB, 16, BLK // 16, 1)]
    return pl.pallas_call(
        pick_kernel,
        in_specs=[HBM, SMEM] + [HBM] * 3,
        out_specs=[VMEM] * 3,
        out_shape=[pltpu.VMEM((2 * count, width), BF16)] + [pltpu.VMEM(t.shape, BF16) for t in more],
        scratch_shapes=[pltpu.VMEM((count, width), F32), DMA((3,))],
        compiler_params=params(),
        name="pick",
    )(near(after), far(weights), *[far(jnp.asarray(t)) for t in [table, *more]])


def side(strip_lo, strip_hi):
    rows = strip_lo.shape[1]
    empty = jnp.zeros((rows, 128 - 2 * HALO), F32)
    return jnp.concatenate([strip_hi.astype(F32).T, empty, strip_lo.astype(F32).T], axis=1)


def across_kernel(first, *refs):
    if first:
        tile, lo, hi, got, own, mgot, mown, send, part = refs
    else:
        _, got, own, mgot, mown, send, part = refs
    received = got[...].reshape(NX * 8, 128)
    z = dot(mgot[...], received, precision=EXACT)
    mine = dot(mown[...], own[...], precision=EXACT)
    z = jnp.concatenate([z[:40] + mine, z[40:]], axis=0).T
    part[...] = z[:80]
    lane = lax.broadcasted_iota(jnp.int32, (8, 128), 1)
    coarse = z[80:88]
    up = jnp.where(lane < 40, z[0:8], jnp.where(lane < 80, z[64:72], coarse))
    down = jnp.where(lane < 40, z[56:64], jnp.where(lane < 80, z[72:80], coarse))
    py = lax.axis_index("gy")
    for p in range(NY):
        send[p, :8] = jnp.where(p < py, up, down)
    if first:
        for n in range(EC // 128):
            lanes = slice(128 * n, 128 * n + 128)
            if n < TC // 128:
                top, bottom = tile[:HALO, lanes].astype(F32), tile[TR - HALO :, lanes].astype(F32)
            else:
                top = side(lo[:, :128], hi[:, :128])[:HALO]
                bottom = side(lo[:, TR - 128 :], hi[:, TR - 128 :])[128 - HALO :]
            for p in range(NY):
                send[p, 8 + HALO * n : 8 + HALO * (n + 1)] = jnp.where(p < py, top, bottom)


def across(first, extra, got, own, mgot, mown):
    count = 8 + HALO * (EC // 128) if first else 8
    specs = [VMEM] * 3 if first else [HBM]
    return pl.pallas_call(
        functools.partial(across_kernel, first),
        in_specs=specs + [VMEM] * 4,
        out_specs=[VMEM] * 2,
        out_shape=[pltpu.VMEM((NY, count, 128), F32), pltpu.VMEM((80, 128), F32)],
        compiler_params=params(),
        name="across",
    )(*([near(x) for x in extra] if first else [near(x) for x in extra]), near(got), near(own), near(mgot), near(mown))


def column_pass(block, cols, half, at):
    tile = [block[:, 128 * n : 128 * (n + 1)] for n in range(EC // 128)]
    join = lambda *which: jnp.concatenate([tile[n] for n in which], axis=1)
    half[at, :256] = dot(join(4, 0, 1, 2), cols[...]).astype(BF16)
    half[at, 256:512] = dot(join(1, 2, 3, 4), cols[...]).astype(BF16)
    if half.shape[1] > TC:
        half[at, 512:] = dot(join(3, 4, 0), cols[:384, :128]).astype(BF16)


def first_half_kernel(tile, lo, hi, cols_far, half_far, dose_far, half, dose, cols, sems, csem):
    load = pltpu.make_async_copy(cols_far, cols, csem)
    load.start()
    stores = []
    for n in range(TR // SB):
        rows, begin = slice(n * SB, (n + 1) * SB), HALO + n * SB
        dose[begin : begin + SB, :TC] = tile[rows]
        dose[begin : begin + SB, TC:] = side(lo[:, rows], hi[:, rows]).astype(BF16)
        if n == 0:
            load.wait()
        column_pass(dose[begin : begin + SB], cols, half, slice(begin, begin + SB))
        at = pl.ds(begin, SB)
        stores.append(pltpu.make_async_copy(half.at[at], half_far.at[at], sems.at[0, n]))
        stores[-1].start()
        stores.append(pltpu.make_async_copy(dose.at[at], dose_far.at[at], sems.at[1, n]))
        stores[-1].start()
    for copy in stores:
        copy.wait()


def half_cost():
    return pl.CostEstimate(flops=4 * ER * EC * EC, bytes_accessed=6 * ER * EC, transcendentals=0)


def first_half(tile, lo, hi):
    return pl.pallas_call(
        first_half_kernel,
        in_specs=[VMEM] * 3 + [HBM],
        out_specs=[HBM, HBM],
        out_shape=[pltpu.HBM((ER, EC), BF16)] * 2,
        scratch_shapes=[
            pltpu.VMEM((ER, EC), BF16),
            pltpu.VMEM((ER, EC), BF16),
            pltpu.VMEM((512, 256), BF16),
            DMA((2, TR // SB)),
            DMA,
        ],
        compiler_params=params(),
        cost_estimate=half_cost(),
        name="first_half",
    )(near(tile), near(lo), near(hi), far(jnp.asarray(fine_columns())))


def half_kernel(dose, cols_far, half, cols, csem):
    load = pltpu.make_async_copy(cols_far, cols, csem)
    load.start()
    load.wait()
    for b in range(NB):
        column_pass(dose[b * BLK : (b + 1) * BLK], cols, half, slice(b * BLK, (b + 1) * BLK))


def half_of(dose, lanes):
    return pl.pallas_call(
        half_kernel,
        in_specs=[VMEM, HBM],
        out_specs=VMEM,
        out_shape=pltpu.VMEM((ER, lanes), BF16),
        scratch_shapes=[pltpu.VMEM((512, 256), BF16), DMA],
        compiler_params=params(),
        cost_estimate=half_cost(),
        name="half",
    )(near(dose), far(jnp.asarray(fine_columns())))


def spread(received, part, matrix, cols, groups):
    m = 16 * groups
    count = matrix.shape[0] // 2
    x, rest, _ = pieces(jnp.concatenate([received, part[...]], axis=0))
    both = dot(matrix[...], x)
    y = both[:count] + both[count:] + dot(matrix[:count], rest)
    lane = lax.broadcasted_iota(jnp.int32, (m, 128), 1)
    fourth = jnp.where(lane < 120, y[2 * m : 3 * m], jnp.where(lane == 120, y[3 * m : 3 * m + 1], 0.0))
    a, b, _ = pieces(jnp.where(lane < 40, y[:m], jnp.where(lane < 80, y[m : 2 * m], fourth)))
    return dot(a, cols) + dot(b, cols)


def short_range(b, rows, half):
    begin = min(max(b * BLK - 16, 0), ER - BLK - 32)
    return dot(rows[(b * BLK - begin) // 16], half[begin : begin + BLK + 32])


def update(b, old_rows, short, grid, out, skip):
    count, lanes = out.shape
    t = (lax.broadcasted_iota(jnp.int32, (8, lanes), 0).astype(F32) + 0.5) / 16.0
    for n in range(BLK // 16):
        row = b * BLK + 16 * n
        if not skip <= row < skip + count:
            continue
        a, m, c = (grid[16 * b + n + k : 16 * b + n + k + 1] for k in range(3))
        back = jnp.concatenate([a + (t + 0.5) * (m - a), m + t * (c - m)], axis=0)
        full = 1.0 + (short[16 * n : 16 * n + 16] + back)
        out[row - skip : row - skip + 16] = (old_rows(row).astype(F32) * 2.0 / full).astype(out.dtype)


def step_kernel(first, got, part, matrix, cols, rpool, dose, half, *refs):
    if first:
        fcols_far, out, send, own, rows, cpool, grid, sums, hbuf, dbuf, fcols, lsem, fsem = refs
        loads = [pltpu.make_async_copy(fcols_far, fcols, fsem)]
        at = pl.ds(HALO, TR)
        loads.append(pltpu.make_async_copy(half.at[at], hbuf.at[at], lsem.at[0]))
        loads.append(pltpu.make_async_copy(dose.at[at], dbuf.at[at], lsem.at[1]))
        for copy in loads:
            copy.start()
    else:
        out, send, own, rows, cpool, grid, sums = refs
        dbuf, hbuf = dose, half
    fill_rows(rows)
    fill_pool(cpool)
    received = got[:, :8].reshape(NY * 8, 128)
    grid[...] = spread(received, part, matrix, cols[...], NB)
    if first:
        py = lax.axis_index("gy")
        loads[0].wait()
        for row, p, real in ((0, jnp.maximum(py - 1, 0), py > 0), (ER - HALO, jnp.minimum(py + 1, NY - 1), py < NY - 1)):
            tiles = [got[p, 8 + HALO * n : 8 + HALO * (n + 1)] for n in range(EC // 128)]
            values = jnp.where(real, jnp.concatenate(tiles, axis=1), 0.0).astype(BF16)
            dbuf[row : row + HALO] = values
            column_pass(values, fcols, hbuf, slice(row, row + HALO))
        for copy in loads[1:]:
            copy.wait()
    for b in range(NB):
        update(b, lambda row: dbuf[row : row + 16], short_range(b, rows, hbuf), grid, out, 0)
        pooled = dot(out[b * BLK : (b + 1) * BLK], cpool[...])
        pooled = jnp.sum(pooled.reshape(BLK // 16, 16, 128), axis=1)
        sums[16 * b : 16 * b + 16] = jnp.concatenate([pooled, jnp.zeros((16 - BLK // 16, 128), F32)], axis=0)
    pooled_out(sums[...], rpool, lax.axis_index("gx"), send, own)


def step(first, got, part, dose, half, ops):
    scratch = [
        pltpu.VMEM((3, BLK, BLK + 32), BF16),
        pltpu.VMEM((EC, 128), BF16),
        pltpu.VMEM((NB * 16, EC), F32),
        pltpu.VMEM((NB * 16, 128), F32),
    ]
    if first:
        scratch += [pltpu.VMEM((ER, EC), BF16)] * 2 + [pltpu.VMEM((512, 256), BF16), DMA((2,)), DMA]
    place = far if first else near
    return pl.pallas_call(
        functools.partial(step_kernel, first),
        in_specs=[VMEM] * 5 + ([HBM] * 3 if first else [VMEM] * 2),
        out_specs=[VMEM] * 3,
        out_shape=[
            pltpu.VMEM((ER, EC), BF16),
            pltpu.HBM((NX, 8, 128), F32),
            pltpu.VMEM((32, 128), F32),
        ],
        scratch_shapes=scratch,
        input_output_aliases={} if first else {5: 0},
        compiler_params=params(),
        name="first_step" if first else "step",
    )(
        near(got), near(part), *[near(x) for x in ops], place(dose), place(half),
        *([far(jnp.asarray(fine_columns()))] if first else []),
    )


def finish_kernel(got, part, matrix, cols, dose, half, out, rows, made, grid, ssem):
    fill_rows(rows)
    grid[...] = spread(got[...].reshape(NY * 8, 128), part, matrix, cols[:, :TC], NB)
    stores = []
    for b in range(NB):
        update(b, lambda row: dose[row : row + 16, :TC], short_range(b, rows, half), grid, made, HALO)
        begin, end = max(b * BLK - HALO, 0), min((b + 1) * BLK - HALO, TR)
        at = pl.ds(begin, end - begin)
        stores.append(pltpu.make_async_copy(made.at[at], out.at[at], ssem.at[b]))
        stores[-1].start()
    for copy in stores:
        copy.wait()


def finish(got, part, dose, half, ops):
    return pl.pallas_call(
        finish_kernel,
        in_specs=[VMEM] * 6,
        out_specs=HBM,
        out_shape=pltpu.HBM((TR, TC), F32),
        scratch_shapes=[
            pltpu.VMEM((3, BLK, BLK + 32), BF16),
            pltpu.VMEM((TR, TC), F32),
            pltpu.VMEM((NB * 16, TC), F32),
            DMA((NB,)),
        ],
        compiler_params=params(),
        name="finish",
    )(near(got), near(part), near(ops[0]), near(ops[1]), near(dose), near(half))


def shifted(x, axis, by):
    n = lax.axis_size(axis)
    return lax.ppermute(x, axis, [(i, i + by) for i in range(n) if 0 <= i + by < n])


def exchanged(x, axis):
    return lax.all_to_all(x, axis, 0, 0, tiled=True)


def local(classes, exponents, gain_field, level_table, level_weights):
    tile, lo, hi, send, own, mgot, mown = start(level_table, exponents, classes, gain_field)
    left, right = shifted(hi, "gx", 1), shifted(lo, "gx", -1)
    got = exchanged(send, "gx")
    send, part = across(True, (tile, left, right), got, own, mgot, mown)
    got = exchanged(send, "gy")
    ops = pick(part, level_weights)
    half, dose = first_half(tile, left, right)
    dose, send, own = step(True, got, part, dose, half, ops)
    for sweep in range(2, ITERS + 1):
        got = exchanged(send, "gx")
        half = half_of(dose, EC if sweep < ITERS else TC)
        send, part = across(False, (half,), got, own, mgot, mown)
        got = exchanged(send, "gy")
        if sweep < ITERS:
            dose, send, own = step(False, got, part, dose, half, ops)
    return finish(got, part, dose, half, ops)


def solution(mesh):
    in_specs = (P("gy", "gx"), P("gy", "gx"), P("gy", "gx"), P(), P())
    return jax.shard_map(local, mesh=mesh, in_specs=in_specs, out_specs=P("gy", "gx"), check_vma=False)
```

```python
import functools

import jax
import jax.numpy as jnp
import ml_dtypes
import numpy as np
from jax import lax
from jax.experimental import pallas as pl
from jax.experimental.pallas import tpu as pltpu
from jax.sharding import PartitionSpec as P

HW = 4
CLASSES = 8
SB = 128
ITERS = 4
NX, NY = 32, 8
TR, TC = 1024, 512
HALO = HW * ITERS
ER = TR + 2 * HALO
EC = TC + 128
BLK = 176
NB = ER // BLK
QC, QR = 36, 68
F32, BF16 = jnp.float32, jnp.bfloat16
EXACT = lax.Precision.HIGHEST


def gauss_taps():
    offsets = np.arange(-HW, HW + 1).astype(np.float32)
    weights = np.exp(-(offsets * offsets) / np.float32(HW * HW)).astype(np.float32)
    return weights / weights.sum(dtype=np.float32)


def blur_operator(n):
    taps = gauss_taps().astype(np.float64)
    out = np.zeros((n, n))
    for k in range(-HW, HW + 1):
        out += taps[k + HW] * np.eye(n, k=k)
    return out


def up_operator(n, factor):
    target = np.arange(n * factor)
    lower = (target - factor // 2) // factor
    t = (target - factor // 2 - factor * lower + 0.5) / factor
    out = np.zeros((n * factor, n))
    np.add.at(out, (target, np.clip(lower, 0, n - 1)), 1 - t)
    np.add.at(out, (target, np.clip(lower + 1, 0, n - 1)), t)
    return out


def level_operators(n_second):
    third, fourth = n_second // 4, n_second // 16
    return (
        blur_operator(n_second),
        up_operator(third, 4) @ blur_operator(third),
        up_operator(third, 4) @ up_operator(fourth, 4) @ blur_operator(fourth),
    )


@functools.cache
def column_matrices():
    second, third, fourth = level_operators(NX * 32)
    got = np.zeros((NX, 128, 256), np.float32)
    own = np.zeros((NX, 40, 32), np.float32)
    for px in range(NX):
        for q in range(QC):
            g = min(max(32 * px + q - 2, 0), NX * 32 - 1)
            for s in np.nonzero(second[g])[0]:
                p, j = divmod(int(s), 32)
                if p == px:
                    own[px, q, j] = second[g, s]
                else:
                    assert j >= 24 if p < px else j < 8
                    got[px, q, p * 8 + j % 8] = second[g, s]
            got[px, 40 + q] = third[g]
            for j in range(2):
                got[px, 80 + q, j::8] = fourth[g, j::2]
        got[px, 120, 0::8] = 1
        got[px, 120, 1::8] = 1
    return got, own


QM = QR + 4


def row_matrices():
    second, third, fourth = level_operators(NY * 64)
    out = np.zeros((NY, 3 * QM + 8, 144), np.float32)
    for py in range(NY):
        for q in range(QR):
            g = min(max(64 * py + q - 2, 0), NY * 64 - 1)
            for s in np.nonzero(second[g])[0]:
                p, j = divmod(int(s), 64)
                assert p == py or (j >= 56 if p < py else j < 8)
                out[py, q, 64 + j if p == py else p * 8 + j % 8] = second[g, s]
            for s in np.nonzero(third[g])[0]:
                p, j = divmod(int(s), 16)
                assert p == py or (j >= 8 if p < py else j < 8)
                out[py, QM + q, 128 + j if p == py else p * 8 + j % 8] = third[g, s]
            for s in np.nonzero(fourth[g])[0]:
                p, j = divmod(int(s), 4)
                out[py, 2 * QM + q, p * 8 + j] = fourth[g, s]
        out[py, 3 * QM, 4:64:8] = 1
    return out


@functools.cache
def column_spread():
    out = np.zeros((128, EC), np.float32)
    for lane in range(EC):
        cell = lane if lane < TC + HALO else lane - EC
        if cell < -HALO:
            continue
        lower = (cell - 8) // 16
        t = (cell - 8 - 16 * lower + 0.5) / 16
        for level in range(3):
            out[40 * level + lower + 2, lane] += 1 - t
            out[40 * level + lower + 3, lane] += t
        out[120, lane] = 1
    return out.astype(ml_dtypes.bfloat16)


@functools.cache
def row_pool(groups, stride, real, first):
    out = np.zeros((128, groups * stride), np.float32)
    for b in range(groups):
        for k in range(real):
            s = b * real + k - first
            if 0 <= s < TR // 16:
                at = b * stride + k
                out[s, at] = 2.0**-8
                out[64 + s // 4, at] = 2.0**-12
                out[80 + s // 16, at] = 2.0**-16
                out[84, at] = 1.0 / (TR * NY * TC * NX)
    return out.astype(ml_dtypes.bfloat16)


def fine_taps():
    return gauss_taps().astype(ml_dtypes.bfloat16)


@functools.cache
def fine_columns():
    out = np.zeros((512, 256), ml_dtypes.bfloat16)
    taps, lane = fine_taps(), np.arange(256)
    for k in range(-HW, HW + 1):
        out[lane + 128 + k, lane] = taps[k + HW]
    return out


VMEM = pl.BlockSpec(memory_space=pltpu.VMEM)
SMEM = pl.BlockSpec(memory_space=pltpu.SMEM)
HBM = pl.BlockSpec(memory_space=pl.ANY)
DMA = pltpu.SemaphoreType.DMA


def params(mib=24):
    return pltpu.CompilerParams(vmem_limit_bytes=mib * 2**20)


def near(x):
    return pltpu.with_memory_space_constraint(x, pltpu.VMEM)


def far(x):
    return pltpu.with_memory_space_constraint(x, pltpu.HBM)


def dot(a, b, **kw):
    return jnp.dot(a, b, preferred_element_type=F32, **kw)


def pieces(x):
    first = x.astype(BF16)
    rest = x - first.astype(F32)
    second = rest.astype(BF16)
    return first, second, (rest - second.astype(F32)).astype(BF16)


def fill_rows(rows):
    shape = (BLK, BLK + 32)
    shift = lax.broadcasted_iota(jnp.int32, shape, 1) - lax.broadcasted_iota(jnp.int32, shape, 0)
    for which in range(3):
        band = jnp.zeros(shape, F32)
        for k in range(-HW, HW + 1):
            band = jnp.where(shift == 16 * which + k, float(fine_taps()[k + HW]), band)
        rows[which] = band.astype(BF16)


def fill_pool(cpool):
    col = lax.broadcasted_iota(jnp.int32, cpool.shape, 0)
    lane = lax.broadcasted_iota(jnp.int32, cpool.shape, 1)
    group = jnp.where(lane < 32, col >> 4, jnp.where(lane < 40, 32 + (col >> 6), 40 + (col >> 8)))
    cpool[...] = jnp.where((group == lane) & (col < TC), 1.0, 0.0).astype(BF16)


def pooled_out(sums, row_pool_ref, px, send_ref, own_ref, corners=None):
    a, b, c = pieces(sums)
    rows = row_pool_ref[...]
    pooled = (dot(rows, a) + dot(rows, b) + dot(rows, c)).T
    own_ref[...] = pooled[:32]
    lane = lax.broadcasted_iota(jnp.int32, (8, 128), 1)
    coarse = jnp.where(lane < 80, pooled[32:40], pooled[40:48])
    left = jnp.where(lane < 64, pooled[0:8], coarse)
    right = jnp.where(lane < 64, pooled[24:32], coarse)
    for p in range(NX):
        send_ref[p, :8] = jnp.where(p < px, left, right)
        if corners is not None:
            send_ref[p, 8:] = jnp.where(p < px, *corners)


def corner(strip):
    lane = lax.broadcasted_iota(jnp.int32, (8, 128), 1)
    both = jnp.where(lane < 64, strip[:8, :128].astype(F32), strip[:8, TR - 128 :].astype(F32))
    more = jnp.where(lane < 64, strip[8:, :128].astype(F32), strip[8:, TR - 128 :].astype(F32))
    inner = jnp.where(lane < 64, pltpu.roll(more, 16, 1), pltpu.roll(more, 112, 1))
    return jnp.where((lane < 16) | (lane >= 112), both, inner)


def start_kernel(table, exps, weights, classes, gain, *refs):
    fars, refs = refs[:6], refs[6:]
    dose, top, bottom, lo, hi, send, own, mgot, mown, matrix, spread_near, rpool_later = refs[:12]
    cbuf, gbuf, cpool, rpool, sums, csem, gsem, tsem = refs[12:]
    steps = TR // SB
    px, py = lax.axis_index("gx"), lax.axis_index("gy")
    loads = []
    for i in range(steps):
        rows = pl.ds(i * SB, SB)
        loads.append(
            (
                pltpu.make_async_copy(classes.at[rows], cbuf.at[rows], csem.at[i]),
                pltpu.make_async_copy(gain.at[rows], gbuf.at[rows], gsem.at[i]),
            )
        )
        for copy in loads[-1]:
            copy.start()
    nears = (rpool, mgot, mown, matrix, spread_near, rpool_later)
    index = (None, px, px, py, None, None)
    tables = []
    for i in range(6):
        source = fars[i] if index[i] is None else fars[i].at[index[i]]
        tables.append(pltpu.make_async_copy(source, nears[i], tsem.at[i]))
        tables[-1].start()
    fill_pool(cpool)
    for i in range(steps):
        for copy in loads[i]:
            copy.wait()
        rows = slice(i * SB, (i + 1) * SB)
        for k in range(TC // SB):
            e = exps[k, i]
            scale = jnp.where(e > 0, 2.0, jnp.where(e < 0, 0.5, 1.0)).astype(F32)
            at = slice(k * SB, (k + 1) * SB)
            c = cbuf[rows, at]
            level = jnp.zeros((SB, SB), F32)
            for j in range(1, CLASSES):
                level = jnp.where(c == j, table[j] * scale, level)
            value = (level * gbuf[rows, at].astype(F32)).astype(BF16)
            dose[rows, at] = value
            if k == 0:
                lo[:, rows] = value.astype(F32).T[:HALO].astype(BF16)
            if k == TC // SB - 1:
                hi[:, rows] = value.astype(F32).T[SB - HALO :].astype(BF16)
        across = dot(dose[rows], cpool[...])
        sums[8 * i : 8 * i + 8] = jnp.sum(across.reshape(8, 16, 128), axis=1)
    top[...] = dose[:HALO]
    bottom[...] = dose[TR - HALO :]
    for copy in tables:
        copy.wait()
    for level in range(3):
        at = slice(QM * level, QM * (level + 1) if level < 2 else matrix.shape[0])
        matrix[at] = matrix[at] * weights[level]
    pooled_out(sums[...], rpool, px, send, own, (corner(lo), corner(hi)))


def start(table, exps, weights, classes, gain):
    steps = TR // SB
    mgot, mown = column_matrices()
    rows, cols, rpool = row_matrices(), column_spread(), row_pool(NB, 16, BLK // 16, 1)
    return pl.pallas_call(
        start_kernel,
        in_specs=[SMEM, SMEM, SMEM] + [HBM] * 8,
        out_specs=[VMEM] * 12,
        out_shape=[
            pltpu.VMEM((TR, TC), BF16),
            pltpu.VMEM((HALO, TC), BF16),
            pltpu.VMEM((HALO, TC), BF16),
            pltpu.VMEM((HALO, TR), BF16),
            pltpu.VMEM((HALO, TR), BF16),
            pltpu.HBM((NX, 16, 128), F32),
            pltpu.VMEM((32, 128), F32),
            pltpu.VMEM(mgot.shape[1:], F32),
            pltpu.VMEM(mown.shape[1:], F32),
            pltpu.VMEM(rows.shape[1:], F32),
            pltpu.VMEM(cols.shape, BF16),
            pltpu.VMEM(rpool.shape, BF16),
        ],
        scratch_shapes=[
            pltpu.VMEM((TR, TC), jnp.int32),
            pltpu.VMEM((TR, TC), BF16),
            pltpu.VMEM((TC, 128), BF16),
            pltpu.VMEM((128, TR // 16), BF16),
            pltpu.VMEM((TR // 16, 128), F32),
            DMA((steps,)),
            DMA((steps,)),
            DMA((6,)),
        ],
        compiler_params=params(),
        name="start",
    )(
        far(table), far(exps.T), far(weights), far(classes), far(gain),
        *[far(jnp.asarray(t)) for t in (row_pool(8, 8, 8, 0), mgot, mown, rows, cols, rpool)],
    )


def side(strip_lo, strip_hi):
    rows = strip_lo.shape[1]
    empty = jnp.zeros((rows, 128 - 2 * HALO), F32)
    return jnp.concatenate([strip_hi.astype(F32).T, empty, strip_lo.astype(F32).T], axis=1)


def across_kernel(first, *refs):
    if first:
        got, own, mgot, mown, send, part = refs
    else:
        _, got, own, mgot, mown, send, part = refs
    received = got[:, :8].reshape(NX * 8, 128)
    z = dot(mgot[...], received, precision=EXACT)
    mine = dot(mown[...], own[...], precision=EXACT)
    z = jnp.concatenate([z[:40] + mine, z[40:]], axis=0).T
    part[...] = z[:80]
    lane = lax.broadcasted_iota(jnp.int32, (8, 128), 1)
    coarse = z[80:88]
    up = jnp.where(lane < 40, z[0:8], jnp.where(lane < 80, z[64:72], coarse))
    down = jnp.where(lane < 40, z[56:64], jnp.where(lane < 80, z[72:80], coarse))
    px, py = lax.axis_index("gx"), lax.axis_index("gy")
    for p in range(NY):
        send[p, :8] = jnp.where(p < py, up, down)
    if first:
        lo = jnp.where(px > 0, got[jnp.maximum(px - 1, 0), 8:], 0.0)
        hi = jnp.where(px < NX - 1, got[jnp.minimum(px + 1, NX - 1), 8:], 0.0)
        ends = []
        for shift in (112, 16):
            ends.append(side(*[jnp.concatenate([x, pltpu.roll(x, shift, 1)], axis=0) for x in (lo, hi)]))
        for p in range(NY):
            send[p, 8:] = jnp.where(p < py, ends[0][:HALO], ends[1][128 - HALO :])


def across(first, extra, got, own, mgot, mown):
    count = 8 + HALO if first else 8
    return pl.pallas_call(
        functools.partial(across_kernel, first),
        in_specs=[VMEM] * 4 if first else [HBM] + [VMEM] * 4,
        out_specs=[VMEM] * 2,
        out_shape=[pltpu.VMEM((NY, count, 128), F32), pltpu.VMEM((80, 128), F32)],
        compiler_params=params(),
        name="across",
    )(*([] if first else [near(extra)]), near(got), near(own), near(mgot), near(mown))


def column_pass(block, cols, half, at):
    tile = [block[:, 128 * n : 128 * (n + 1)] for n in range(EC // 128)]
    join = lambda *which: jnp.concatenate([tile[n] for n in which], axis=1)
    half[at, :256] = dot(join(4, 0, 1, 2), cols[...]).astype(BF16)
    half[at, 256:512] = dot(join(1, 2, 3, 4), cols[...]).astype(BF16)
    if half.shape[1] > TC:
        half[at, 512:] = dot(join(3, 4, 0), cols[:384, :128]).astype(BF16)


def first_half_kernel(tile, lo, hi, cols_far, half_far, dose_far, half, dose, cols, sems, csem):
    load = pltpu.make_async_copy(cols_far, cols, csem)
    load.start()
    stores = []
    for n in range(TR // SB):
        rows, begin = slice(n * SB, (n + 1) * SB), HALO + n * SB
        dose[begin : begin + SB, :TC] = tile[rows]
        dose[begin : begin + SB, TC:] = side(lo[:, rows], hi[:, rows]).astype(BF16)
        if n == 0:
            load.wait()
        column_pass(dose[begin : begin + SB], cols, half, slice(begin, begin + SB))
        at = pl.ds(begin, SB)
        stores.append(pltpu.make_async_copy(half.at[at], half_far.at[at], sems.at[0, n]))
        stores[-1].start()
        stores.append(pltpu.make_async_copy(dose.at[at], dose_far.at[at], sems.at[1, n]))
        stores[-1].start()
    for copy in stores:
        copy.wait()


def half_cost():
    return pl.CostEstimate(flops=4 * ER * EC * EC, bytes_accessed=6 * ER * EC, transcendentals=0)


def first_half(tile, lo, hi):
    return pl.pallas_call(
        first_half_kernel,
        in_specs=[VMEM] * 3 + [HBM],
        out_specs=[HBM, HBM],
        out_shape=[pltpu.HBM((ER, EC), BF16)] * 2,
        scratch_shapes=[
            pltpu.VMEM((ER, EC), BF16),
            pltpu.VMEM((ER, EC), BF16),
            pltpu.VMEM((512, 256), BF16),
            DMA((2, TR // SB)),
            DMA,
        ],
        compiler_params=params(),
        cost_estimate=half_cost(),
        name="first_half",
    )(near(tile), near(lo), near(hi), far(jnp.asarray(fine_columns())))


def half_kernel(dose, cols_far, half, cols, csem):
    load = pltpu.make_async_copy(cols_far, cols, csem)
    load.start()
    load.wait()
    for b in range(NB):
        column_pass(dose[b * BLK : (b + 1) * BLK], cols, half, slice(b * BLK, (b + 1) * BLK))


def half_of(dose, lanes):
    return pl.pallas_call(
        half_kernel,
        in_specs=[VMEM, HBM],
        out_specs=VMEM,
        out_shape=pltpu.VMEM((ER, lanes), BF16),
        scratch_shapes=[pltpu.VMEM((512, 256), BF16), DMA],
        compiler_params=params(),
        cost_estimate=half_cost(),
        name="half",
    )(near(dose), far(jnp.asarray(fine_columns())))


def spread(received, part, matrix, cols):
    y = dot(matrix[...], jnp.concatenate([received, part[...]], axis=0), precision=EXACT)
    lane = lax.broadcasted_iota(jnp.int32, (QM, 128), 1)
    fourth = jnp.where(lane < 120, y[2 * QM : 3 * QM], jnp.where(lane == 120, y[3 * QM : 3 * QM + 1], 0.0))
    a, b, c = pieces(jnp.where(lane < 40, y[:QM], jnp.where(lane < 80, y[QM : 2 * QM], fourth)))
    return dot(a, cols) + dot(b, cols) + dot(c, cols)


def short_range(b, rows, half):
    begin = min(max(b * BLK - 16, 0), ER - BLK - 32)
    return dot(rows[(b * BLK - begin) // 16], half[begin : begin + BLK + 32])


def update(b, old_rows, short, grid, out, skip):
    count, lanes = out.shape
    t = (lax.broadcasted_iota(jnp.int32, (8, lanes), 0).astype(F32) + 0.5) / 16.0
    for n in range(BLK // 16):
        row = b * BLK + 16 * n
        if not skip <= row < skip + count:
            continue
        at = row // 16
        a, m, c = (grid[at + k : at + k + 1] for k in range(3))
        back = jnp.concatenate([a + (t + 0.5) * (m - a), m + t * (c - m)], axis=0)
        full = 1.0 + (short[16 * n : 16 * n + 16] + back)
        out[row - skip : row - skip + 16] = (old_rows(row).astype(F32) * 2.0 / full).astype(out.dtype)


def step_kernel(first, got, part, matrix, cols, rpool, dose, half, *refs):
    if first:
        above, below, fcols_far, out, send, own, rows, cpool, grid, sums, hbuf, dbuf, fcols, lsem, fsem = refs
        loads = [pltpu.make_async_copy(fcols_far, fcols, fsem)]
        at = pl.ds(HALO, TR)
        loads.append(pltpu.make_async_copy(half.at[at], hbuf.at[at], lsem.at[0]))
        loads.append(pltpu.make_async_copy(dose.at[at], dbuf.at[at], lsem.at[1]))
        for copy in loads:
            copy.start()
    else:
        out, send, own, rows, cpool, grid, sums = refs
        dbuf, hbuf = dose, half
    fill_rows(rows)
    fill_pool(cpool)
    received = got[:, :8].reshape(NY * 8, 128)
    grid[...] = spread(received, part, matrix, cols[...])
    if first:
        py = lax.axis_index("gy")
        loads[0].wait()
        for row, strip, p, real in (
            (0, above, jnp.maximum(py - 1, 0), py > 0),
            (ER - HALO, below, jnp.minimum(py + 1, NY - 1), py < NY - 1),
        ):
            beside = jnp.where(real, got[p, 8:], 0.0).astype(BF16)
            values = jnp.concatenate([strip[...], beside], axis=1)
            dbuf[row : row + HALO] = values
            column_pass(values, fcols, hbuf, slice(row, row + HALO))
        for copy in loads[1:]:
            copy.wait()
    for b in range(NB):
        update(b, lambda row: dbuf[row : row + 16], short_range(b, rows, hbuf), grid, out, 0)
        pooled = dot(out[b * BLK : (b + 1) * BLK], cpool[...])
        pooled = jnp.sum(pooled.reshape(BLK // 16, 16, 128), axis=1)
        sums[16 * b : 16 * b + 16] = jnp.concatenate([pooled, jnp.zeros((16 - BLK // 16, 128), F32)], axis=0)
    pooled_out(sums[...], rpool, lax.axis_index("gx"), send, own)


def step(got, part, dose, half, ops, strips=None):
    first = strips is not None
    scratch = [
        pltpu.VMEM((3, BLK, BLK + 32), BF16),
        pltpu.VMEM((EC, 128), BF16),
        pltpu.VMEM((QM, EC), F32),
        pltpu.VMEM((NB * 16, 128), F32),
    ]
    if first:
        scratch += [pltpu.VMEM((ER, EC), BF16)] * 2 + [pltpu.VMEM((512, 256), BF16), DMA((2,)), DMA]
    place = far if first else near
    return pl.pallas_call(
        functools.partial(step_kernel, first),
        in_specs=[VMEM] * 5 + ([HBM] * 2 + [VMEM] * 2 + [HBM] if first else [VMEM] * 2),
        out_specs=[VMEM] * 3,
        out_shape=[
            pltpu.VMEM((ER, EC), BF16),
            pltpu.HBM((NX, 8, 128), F32),
            pltpu.VMEM((32, 128), F32),
        ],
        scratch_shapes=scratch,
        input_output_aliases={} if first else {5: 0},
        compiler_params=params(),
        name="first_step" if first else "step",
    )(
        near(got), near(part), *[near(x) for x in ops], place(dose), place(half),
        *([*[near(x) for x in strips], far(jnp.asarray(fine_columns()))] if first else []),
    )


def finish_kernel(got, part, matrix, cols, dose, half, out, rows, made, grid, ssem):
    fill_rows(rows)
    grid[...] = spread(got[...].reshape(NY * 8, 128), part, matrix, cols[:, :TC])
    stores = []
    for b in range(NB):
        update(b, lambda row: dose[row : row + 16, :TC], short_range(b, rows, half), grid, made, HALO)
        begin, end = max(b * BLK - HALO, 0), min((b + 1) * BLK - HALO, TR)
        at = pl.ds(begin, end - begin)
        stores.append(pltpu.make_async_copy(made.at[at], out.at[at], ssem.at[b]))
        stores[-1].start()
    for copy in stores:
        copy.wait()


def finish(got, part, dose, half, ops):
    return pl.pallas_call(
        finish_kernel,
        in_specs=[VMEM] * 6,
        out_specs=HBM,
        out_shape=pltpu.HBM((TR, TC), F32),
        scratch_shapes=[
            pltpu.VMEM((3, BLK, BLK + 32), BF16),
            pltpu.VMEM((TR, TC), F32),
            pltpu.VMEM((QM, TC), F32),
            DMA((NB,)),
        ],
        compiler_params=params(),
        name="finish",
    )(near(got), near(part), near(ops[0]), near(ops[1]), near(dose), near(half))


def shifted(x, axis, by):
    n = lax.axis_size(axis)
    return lax.ppermute(x, axis, [(i, i + by) for i in range(n) if 0 <= i + by < n])


def exchanged(x, axis):
    return lax.all_to_all(x, axis, 0, 0, tiled=True)


def local(classes, exponents, gain_field, level_table, level_weights):
    tile, top, bottom, lo, hi, send, own, mgot, mown, *ops = start(
        level_table, exponents, level_weights, classes, gain_field
    )
    left, right = shifted(hi, "gx", 1), shifted(lo, "gx", -1)
    above, below = shifted(bottom, "gy", 1), shifted(top, "gy", -1)
    got = exchanged(send, "gx")
    send, part = across(True, None, got, own, mgot, mown)
    got = exchanged(send, "gy")
    half, dose = first_half(tile, left, right)
    dose, send, own = step(got, part, dose, half, ops, (above, below))
    for sweep in range(2, ITERS + 1):
        got = exchanged(send, "gx")
        half = half_of(dose, EC if sweep < ITERS else TC)
        send, part = across(False, half, got, own, mgot, mown)
        got = exchanged(send, "gy")
        if sweep < ITERS:
            dose, send, own = step(got, part, dose, half, ops)
    return finish(got, part, dose, half, ops)


def solution(mesh):
    in_specs = (P("gy", "gx"), P("gy", "gx"), P("gy", "gx"), P(), P())
    return jax.shard_map(local, mesh=mesh, in_specs=in_specs, out_specs=P("gy", "gx"), check_vma=False)
```

```python
import functools

import jax
import jax.numpy as jnp
import ml_dtypes
import numpy as np
from jax import lax
from jax.experimental import pallas as pl
from jax.experimental.pallas import tpu as pltpu
from jax.sharding import PartitionSpec as P

HW = 4
CLASSES = 8
SB = 128
ITERS = 4
NX, NY = 32, 8
TR, TC = 1024, 512
HALO = HW * ITERS
ER = TR + 2 * HALO
EC = TC + 128
BLK = 176
NB = ER // BLK
QC, QR = 36, 68
F32, BF16 = jnp.float32, jnp.bfloat16
EXACT = lax.Precision.HIGHEST


def gauss_taps():
    offsets = np.arange(-HW, HW + 1).astype(np.float32)
    weights = np.exp(-(offsets * offsets) / np.float32(HW * HW)).astype(np.float32)
    return weights / weights.sum(dtype=np.float32)


def blur_operator(n):
    taps = gauss_taps().astype(np.float64)
    out = np.zeros((n, n))
    for k in range(-HW, HW + 1):
        out += taps[k + HW] * np.eye(n, k=k)
    return out


def up_operator(n, factor):
    target = np.arange(n * factor)
    lower = (target - factor // 2) // factor
    t = (target - factor // 2 - factor * lower + 0.5) / factor
    out = np.zeros((n * factor, n))
    np.add.at(out, (target, np.clip(lower, 0, n - 1)), 1 - t)
    np.add.at(out, (target, np.clip(lower + 1, 0, n - 1)), t)
    return out


def level_operators(n_second):
    third, fourth = n_second // 4, n_second // 16
    return (
        blur_operator(n_second),
        up_operator(third, 4) @ blur_operator(third),
        up_operator(third, 4) @ up_operator(fourth, 4) @ blur_operator(fourth),
    )


@functools.cache
def column_matrices():
    second, third, fourth = level_operators(NX * 32)
    got = np.zeros((NX, 128, 256), np.float32)
    own = np.zeros((NX, 40, 32), np.float32)
    for px in range(NX):
        for q in range(QC):
            g = min(max(32 * px + q - 2, 0), NX * 32 - 1)
            for s in np.nonzero(second[g])[0]:
                p, j = divmod(int(s), 32)
                if p == px:
                    own[px, q, j] = second[g, s]
                else:
                    assert j >= 24 if p < px else j < 8
                    got[px, q, p * 8 + j % 8] = second[g, s]
            got[px, 40 + q] = third[g]
            for j in range(2):
                got[px, 80 + q, j::8] = fourth[g, j::2]
        got[px, 120, 0::8] = 1
        got[px, 120, 1::8] = 1
    return got, own


QM = QR + 4


def row_matrices():
    second, third, fourth = level_operators(NY * 64)
    out = np.zeros((NY, 3 * QM + 8, 144), np.float32)
    for py in range(NY):
        for q in range(QR):
            g = min(max(64 * py + q - 2, 0), NY * 64 - 1)
            for s in np.nonzero(second[g])[0]:
                p, j = divmod(int(s), 64)
                assert p == py or (j >= 56 if p < py else j < 8)
                out[py, q, 64 + j if p == py else p * 8 + j % 8] = second[g, s]
            for s in np.nonzero(third[g])[0]:
                p, j = divmod(int(s), 16)
                assert p == py or (j >= 8 if p < py else j < 8)
                out[py, QM + q, 128 + j if p == py else p * 8 + j % 8] = third[g, s]
            for s in np.nonzero(fourth[g])[0]:
                p, j = divmod(int(s), 4)
                out[py, 2 * QM + q, p * 8 + j] = fourth[g, s]
        out[py, 3 * QM, 4:64:8] = 1
    return out


@functools.cache
def column_spread():
    out = np.zeros((128, EC), np.float32)
    for lane in range(EC):
        cell = lane if lane < TC + HALO else lane - EC
        if cell < -HALO:
            continue
        lower = (cell - 8) // 16
        t = (cell - 8 - 16 * lower + 0.5) / 16
        for level in range(3):
            out[40 * level + lower + 2, lane] += 1 - t
            out[40 * level + lower + 3, lane] += t
        out[120, lane] = 1
    return out.astype(ml_dtypes.bfloat16)


@functools.cache
def row_pool(groups, stride, real, first):
    out = np.zeros((128, groups * stride), np.float32)
    for b in range(groups):
        for k in range(real):
            s = b * real + k - first
            if 0 <= s < TR // 16:
                at = b * stride + k
                out[s, at] = 2.0**-8
                out[64 + s // 4, at] = 2.0**-12
                out[80 + s // 16, at] = 2.0**-16
                out[84, at] = 1.0 / (TR * NY * TC * NX)
    return out.astype(ml_dtypes.bfloat16)


def fine_taps():
    return gauss_taps().astype(ml_dtypes.bfloat16)


@functools.cache
def fine_columns():
    out = np.zeros((512, 256), ml_dtypes.bfloat16)
    taps, lane = fine_taps(), np.arange(256)
    for k in range(-HW, HW + 1):
        out[lane + 128 + k, lane] = taps[k + HW]
    return out


VMEM = pl.BlockSpec(memory_space=pltpu.VMEM)
SMEM = pl.BlockSpec(memory_space=pltpu.SMEM)
HBM = pl.BlockSpec(memory_space=pl.ANY)
DMA = pltpu.SemaphoreType.DMA


def params(mib=24):
    return pltpu.CompilerParams(vmem_limit_bytes=mib * 2**20)


def near(x):
    return pltpu.with_memory_space_constraint(x, pltpu.VMEM)


def far(x):
    return pltpu.with_memory_space_constraint(x, pltpu.HBM)


def dot(a, b, **kw):
    return jnp.dot(a, b, preferred_element_type=F32, **kw)


def pieces(x):
    first = x.astype(BF16)
    rest = x - first.astype(F32)
    second = rest.astype(BF16)
    return first, second, (rest - second.astype(F32)).astype(BF16)


def fill_rows(rows):
    shape = (BLK, BLK + 32)
    shift = lax.broadcasted_iota(jnp.int32, shape, 1) - lax.broadcasted_iota(jnp.int32, shape, 0)
    for which in range(3):
        band = jnp.zeros(shape, F32)
        for k in range(-HW, HW + 1):
            band = jnp.where(shift == 16 * which + k, float(fine_taps()[k + HW]), band)
        rows[which] = band.astype(BF16)


def fill_pool(cpool):
    col = lax.broadcasted_iota(jnp.int32, cpool.shape, 0)
    lane = lax.broadcasted_iota(jnp.int32, cpool.shape, 1)
    group = jnp.where(lane < 32, col >> 4, jnp.where(lane < 40, 32 + (col >> 6), 40 + (col >> 8)))
    cpool[...] = jnp.where((group == lane) & (col < TC), 1.0, 0.0).astype(BF16)


def pooled_out(sums, row_pool_ref, px, send_ref, own_ref, corners=None):
    a, b, c = pieces(sums)
    rows = row_pool_ref[...]
    pooled = (dot(rows, a) + dot(rows, b) + dot(rows, c)).T
    own_ref[...] = pooled[:32]
    lane = lax.broadcasted_iota(jnp.int32, (8, 128), 1)
    coarse = jnp.where(lane < 80, pooled[32:40], pooled[40:48])
    left = jnp.where(lane < 64, pooled[0:8], coarse)
    right = jnp.where(lane < 64, pooled[24:32], coarse)
    for p in range(NX):
        send_ref[p, :8] = jnp.where(p < px, left, right)
        if corners is not None:
            send_ref[p, 8:] = jnp.where(p < px, *corners)


def corner(strip):
    lane = lax.broadcasted_iota(jnp.int32, (8, 128), 1)
    both = jnp.where(lane < 64, strip[:8, :128].astype(F32), strip[:8, TR - 128 :].astype(F32))
    more = jnp.where(lane < 64, strip[8:, :128].astype(F32), strip[8:, TR - 128 :].astype(F32))
    inner = jnp.where(lane < 64, pltpu.roll(more, 16, 1), pltpu.roll(more, 112, 1))
    return jnp.where((lane < 16) | (lane >= 112), both, inner)


def start_kernel(table, exps, weights, classes, gain, *refs):
    fars, refs = refs[:6], refs[6:]
    dose, top, bottom, lo, hi, send, own, mgot, mown, matrix, spread_near, rpool_later = refs[:12]
    cbuf, gbuf, cpool, rpool, sums, csem, gsem, tsem = refs[12:]
    steps = TR // SB
    px, py = lax.axis_index("gx"), lax.axis_index("gy")
    loads = []
    for i in range(steps):
        rows = pl.ds(i * SB, SB)
        loads.append(
            (
                pltpu.make_async_copy(classes.at[rows], cbuf.at[rows], csem.at[i]),
                pltpu.make_async_copy(gain.at[rows], gbuf.at[rows], gsem.at[i]),
            )
        )
        for copy in loads[-1]:
            copy.start()
    nears = (rpool, mgot, mown, matrix, spread_near, rpool_later)
    index = (None, px, px, py, None, None)
    tables = []
    for i in range(6):
        source = fars[i] if index[i] is None else fars[i].at[index[i]]
        tables.append(pltpu.make_async_copy(source, nears[i], tsem.at[i]))
        tables[-1].start()
    fill_pool(cpool)
    for i in range(steps):
        for copy in loads[i]:
            copy.wait()
        rows = slice(i * SB, (i + 1) * SB)
        for k in range(TC // SB):
            e = exps[k, i]
            scale = jnp.where(e > 0, 2.0, jnp.where(e < 0, 0.5, 1.0)).astype(F32)
            at = slice(k * SB, (k + 1) * SB)
            c = cbuf[rows, at]
            level = jnp.zeros((SB, SB), F32)
            for j in range(1, CLASSES):
                level = jnp.where(c == j, table[j] * scale, level)
            value = (level * gbuf[rows, at].astype(F32)).astype(BF16)
            dose[rows, at] = value
            if k == 0:
                lo[:, rows] = value.astype(F32).T[:HALO].astype(BF16)
            if k == TC // SB - 1:
                hi[:, rows] = value.astype(F32).T[SB - HALO :].astype(BF16)
        across = dot(dose[rows], cpool[...])
        sums[8 * i : 8 * i + 8] = jnp.sum(across.reshape(8, 16, 128), axis=1)
    top[...] = dose[:HALO]
    bottom[...] = dose[TR - HALO :]
    for copy in tables:
        copy.wait()
    for level in range(3):
        at = slice(QM * level, QM * (level + 1) if level < 2 else matrix.shape[0])
        matrix[at] = matrix[at] * weights[level]
    pooled_out(sums[...], rpool, px, send, own, (corner(lo), corner(hi)))


def start(table, exps, weights, classes, gain):
    steps = TR // SB
    mgot, mown = column_matrices()
    rows, cols, rpool = row_matrices(), column_spread(), row_pool(NB, 16, BLK // 16, 1)
    return pl.pallas_call(
        start_kernel,
        in_specs=[SMEM, SMEM, SMEM] + [HBM] * 8,
        out_specs=[VMEM] * 12,
        out_shape=[
            pltpu.VMEM((TR, TC), BF16),
            pltpu.VMEM((HALO, TC), BF16),
            pltpu.VMEM((HALO, TC), BF16),
            pltpu.VMEM((HALO, TR), BF16),
            pltpu.VMEM((HALO, TR), BF16),
            pltpu.HBM((NX, 16, 128), F32),
            pltpu.VMEM((32, 128), F32),
            pltpu.VMEM(mgot.shape[1:], F32),
            pltpu.VMEM(mown.shape[1:], F32),
            pltpu.VMEM(rows.shape[1:], F32),
            pltpu.VMEM(cols.shape, BF16),
            pltpu.VMEM(rpool.shape, BF16),
        ],
        scratch_shapes=[
            pltpu.VMEM((TR, TC), jnp.int32),
            pltpu.VMEM((TR, TC), BF16),
            pltpu.VMEM((TC, 128), BF16),
            pltpu.VMEM((128, TR // 16), BF16),
            pltpu.VMEM((TR // 16, 128), F32),
            DMA((steps,)),
            DMA((steps,)),
            DMA((6,)),
        ],
        compiler_params=params(),
        name="start",
    )(
        far(table), far(exps.T), far(weights), far(classes), far(gain),
        *[far(jnp.asarray(t)) for t in (row_pool(8, 8, 8, 0), mgot, mown, rows, cols, rpool)],
    )


def side(strip_lo, strip_hi):
    rows = strip_lo.shape[1]
    empty = jnp.zeros((rows, 128 - 2 * HALO), F32)
    return jnp.concatenate([strip_hi.astype(F32).T, empty, strip_lo.astype(F32).T], axis=1)


def across_kernel(first, got, own, mgot, mown, send, part):
    received = got[:, :8].reshape(NX * 8, 128)
    z = dot(mgot[...], received, precision=EXACT)
    mine = dot(mown[...], own[...], precision=EXACT)
    z = jnp.concatenate([z[:40] + mine, z[40:]], axis=0).T
    part[...] = z[:80]
    lane = lax.broadcasted_iota(jnp.int32, (8, 128), 1)
    coarse = z[80:88]
    up = jnp.where(lane < 40, z[0:8], jnp.where(lane < 80, z[64:72], coarse))
    down = jnp.where(lane < 40, z[56:64], jnp.where(lane < 80, z[72:80], coarse))
    px, py = lax.axis_index("gx"), lax.axis_index("gy")
    for p in range(NY):
        send[p, :8] = jnp.where(p < py, up, down)
    if first:
        lo = jnp.where(px > 0, got[jnp.maximum(px - 1, 0), 8:], 0.0)
        hi = jnp.where(px < NX - 1, got[jnp.minimum(px + 1, NX - 1), 8:], 0.0)
        ends = []
        for shift in (112, 16):
            ends.append(side(*[jnp.concatenate([x, pltpu.roll(x, shift, 1)], axis=0) for x in (lo, hi)]))
        for p in range(NY):
            send[p, 8:] = jnp.where(p < py, ends[0][:HALO], ends[1][128 - HALO :])


def across(first, got, own, mgot, mown):
    count = 8 + HALO if first else 8
    return pl.pallas_call(
        functools.partial(across_kernel, first),
        in_specs=[VMEM] * 4,
        out_specs=[VMEM] * 2,
        out_shape=[pltpu.VMEM((NY, count, 128), F32), pltpu.VMEM((80, 128), F32)],
        compiler_params=params(),
        name="across",
    )(near(got), near(own), near(mgot), near(mown))


def column_pass(block, cols, half, at):
    tile = [block[:, 128 * n : 128 * (n + 1)] for n in range(EC // 128)]
    join = lambda *which: jnp.concatenate([tile[n] for n in which], axis=1)
    half[at, :256] = dot(join(4, 0, 1, 2), cols[...]).astype(BF16)
    half[at, 256:512] = dot(join(1, 2, 3, 4), cols[...]).astype(BF16)
    if half.shape[1] > TC:
        half[at, 512:] = dot(join(3, 4, 0), cols[:384, :128]).astype(BF16)


def first_half_kernel(tile, lo, hi, cols_far, half_far, sides, half, cols, sems, csem):
    load = pltpu.make_async_copy(cols_far, cols, csem)
    load.start()
    stores = []
    for n in range(TR // SB):
        rows, begin = slice(n * SB, (n + 1) * SB), HALO + n * SB
        beside = side(lo[:, rows], hi[:, rows]).astype(BF16)
        sides[rows] = beside
        if n == 0:
            load.wait()
        column_pass(jnp.concatenate([tile[rows], beside], axis=1), cols, half, slice(begin, begin + SB))
        at = pl.ds(begin, SB)
        stores.append(pltpu.make_async_copy(half.at[at], half_far.at[at], sems.at[n]))
        stores[-1].start()
    for copy in stores:
        copy.wait()


def half_cost():
    return pl.CostEstimate(flops=4 * ER * EC * EC, bytes_accessed=6 * ER * EC, transcendentals=0)


def first_half(tile, lo, hi):
    return pl.pallas_call(
        first_half_kernel,
        in_specs=[VMEM] * 3 + [HBM],
        out_specs=[HBM, VMEM],
        out_shape=[pltpu.HBM((ER, EC), BF16), pltpu.VMEM((TR, EC - TC), BF16)],
        scratch_shapes=[pltpu.VMEM((ER, EC), BF16), pltpu.VMEM((512, 256), BF16), DMA((TR // SB,)), DMA],
        compiler_params=params(),
        cost_estimate=half_cost(),
        name="first_half",
    )(near(tile), near(lo), near(hi), far(jnp.asarray(fine_columns())))


def half_kernel(dose, cols_far, half, cols, csem):
    load = pltpu.make_async_copy(cols_far, cols, csem)
    load.start()
    load.wait()
    for b in range(NB):
        column_pass(dose[b * BLK : (b + 1) * BLK], cols, half, slice(b * BLK, (b + 1) * BLK))


def half_of(dose, lanes):
    return pl.pallas_call(
        half_kernel,
        in_specs=[VMEM, HBM],
        out_specs=VMEM,
        out_shape=pltpu.VMEM((ER, lanes), BF16),
        scratch_shapes=[pltpu.VMEM((512, 256), BF16), DMA],
        compiler_params=params(),
        cost_estimate=half_cost(),
        name="half",
    )(near(dose), far(jnp.asarray(fine_columns())))


def spread(received, part, matrix, cols):
    y = dot(matrix[...], jnp.concatenate([received, part[...]], axis=0), precision=EXACT)
    lane = lax.broadcasted_iota(jnp.int32, (QM, 128), 1)
    fourth = jnp.where(lane < 120, y[2 * QM : 3 * QM], jnp.where(lane == 120, y[3 * QM : 3 * QM + 1], 0.0))
    a, b, c = pieces(jnp.where(lane < 40, y[:QM], jnp.where(lane < 80, y[QM : 2 * QM], fourth)))
    return dot(a, cols) + dot(b, cols) + dot(c, cols)


def short_range(b, rows, half):
    begin = min(max(b * BLK - 16, 0), ER - BLK - 32)
    return dot(rows[(b * BLK - begin) // 16], half[begin : begin + BLK + 32])


def update(b, old_rows, short, grid, out, skip):
    count, lanes = out.shape
    t = (lax.broadcasted_iota(jnp.int32, (8, lanes), 0).astype(F32) + 0.5) / 16.0
    for n in range(BLK // 16):
        row = b * BLK + 16 * n
        if not skip <= row < skip + count:
            continue
        at = row // 16
        a, m, c = (grid[at + k : at + k + 1] for k in range(3))
        back = jnp.concatenate([a + (t + 0.5) * (m - a), m + t * (c - m)], axis=0)
        full = 1.0 + (short[16 * n : 16 * n + 16] + back)
        out[row - skip : row - skip + 16] = (old_rows(row).astype(F32) * 2.0 / full).astype(out.dtype)


def step_kernel(first, got, part, matrix, cols, rpool, dose, half, *refs):
    if first:
        sides, above, below, fcols_far, out, send, own, rows, cpool, grid, sums, hbuf, fcols, lsem, fsem = refs
        loads = [pltpu.make_async_copy(fcols_far, fcols, fsem)]
        at = pl.ds(HALO, TR)
        loads.append(pltpu.make_async_copy(half.at[at], hbuf.at[at], lsem))
        for copy in loads:
            copy.start()
    else:
        out, send, own, rows, cpool, grid, sums = refs
        hbuf = half
    edge = {}
    fill_rows(rows)
    fill_pool(cpool)
    received = got[:, :8].reshape(NY * 8, 128)
    grid[...] = spread(received, part, matrix, cols[...])
    if first:
        py = lax.axis_index("gy")
        loads[0].wait()
        for row, strip, p, real in (
            (0, above, jnp.maximum(py - 1, 0), py > 0),
            (ER - HALO, below, jnp.minimum(py + 1, NY - 1), py < NY - 1),
        ):
            beside = jnp.where(real, got[p, 8:], 0.0).astype(BF16)
            values = jnp.concatenate([strip[...], beside], axis=1)
            edge[row] = values
            column_pass(values, fcols, hbuf, slice(row, row + HALO))
        for copy in loads[1:]:
            copy.wait()

    def old_rows(row):
        if row in edge:
            return edge[row]
        if first:
            at = slice(row - HALO, row - HALO + 16)
            return jnp.concatenate([dose[at], sides[at]], axis=1)
        return dose[row : row + 16]

    for b in range(NB):
        update(b, old_rows, short_range(b, rows, hbuf), grid, out, 0)
        pooled = dot(out[b * BLK : (b + 1) * BLK], cpool[...])
        pooled = jnp.sum(pooled.reshape(BLK // 16, 16, 128), axis=1)
        sums[16 * b : 16 * b + 16] = jnp.concatenate([pooled, jnp.zeros((16 - BLK // 16, 128), F32)], axis=0)
    pooled_out(sums[...], rpool, lax.axis_index("gx"), send, own)


def step(got, part, dose, half, ops, strips=None):
    first = strips is not None
    scratch = [
        pltpu.VMEM((3, BLK, BLK + 32), BF16),
        pltpu.VMEM((EC, 128), BF16),
        pltpu.VMEM((QM, EC), F32),
        pltpu.VMEM((NB * 16, 128), F32),
    ]
    if first:
        scratch += [pltpu.VMEM((ER, EC), BF16), pltpu.VMEM((512, 256), BF16), DMA, DMA]
    return pl.pallas_call(
        functools.partial(step_kernel, first),
        in_specs=[VMEM] * 6 + ([HBM] + [VMEM] * 3 + [HBM] if first else [VMEM]),
        out_specs=[VMEM] * 3,
        out_shape=[
            pltpu.VMEM((ER, EC), BF16),
            pltpu.HBM((NX, 8, 128), F32),
            pltpu.VMEM((32, 128), F32),
        ],
        scratch_shapes=scratch,
        input_output_aliases={} if first else {5: 0},
        compiler_params=params(),
        name="first_step" if first else "step",
    )(
        near(got), near(part), *[near(x) for x in ops], near(dose), far(half) if first else near(half),
        *([*[near(x) for x in strips], far(jnp.asarray(fine_columns()))] if first else []),
    )


def finish_kernel(got, part, matrix, cols, dose, half, out, rows, made, grid, ssem):
    fill_rows(rows)
    grid[...] = spread(got[...].reshape(NY * 8, 128), part, matrix, cols[:, :TC])
    stores = []
    for b in range(NB):
        update(b, lambda row: dose[row : row + 16, :TC], short_range(b, rows, half), grid, made, HALO)
        begin, end = max(b * BLK - HALO, 0), min((b + 1) * BLK - HALO, TR)
        at = pl.ds(begin, end - begin)
        stores.append(pltpu.make_async_copy(made.at[at], out.at[at], ssem.at[b]))
        stores[-1].start()
    for copy in stores:
        copy.wait()


def finish(got, part, dose, half, ops):
    return pl.pallas_call(
        finish_kernel,
        in_specs=[VMEM] * 6,
        out_specs=HBM,
        out_shape=pltpu.HBM((TR, TC), F32),
        scratch_shapes=[
            pltpu.VMEM((3, BLK, BLK + 32), BF16),
            pltpu.VMEM((TR, TC), F32),
            pltpu.VMEM((QM, TC), F32),
            DMA((NB,)),
        ],
        compiler_params=params(),
        name="finish",
    )(near(got), near(part), near(ops[0]), near(ops[1]), near(dose), near(half))


def shifted(x, axis, by):
    n = lax.axis_size(axis)
    return lax.ppermute(x, axis, [(i, i + by) for i in range(n) if 0 <= i + by < n])


def exchanged(x, axis):
    return lax.all_to_all(x, axis, 0, 0, tiled=True)


def local(classes, exponents, gain_field, level_table, level_weights):
    tile, top, bottom, lo, hi, send, own, mgot, mown, *ops = start(
        level_table, exponents, level_weights, classes, gain_field
    )
    left, right = shifted(hi, "gx", 1), shifted(lo, "gx", -1)
    above, below = shifted(bottom, "gy", 1), shifted(top, "gy", -1)
    got = exchanged(send, "gx")
    send, part = across(True, got, own, mgot, mown)
    got = exchanged(send, "gy")
    half, sides = first_half(tile, left, right)
    dose, send, own = step(got, part, tile, half, ops, (sides, above, below))
    for sweep in range(2, ITERS + 1):
        got = exchanged(send, "gx")
        half = half_of(dose, EC if sweep < ITERS else TC)
        send, part = across(False, got, own, mgot, mown)
        got = exchanged(send, "gy")
        if sweep < ITERS:
            dose, send, own = step(got, part, dose, half, ops)
    return finish(got, part, dose, half, ops)


def solution(mesh):
    in_specs = (P("gy", "gx"), P("gy", "gx"), P("gy", "gx"), P(), P())
    return jax.shard_map(local, mesh=mesh, in_specs=in_specs, out_specs=P("gy", "gx"), check_vma=False)
```

```python
import functools

import jax
import jax.numpy as jnp
import ml_dtypes
import numpy as np
from jax import lax
from jax.experimental import pallas as pl
from jax.experimental.pallas import tpu as pltpu
from jax.sharding import PartitionSpec as P

HW = 4
CLASSES = 8
SB = 128
ITERS = 4
NX, NY = 32, 8
TR, TC = 1024, 512
HALO = HW * ITERS
ER = TR + 2 * HALO
EC = TC + 128
BLK = 176
NB = ER // BLK
QC, QR = 36, 68
F32, BF16 = jnp.float32, jnp.bfloat16
EXACT = lax.Precision.HIGHEST


def gauss_taps():
    offsets = np.arange(-HW, HW + 1).astype(np.float32)
    weights = np.exp(-(offsets * offsets) / np.float32(HW * HW)).astype(np.float32)
    return weights / weights.sum(dtype=np.float32)


def blur_operator(n):
    taps = gauss_taps().astype(np.float64)
    out = np.zeros((n, n))
    for k in range(-HW, HW + 1):
        out += taps[k + HW] * np.eye(n, k=k)
    return out


def up_operator(n, factor):
    target = np.arange(n * factor)
    lower = (target - factor // 2) // factor
    t = (target - factor // 2 - factor * lower + 0.5) / factor
    out = np.zeros((n * factor, n))
    np.add.at(out, (target, np.clip(lower, 0, n - 1)), 1 - t)
    np.add.at(out, (target, np.clip(lower + 1, 0, n - 1)), t)
    return out


def level_operators(n_second):
    third, fourth = n_second // 4, n_second // 16
    return (
        blur_operator(n_second),
        up_operator(third, 4) @ blur_operator(third),
        up_operator(third, 4) @ up_operator(fourth, 4) @ blur_operator(fourth),
    )


@functools.cache
def column_matrices():
    second, third, fourth = level_operators(NX * 32)
    got = np.zeros((NX, 128, 256), np.float32)
    own = np.zeros((NX, 40, 32), np.float32)
    for px in range(NX):
        for q in range(QC):
            g = min(max(32 * px + q - 2, 0), NX * 32 - 1)
            for s in np.nonzero(second[g])[0]:
                p, j = divmod(int(s), 32)
                if p == px:
                    own[px, q, j] = second[g, s]
                else:
                    assert j >= 24 if p < px else j < 8
                    got[px, q, p * 8 + j % 8] = second[g, s]
            got[px, 40 + q] = third[g]
            for j in range(2):
                got[px, 80 + q, j::8] = fourth[g, j::2]
        got[px, 120, 0::8] = 1
        got[px, 120, 1::8] = 1
    return got, own


QM = QR + 4


def row_matrices():
    second, third, fourth = level_operators(NY * 64)
    out = np.zeros((NY, 3 * QM + 8, 144), np.float32)
    for py in range(NY):
        for q in range(QR):
            g = min(max(64 * py + q - 2, 0), NY * 64 - 1)
            for s in np.nonzero(second[g])[0]:
                p, j = divmod(int(s), 64)
                assert p == py or (j >= 56 if p < py else j < 8)
                out[py, q, 64 + j if p == py else p * 8 + j % 8] = second[g, s]
            for s in np.nonzero(third[g])[0]:
                p, j = divmod(int(s), 16)
                assert p == py or (j >= 8 if p < py else j < 8)
                out[py, QM + q, 128 + j if p == py else p * 8 + j % 8] = third[g, s]
            for s in np.nonzero(fourth[g])[0]:
                p, j = divmod(int(s), 4)
                out[py, 2 * QM + q, p * 8 + j] = fourth[g, s]
        out[py, 3 * QM, 4:64:8] = 1
    return out


@functools.cache
def column_spread():
    out = np.zeros((128, EC), np.float32)
    for lane in range(EC):
        cell = lane if lane < TC + HALO else lane - EC
        if cell < -HALO:
            continue
        lower = (cell - 8) // 16
        t = (cell - 8 - 16 * lower + 0.5) / 16
        for level in range(3):
            out[40 * level + lower + 2, lane] += 1 - t
            out[40 * level + lower + 3, lane] += t
        out[120, lane] = 1
    return out.astype(ml_dtypes.bfloat16)


@functools.cache
def row_pool(groups, stride, real, first):
    out = np.zeros((128, groups * stride), np.float32)
    for b in range(groups):
        for k in range(real):
            s = b * real + k - first
            if 0 <= s < TR // 16:
                at = b * stride + k
                out[s, at] = 2.0**-8
                out[64 + s // 4, at] = 2.0**-12
                out[80 + s // 16, at] = 2.0**-16
                out[84, at] = 1.0 / (TR * NY * TC * NX)
    return out.astype(ml_dtypes.bfloat16)


def fine_taps():
    return gauss_taps().astype(ml_dtypes.bfloat16)


@functools.cache
def fine_columns():
    out = np.zeros((512, 256), ml_dtypes.bfloat16)
    taps, lane = fine_taps(), np.arange(256)
    for k in range(-HW, HW + 1):
        out[lane + 128 + k, lane] = taps[k + HW]
    return out


VMEM = pl.BlockSpec(memory_space=pltpu.VMEM)
SMEM = pl.BlockSpec(memory_space=pltpu.SMEM)
HBM = pl.BlockSpec(memory_space=pl.ANY)
DMA = pltpu.SemaphoreType.DMA


def params(mib=24):
    return pltpu.CompilerParams(vmem_limit_bytes=mib * 2**20)


def near(x):
    return pltpu.with_memory_space_constraint(x, pltpu.VMEM)


def far(x):
    return pltpu.with_memory_space_constraint(x, pltpu.HBM)


def dot(a, b, **kw):
    return jnp.dot(a, b, preferred_element_type=F32, **kw)


def pieces(x):
    first = x.astype(BF16)
    rest = x - first.astype(F32)
    second = rest.astype(BF16)
    return first, second, (rest - second.astype(F32)).astype(BF16)


def fill_rows(rows):
    shape = (BLK, BLK + 32)
    shift = lax.broadcasted_iota(jnp.int32, shape, 1) - lax.broadcasted_iota(jnp.int32, shape, 0)
    for which in range(3):
        band = jnp.zeros(shape, F32)
        for k in range(-HW, HW + 1):
            band = jnp.where(shift == 16 * which + k, float(fine_taps()[k + HW]), band)
        rows[which] = band.astype(BF16)


def fill_pool(cpool):
    col = lax.broadcasted_iota(jnp.int32, cpool.shape, 0)
    lane = lax.broadcasted_iota(jnp.int32, cpool.shape, 1)
    group = jnp.where(lane < 32, col >> 4, jnp.where(lane < 40, 32 + (col >> 6), 40 + (col >> 8)))
    cpool[...] = jnp.where((group == lane) & (col < TC), 1.0, 0.0).astype(BF16)


def pooled_out(sums, row_pool_ref, px, send_ref, own_ref):
    a, b, c = pieces(sums)
    rows = row_pool_ref[...]
    pooled = (dot(rows, a) + dot(rows, b) + dot(rows, c)).T
    own_ref[...] = pooled[:32]
    lane = lax.broadcasted_iota(jnp.int32, (8, 128), 1)
    coarse = jnp.where(lane < 80, pooled[32:40], pooled[40:48])
    left = jnp.where(lane < 64, pooled[0:8], coarse)
    right = jnp.where(lane < 64, pooled[24:32], coarse)
    for p in range(NX):
        send_ref[p] = jnp.where(p < px, left, right)


def start_kernel(table, exps, weights, classes, gain, *refs):
    fars, refs = refs[:6], refs[6:]
    dose, top, bottom, lo, hi, send, own, mgot, mown, matrix, spread_near, rpool_later = refs[:12]
    cbuf, gbuf, cpool, rpool, sums, csem, gsem, tsem = refs[12:]
    steps = TR // SB
    px, py = lax.axis_index("gx"), lax.axis_index("gy")
    loads = []
    for i in range(steps):
        rows = pl.ds(i * SB, SB)
        loads.append(
            (
                pltpu.make_async_copy(classes.at[rows], cbuf.at[rows], csem.at[i]),
                pltpu.make_async_copy(gain.at[rows], gbuf.at[rows], gsem.at[i]),
            )
        )
        for copy in loads[-1]:
            copy.start()
    nears = (rpool, mgot, mown, matrix, spread_near, rpool_later)
    index = (None, px, px, py, None, None)
    tables = []
    for i in range(6):
        source = fars[i] if index[i] is None else fars[i].at[index[i]]
        tables.append(pltpu.make_async_copy(source, nears[i], tsem.at[i]))
        tables[-1].start()
    fill_pool(cpool)
    for i in range(steps):
        for copy in loads[i]:
            copy.wait()
        rows = slice(i * SB, (i + 1) * SB)
        for k in range(TC // SB):
            e = exps[k, i]
            scale = jnp.where(e > 0, 2.0, jnp.where(e < 0, 0.5, 1.0)).astype(F32)
            at = slice(k * SB, (k + 1) * SB)
            c = cbuf[rows, at]
            level = jnp.zeros((SB, SB), F32)
            for j in range(1, CLASSES):
                level = jnp.where(c == j, table[j] * scale, level)
            value = (level * gbuf[rows, at].astype(F32)).astype(BF16)
            dose[rows, at] = value
            if k == 0:
                lo[:, rows] = value.astype(F32).T[:HALO].astype(BF16)
            if k == TC // SB - 1:
                hi[:, rows] = value.astype(F32).T[SB - HALO :].astype(BF16)
        across = dot(dose[rows], cpool[...])
        sums[8 * i : 8 * i + 8] = jnp.sum(across.reshape(8, 16, 128), axis=1)
    top[...] = dose[:HALO]
    bottom[...] = dose[TR - HALO :]
    for copy in tables:
        copy.wait()
    for level in range(3):
        at = slice(QM * level, QM * (level + 1) if level < 2 else matrix.shape[0])
        matrix[at] = matrix[at] * weights[level]
    pooled_out(sums[...], rpool, px, send, own)


def start(table, exps, weights, classes, gain):
    steps = TR // SB
    mgot, mown = column_matrices()
    rows, cols, rpool = row_matrices(), column_spread(), row_pool(NB, 16, BLK // 16, 1)
    return pl.pallas_call(
        start_kernel,
        in_specs=[SMEM, SMEM, SMEM] + [HBM] * 8,
        out_specs=[VMEM] * 12,
        out_shape=[
            pltpu.VMEM((TR, TC), BF16),
            pltpu.VMEM((HALO, TC), BF16),
            pltpu.VMEM((HALO, TC), BF16),
            pltpu.VMEM((HALO, TR), BF16),
            pltpu.VMEM((HALO, TR), BF16),
            pltpu.HBM((NX, 8, 128), F32),
            pltpu.VMEM((32, 128), F32),
            pltpu.VMEM(mgot.shape[1:], F32),
            pltpu.VMEM(mown.shape[1:], F32),
            pltpu.VMEM(rows.shape[1:], F32),
            pltpu.VMEM(cols.shape, BF16),
            pltpu.VMEM(rpool.shape, BF16),
        ],
        scratch_shapes=[
            pltpu.VMEM((TR, TC), jnp.int32),
            pltpu.VMEM((TR, TC), BF16),
            pltpu.VMEM((TC, 128), BF16),
            pltpu.VMEM((128, TR // 16), BF16),
            pltpu.VMEM((TR // 16, 128), F32),
            DMA((steps,)),
            DMA((steps,)),
            DMA((6,)),
        ],
        compiler_params=params(),
        name="start",
    )(
        far(table), far(exps.T), far(weights), far(classes), far(gain),
        *[far(jnp.asarray(t)) for t in (row_pool(8, 8, 8, 0), mgot, mown, rows, cols, rpool)],
    )


def side(strip_lo, strip_hi):
    rows = strip_lo.shape[1]
    empty = jnp.zeros((rows, 128 - 2 * HALO), F32)
    return jnp.concatenate([strip_hi.astype(F32).T, empty, strip_lo.astype(F32).T], axis=1)


def across_kernel(first, *refs):
    if first:
        top, bottom, lo, hi, got, own, mgot, mown, send, part = refs
    else:
        _, got, own, mgot, mown, send, part = refs
    received = got[...].reshape(NX * 8, 128)
    z = dot(mgot[...], received, precision=EXACT)
    mine = dot(mown[...], own[...], precision=EXACT)
    z = jnp.concatenate([z[:40] + mine, z[40:]], axis=0).T
    part[...] = z[:80]
    lane = lax.broadcasted_iota(jnp.int32, (8, 128), 1)
    coarse = z[80:88]
    up = jnp.where(lane < 40, z[0:8], jnp.where(lane < 80, z[64:72], coarse))
    down = jnp.where(lane < 40, z[56:64], jnp.where(lane < 80, z[72:80], coarse))
    py = lax.axis_index("gy")
    if not first:
        for p in range(NY):
            send[p] = jnp.where(p < py, up, down)
        return
    above = side(lo[:, :128], hi[:, :128])[:HALO]
    below = side(lo[:, TR - 128 :], hi[:, TR - 128 :])[128 - HALO :]
    blocks = []
    for strip, coarse_part, beside in ((top, up, above), (bottom, down, below)):
        parts = [x.astype(F32) for x in pieces(coarse_part)] + [jnp.zeros((8, 128), F32)]
        parts += [strip[:, 128 * n : 128 * n + 128].astype(F32) for n in range(TC // 128)] + [beside]
        blocks.append(jnp.concatenate(parts, axis=0).astype(BF16))
    for p in range(NY):

        @pl.when(p < py)
        def _():
            send[p] = blocks[0]

        @pl.when(p >= py)
        def _():
            send[p] = blocks[1]


def across(first, extra, got, own, mgot, mown):
    rows, kind = (32 + HALO * (EC // 128), BF16) if first else (8, F32)
    return pl.pallas_call(
        functools.partial(across_kernel, first),
        in_specs=([VMEM] * 4 if first else [HBM]) + [VMEM] * 4,
        out_specs=[VMEM] * 2,
        out_shape=[pltpu.VMEM((NY, rows, 128), kind), pltpu.VMEM((80, 128), F32)],
        compiler_params=params(),
        name="across",
    )(*[near(x) for x in extra], near(got), near(own), near(mgot), near(mown))


def column_pass(block, cols, half, at):
    tile = [block[:, 128 * n : 128 * (n + 1)] for n in range(EC // 128)]
    join = lambda *which: jnp.concatenate([tile[n] for n in which], axis=1)
    half[at, :256] = dot(join(4, 0, 1, 2), cols[...]).astype(BF16)
    half[at, 256:512] = dot(join(1, 2, 3, 4), cols[...]).astype(BF16)
    if half.shape[1] > TC:
        half[at, 512:] = dot(join(3, 4, 0), cols[:384, :128]).astype(BF16)


def first_half_kernel(tile, lo, hi, cols_far, half_far, sides, half, cols, sems, csem):
    load = pltpu.make_async_copy(cols_far, cols, csem)
    load.start()
    stores = []
    for n in range(TR // SB):
        rows, begin = slice(n * SB, (n + 1) * SB), HALO + n * SB
        beside = side(lo[:, rows], hi[:, rows]).astype(BF16)
        sides[rows] = beside
        if n == 0:
            load.wait()
        column_pass(jnp.concatenate([tile[rows], beside], axis=1), cols, half, slice(begin, begin + SB))
        at = pl.ds(begin, SB)
        stores.append(pltpu.make_async_copy(half.at[at], half_far.at[at], sems.at[n]))
        stores[-1].start()
    for copy in stores:
        copy.wait()


def half_cost():
    return pl.CostEstimate(flops=4 * ER * EC * EC, bytes_accessed=6 * ER * EC, transcendentals=0)


def first_half(tile, lo, hi):
    return pl.pallas_call(
        first_half_kernel,
        in_specs=[VMEM] * 3 + [HBM],
        out_specs=[HBM, VMEM],
        out_shape=[pltpu.HBM((ER, EC), BF16), pltpu.HBM((TR, EC - TC), BF16)],
        scratch_shapes=[pltpu.VMEM((ER, EC), BF16), pltpu.VMEM((512, 256), BF16), DMA((TR // SB,)), DMA],
        compiler_params=params(),
        cost_estimate=half_cost(),
        name="first_half",
    )(near(tile), near(lo), near(hi), far(jnp.asarray(fine_columns())))


def half_kernel(dose, cols_far, half, cols, csem):
    load = pltpu.make_async_copy(cols_far, cols, csem)
    load.start()
    load.wait()
    for b in range(NB):
        column_pass(dose[b * BLK : (b + 1) * BLK], cols, half, slice(b * BLK, (b + 1) * BLK))


def half_of(dose, lanes):
    return pl.pallas_call(
        half_kernel,
        in_specs=[VMEM, HBM],
        out_specs=VMEM,
        out_shape=pltpu.VMEM((ER, lanes), BF16),
        scratch_shapes=[pltpu.VMEM((512, 256), BF16), DMA],
        compiler_params=params(),
        cost_estimate=half_cost(),
        name="half",
    )(near(dose), far(jnp.asarray(fine_columns())))


def spread(received, part, matrix, cols):
    y = dot(matrix[...], jnp.concatenate([received, part[...]], axis=0), precision=EXACT)
    lane = lax.broadcasted_iota(jnp.int32, (QM, 128), 1)
    fourth = jnp.where(lane < 120, y[2 * QM : 3 * QM], jnp.where(lane == 120, y[3 * QM : 3 * QM + 1], 0.0))
    a, b, c = pieces(jnp.where(lane < 40, y[:QM], jnp.where(lane < 80, y[QM : 2 * QM], fourth)))
    return dot(a, cols) + dot(b, cols) + dot(c, cols)


def short_range(b, rows, half):
    begin = min(max(b * BLK - 16, 0), ER - BLK - 32)
    return dot(rows[(b * BLK - begin) // 16], half[begin : begin + BLK + 32])


def update(b, old_rows, short, grid, out, skip):
    count, lanes = out.shape
    t = (lax.broadcasted_iota(jnp.int32, (8, lanes), 0).astype(F32) + 0.5) / 16.0
    for n in range(BLK // 16):
        row = b * BLK + 16 * n
        if not skip <= row < skip + count:
            continue
        at = row // 16
        a, m, c = (grid[at + k : at + k + 1] for k in range(3))
        back = jnp.concatenate([a + (t + 0.5) * (m - a), m + t * (c - m)], axis=0)
        full = 1.0 + (short[16 * n : 16 * n + 16] + back)
        out[row - skip : row - skip + 16] = (old_rows(row).astype(F32) * 2.0 / full).astype(out.dtype)


def step_kernel(first, got, part, matrix, cols, rpool, dose, half, *refs):
    if first:
        sides_far, fcols_far, out, send, own, rows, cpool, grid, sums, hbuf, sides, fcols, lsem, ssem, fsem = refs
        loads = [pltpu.make_async_copy(fcols_far, fcols, fsem)]
        at = pl.ds(HALO, TR)
        loads.append(pltpu.make_async_copy(half.at[at], hbuf.at[at], lsem))
        loads.append(pltpu.make_async_copy(sides_far, sides, ssem))
        for copy in loads:
            copy.start()
    else:
        out, send, own, rows, cpool, grid, sums = refs
        hbuf = half
    edge = {}
    fill_rows(rows)
    fill_pool(cpool)
    if first:
        parts = got[:, :32].astype(F32)
        received = parts[:, :8] + (parts[:, 8:16] + parts[:, 16:24])
    else:
        received = got[...]
    received = received.reshape(NY * 8, 128)
    grid[...] = spread(received, part, matrix, cols[...])
    if first:
        py = lax.axis_index("gy")
        loads[0].wait()
        for row, p, real in (
            (0, jnp.maximum(py - 1, 0), py > 0),
            (ER - HALO, jnp.minimum(py + 1, NY - 1), py < NY - 1),
        ):
            tiles = [got[p, 32 + HALO * n : 32 + HALO * (n + 1)].astype(F32) for n in range(EC // 128)]
            values = jnp.where(real, jnp.concatenate(tiles, axis=1), 0.0).astype(BF16)
            edge[row] = values
            column_pass(values, fcols, hbuf, slice(row, row + HALO))
        for copy in loads[1:]:
            copy.wait()

    def old_rows(row):
        if row in edge:
            return edge[row]
        if first:
            at = slice(row - HALO, row - HALO + 16)
            return jnp.concatenate([dose[at], sides[at]], axis=1)
        return dose[row : row + 16]

    for b in range(NB):
        update(b, old_rows, short_range(b, rows, hbuf), grid, out, 0)
        pooled = dot(out[b * BLK : (b + 1) * BLK], cpool[...])
        pooled = jnp.sum(pooled.reshape(BLK // 16, 16, 128), axis=1)
        sums[16 * b : 16 * b + 16] = jnp.concatenate([pooled, jnp.zeros((16 - BLK // 16, 128), F32)], axis=0)
    pooled_out(sums[...], rpool, lax.axis_index("gx"), send, own)


def step(got, part, dose, half, ops, sides=None):
    first = sides is not None
    scratch = [
        pltpu.VMEM((3, BLK, BLK + 32), BF16),
        pltpu.VMEM((EC, 128), BF16),
        pltpu.VMEM((QM, EC), F32),
        pltpu.VMEM((NB * 16, 128), F32),
    ]
    if first:
        scratch += [pltpu.VMEM((ER, EC), BF16), pltpu.VMEM((TR, EC - TC), BF16), pltpu.VMEM((512, 256), BF16)]
        scratch += [DMA] * 3
    return pl.pallas_call(
        functools.partial(step_kernel, first),
        in_specs=[VMEM] * 6 + ([HBM] * 3 if first else [VMEM]),
        out_specs=[VMEM] * 3,
        out_shape=[
            pltpu.VMEM((ER, EC), BF16),
            pltpu.HBM((NX, 8, 128), F32),
            pltpu.VMEM((32, 128), F32),
        ],
        scratch_shapes=scratch,
        input_output_aliases={} if first else {5: 0},
        compiler_params=params(),
        name="first_step" if first else "step",
    )(
        near(got), near(part), *[near(x) for x in ops], near(dose), far(half) if first else near(half),
        *([far(sides), far(jnp.asarray(fine_columns()))] if first else []),
    )


def finish_kernel(got, part, matrix, cols, dose, half, out, rows, made, grid, ssem):
    fill_rows(rows)
    grid[...] = spread(got[...].reshape(NY * 8, 128), part, matrix, cols[:, :TC])
    stores = []
    for b in range(NB):
        update(b, lambda row: dose[row : row + 16, :TC], short_range(b, rows, half), grid, made, HALO)
        begin, end = max(b * BLK - HALO, 0), min((b + 1) * BLK - HALO, TR)
        at = pl.ds(begin, end - begin)
        stores.append(pltpu.make_async_copy(made.at[at], out.at[at], ssem.at[b]))
        stores[-1].start()
    for copy in stores:
        copy.wait()


def finish(got, part, dose, half, ops):
    return pl.pallas_call(
        finish_kernel,
        in_specs=[VMEM] * 6,
        out_specs=HBM,
        out_shape=pltpu.HBM((TR, TC), F32),
        scratch_shapes=[
            pltpu.VMEM((3, BLK, BLK + 32), BF16),
            pltpu.VMEM((TR, TC), F32),
            pltpu.VMEM((QM, TC), F32),
            DMA((NB,)),
        ],
        compiler_params=params(),
        name="finish",
    )(near(got), near(part), near(ops[0]), near(ops[1]), near(dose), near(half))


def shifted(x, axis, by):
    n = lax.axis_size(axis)
    return lax.ppermute(x, axis, [(i, i + by) for i in range(n) if 0 <= i + by < n])


def exchanged(x, axis):
    return lax.all_to_all(x, axis, 0, 0, tiled=True)


def local(classes, exponents, gain_field, level_table, level_weights):
    tile, top, bottom, lo, hi, send, own, mgot, mown, *ops = start(
        level_table, exponents, level_weights, classes, gain_field
    )
    left, right = shifted(hi, "gx", 1), shifted(lo, "gx", -1)
    got = exchanged(send, "gx")
    send, part = across(True, (top, bottom, left, right), got, own, mgot, mown)
    got = exchanged(send, "gy")
    half, sides = first_half(tile, left, right)
    dose, send, own = step(got, part, tile, half, ops, sides)
    for sweep in range(2, ITERS + 1):
        got = exchanged(send, "gx")
        half = half_of(dose, EC if sweep < ITERS else TC)
        send, part = across(False, (half,), got, own, mgot, mown)
        got = exchanged(send, "gy")
        if sweep < ITERS:
            dose, send, own = step(got, part, dose, half, ops)
    return finish(got, part, dose, half, ops)


def solution(mesh):
    in_specs = (P("gy", "gx"), P("gy", "gx"), P("gy", "gx"), P(), P())
    return jax.shard_map(local, mesh=mesh, in_specs=in_specs, out_specs=P("gy", "gx"), check_vma=False)
```

```python
import functools

import jax
import jax.numpy as jnp
import ml_dtypes
import numpy as np
from jax import lax
from jax.experimental import pallas as pl
from jax.experimental.pallas import tpu as pltpu
from jax.sharding import PartitionSpec as P

HW = 4
CLASSES = 8
SB = 128
ITERS = 4
NX, NY = 32, 8
TR, TC = 1024, 512
HALO = HW * ITERS
ER = TR + 2 * HALO
EC = TC + 128
PAD = 16
BLK = 176
NB = ER // BLK
QC, QR = 36, 68
F32, BF16 = jnp.float32, jnp.bfloat16
EXACT = lax.Precision.HIGHEST


def gauss_taps():
    offsets = np.arange(-HW, HW + 1).astype(np.float32)
    weights = np.exp(-(offsets * offsets) / np.float32(HW * HW)).astype(np.float32)
    return weights / weights.sum(dtype=np.float32)


def blur_operator(n):
    taps = gauss_taps().astype(np.float64)
    out = np.zeros((n, n))
    for k in range(-HW, HW + 1):
        out += taps[k + HW] * np.eye(n, k=k)
    return out


def up_operator(n, factor):
    target = np.arange(n * factor)
    lower = (target - factor // 2) // factor
    t = (target - factor // 2 - factor * lower + 0.5) / factor
    out = np.zeros((n * factor, n))
    np.add.at(out, (target, np.clip(lower, 0, n - 1)), 1 - t)
    np.add.at(out, (target, np.clip(lower + 1, 0, n - 1)), t)
    return out


def level_operators(n_second):
    third, fourth = n_second // 4, n_second // 16
    return (
        blur_operator(n_second),
        up_operator(third, 4) @ blur_operator(third),
        up_operator(third, 4) @ up_operator(fourth, 4) @ blur_operator(fourth),
    )


@functools.cache
def column_matrices():
    second, third, fourth = level_operators(NX * 32)
    got = np.zeros((NX, 128, 256), np.float32)
    own = np.zeros((NX, 40, 32), np.float32)
    for px in range(NX):
        for q in range(QC):
            g = min(max(32 * px + q - 2, 0), NX * 32 - 1)
            for s in np.nonzero(second[g])[0]:
                p, j = divmod(int(s), 32)
                if p == px:
                    own[px, q, j] = second[g, s]
                else:
                    assert j >= 24 if p < px else j < 8
                    got[px, q, p * 8 + j % 8] = second[g, s]
            got[px, 40 + q] = third[g]
            for j in range(2):
                got[px, 80 + q, j::8] = fourth[g, j::2]
        got[px, 120, 0::8] = 1
        got[px, 120, 1::8] = 1
    return got, own


QM = QR + 4


def row_matrices():
    second, third, fourth = level_operators(NY * 64)
    out = np.zeros((NY, 3 * QM + 8, 144), np.float32)
    for py in range(NY):
        for q in range(QR):
            g = min(max(64 * py + q - 2, 0), NY * 64 - 1)
            for s in np.nonzero(second[g])[0]:
                p, j = divmod(int(s), 64)
                assert p == py or (j >= 56 if p < py else j < 8)
                out[py, q, 64 + j if p == py else p * 8 + j % 8] = second[g, s]
            for s in np.nonzero(third[g])[0]:
                p, j = divmod(int(s), 16)
                assert p == py or (j >= 8 if p < py else j < 8)
                out[py, QM + q, 128 + j if p == py else p * 8 + j % 8] = third[g, s]
            for s in np.nonzero(fourth[g])[0]:
                p, j = divmod(int(s), 4)
                out[py, 2 * QM + q, p * 8 + j] = fourth[g, s]
        out[py, 3 * QM, 4:64:8] = 1
    return out


@functools.cache
def column_spread():
    out = np.zeros((128, EC), np.float32)
    for lane in range(EC):
        cell = lane if lane < TC + HALO else lane - EC
        if cell < -HALO:
            continue
        lower = (cell - 8) // 16
        t = (cell - 8 - 16 * lower + 0.5) / 16
        for level in range(3):
            out[40 * level + lower + 2, lane] += 1 - t
            out[40 * level + lower + 3, lane] += t
        out[120, lane] = 1
    return out.astype(ml_dtypes.bfloat16)


@functools.cache
def row_pool(groups, stride, real, first):
    out = np.zeros((128, groups * stride), np.float32)
    for b in range(groups):
        for k in range(real):
            s = b * real + k - first
            if 0 <= s < TR // 16:
                at = b * stride + k
                out[s, at] = 2.0**-8
                out[64 + s // 4, at] = 2.0**-12
                out[80 + s // 16, at] = 2.0**-16
                out[84, at] = 1.0 / (TR * NY * TC * NX)
    return out.astype(ml_dtypes.bfloat16)


def fine_taps():
    return gauss_taps().astype(ml_dtypes.bfloat16)


@functools.cache
def fine_columns():
    out = np.zeros((512, 256), ml_dtypes.bfloat16)
    taps, lane = fine_taps(), np.arange(256)
    for k in range(-HW, HW + 1):
        out[lane + 128 + k, lane] = taps[k + HW]
    return out


VMEM = pl.BlockSpec(memory_space=pltpu.VMEM)
SMEM = pl.BlockSpec(memory_space=pltpu.SMEM)
HBM = pl.BlockSpec(memory_space=pl.ANY)
DMA = pltpu.SemaphoreType.DMA


def params(mib=24):
    return pltpu.CompilerParams(vmem_limit_bytes=mib * 2**20)


def near(x):
    return pltpu.with_memory_space_constraint(x, pltpu.VMEM)


def far(x):
    return pltpu.with_memory_space_constraint(x, pltpu.HBM)


def dot(a, b, **kw):
    return jnp.dot(a, b, preferred_element_type=F32, **kw)


def pieces(x):
    first = x.astype(BF16)
    rest = x - first.astype(F32)
    second = rest.astype(BF16)
    return first, second, (rest - second.astype(F32)).astype(BF16)


def fill_rows(rows):
    shift = lax.broadcasted_iota(jnp.int32, rows.shape, 1) - lax.broadcasted_iota(jnp.int32, rows.shape, 0)
    band = jnp.zeros(rows.shape, F32)
    for k in range(-HW, HW + 1):
        band = jnp.where(shift == PAD + k, float(fine_taps()[k + HW]), band)
    rows[...] = band.astype(BF16)


def fill_pads(half):
    for at in (slice(0, PAD), slice(PAD + ER, PAD + ER + PAD)):
        half[at] = jnp.zeros((PAD, half.shape[1]), BF16)


def fill_pool(cpool):
    col = lax.broadcasted_iota(jnp.int32, cpool.shape, 0)
    lane = lax.broadcasted_iota(jnp.int32, cpool.shape, 1)
    group = jnp.where(lane < 32, col >> 4, jnp.where(lane < 40, 32 + (col >> 6), 40 + (col >> 8)))
    cpool[...] = jnp.where((group == lane) & (col < TC), 1.0, 0.0).astype(BF16)


def pooled_out(sums, row_pool_ref, px, send_ref, own_ref):
    a, b, c = pieces(sums)
    rows = row_pool_ref[...]
    pooled = (dot(rows, a) + dot(rows, b) + dot(rows, c)).T
    own_ref[...] = pooled[:32]
    lane = lax.broadcasted_iota(jnp.int32, (8, 128), 1)
    coarse = jnp.where(lane < 80, pooled[32:40], pooled[40:48])
    left = jnp.where(lane < 64, pooled[0:8], coarse)
    right = jnp.where(lane < 64, pooled[24:32], coarse)
    for p in range(NX):
        send_ref[p] = jnp.where(p < px, left, right)


def start_kernel(table_far, exps_far, weights_far, classes, gain, *refs):
    fars, refs = refs[:6], refs[6:]
    dose, top, bottom, lo, hi, send, own, mgot, mown, matrix, spread_near, rpool_later = refs[:12]
    cbuf, gbuf, cpool, rpool, sums, table, exps, weights, csem, gsem, tsem, ssem = refs[12:]
    steps = TR // SB
    px, py = lax.axis_index("gx"), lax.axis_index("gy")
    scalars = [
        pltpu.make_async_copy(source, to, ssem.at[i])
        for i, (source, to) in enumerate(((table_far, table), (exps_far, exps), (weights_far, weights)))
    ]
    for copy in scalars:
        copy.start()
    loads = []
    for i in range(steps):
        rows = pl.ds(i * SB, SB)
        loads.append(
            (
                pltpu.make_async_copy(classes.at[rows], cbuf.at[rows], csem.at[i]),
                pltpu.make_async_copy(gain.at[rows], gbuf.at[rows], gsem.at[i]),
            )
        )
        for copy in loads[-1]:
            copy.start()
    nears = (rpool, mgot, mown, matrix, spread_near, rpool_later)
    index = (None, px, px, py, None, None)
    tables = []
    for i in range(6):
        source = fars[i] if index[i] is None else fars[i].at[index[i]]
        tables.append(pltpu.make_async_copy(source, nears[i], tsem.at[i]))
        tables[-1].start()
    fill_pool(cpool)
    for copy in scalars:
        copy.wait()
    for i in range(steps):
        for copy in loads[i]:
            copy.wait()
        rows = slice(i * SB, (i + 1) * SB)
        for k in range(TC // SB):
            e = exps[k, i]
            scale = jnp.where(e > 0, 2.0, jnp.where(e < 0, 0.5, 1.0)).astype(F32)
            at = slice(k * SB, (k + 1) * SB)
            c = cbuf[rows, at]
            level = jnp.zeros((SB, SB), F32)
            for j in range(1, CLASSES):
                level = jnp.where(c == j, table[j] * scale, level)
            value = (level * gbuf[rows, at].astype(F32)).astype(BF16)
            dose[rows, at] = value
            if k == 0:
                lo[:, rows] = value.astype(F32).T[:HALO].astype(BF16)
            if k == TC // SB - 1:
                hi[:, rows] = value.astype(F32).T[SB - HALO :].astype(BF16)
        across = dot(dose[rows], cpool[...])
        sums[8 * i : 8 * i + 8] = jnp.sum(across.reshape(8, 16, 128), axis=1)
    top[...] = dose[:HALO]
    bottom[...] = dose[TR - HALO :]
    for copy in tables:
        copy.wait()
    for level in range(3):
        at = slice(QM * level, QM * (level + 1) if level < 2 else matrix.shape[0])
        matrix[at] = matrix[at] * weights[level]
    pooled_out(sums[...], rpool, px, send, own)


def start(table, exps, weights, classes, gain):
    steps = TR // SB
    mgot, mown = column_matrices()
    rows, cols, rpool = row_matrices(), column_spread(), row_pool(NB, 16, BLK // 16, 1)
    return pl.pallas_call(
        start_kernel,
        in_specs=[HBM] * 11,
        out_specs=[VMEM] * 12,
        out_shape=[
            pltpu.VMEM((TR, TC), BF16),
            pltpu.VMEM((HALO, TC), BF16),
            pltpu.VMEM((HALO, TC), BF16),
            pltpu.VMEM((HALO, TR), BF16),
            pltpu.VMEM((HALO, TR), BF16),
            pltpu.HBM((NX, 8, 128), F32),
            pltpu.VMEM((32, 128), F32),
            pltpu.VMEM(mgot.shape[1:], F32),
            pltpu.VMEM(mown.shape[1:], F32),
            pltpu.VMEM(rows.shape[1:], F32),
            pltpu.VMEM(cols.shape, BF16),
            pltpu.VMEM(rpool.shape, BF16),
        ],
        scratch_shapes=[
            pltpu.VMEM((TR, TC), jnp.int32),
            pltpu.VMEM((TR, TC), BF16),
            pltpu.VMEM((TC, 128), BF16),
            pltpu.VMEM((128, TR // 16), BF16),
            pltpu.VMEM((TR // 16, 128), F32),
            pltpu.SMEM((CLASSES,), F32),
            pltpu.SMEM((TC // SB, TR // SB), jnp.int32),
            pltpu.SMEM((3,), F32),
            DMA((steps,)),
            DMA((steps,)),
            DMA((6,)),
            DMA((3,)),
        ],
        compiler_params=params(),
        name="start",
    )(
        far(table), far(exps.T), far(weights), far(classes), far(gain),
        *[far(jnp.asarray(t)) for t in (row_pool(8, 8, 8, 0), mgot, mown, rows, cols, rpool)],
    )


def side(strip_lo, strip_hi):
    rows = strip_lo.shape[1]
    empty = jnp.zeros((rows, 128 - 2 * HALO), F32)
    return jnp.concatenate([strip_hi.astype(F32).T, empty, strip_lo.astype(F32).T], axis=1)


def across_kernel(first, *refs):
    if first:
        top, bottom, lo, hi, got, own, mgot, mown, send, part = refs
    else:
        _, got, own, mgot, mown, send, part = refs
    received = got[...].reshape(NX * 8, 128)
    z = dot(mgot[...], received, precision=EXACT)
    mine = dot(mown[...], own[...], precision=EXACT)
    z = jnp.concatenate([z[:40] + mine, z[40:]], axis=0).T
    part[...] = z[:80]
    lane = lax.broadcasted_iota(jnp.int32, (8, 128), 1)
    coarse = z[80:88]
    up = jnp.where(lane < 40, z[0:8], jnp.where(lane < 80, z[64:72], coarse))
    down = jnp.where(lane < 40, z[56:64], jnp.where(lane < 80, z[72:80], coarse))
    py = lax.axis_index("gy")
    if not first:
        for p in range(NY):
            send[p] = jnp.where(p < py, up, down)
        return
    above = side(lo[:, :128], hi[:, :128])[:HALO]
    below = side(lo[:, TR - 128 :], hi[:, TR - 128 :])[128 - HALO :]
    blocks = []
    for strip, coarse_part, beside in ((top, up, above), (bottom, down, below)):
        parts = [x.astype(F32) for x in pieces(coarse_part)] + [jnp.zeros((8, 128), F32)]
        parts += [strip[:, 128 * n : 128 * n + 128].astype(F32) for n in range(TC // 128)] + [beside]
        blocks.append(jnp.concatenate(parts, axis=0).astype(BF16))
    for p in range(NY):

        @pl.when(p < py)
        def _():
            send[p] = blocks[0]

        @pl.when(p >= py)
        def _():
            send[p] = blocks[1]


def across(first, extra, got, own, mgot, mown):
    rows, kind = (32 + HALO * (EC // 128), BF16) if first else (8, F32)
    return pl.pallas_call(
        functools.partial(across_kernel, first),
        in_specs=([VMEM] * 4 if first else [HBM]) + [VMEM] * 4,
        out_specs=[VMEM] * 2,
        out_shape=[pltpu.VMEM((NY, rows, 128), kind), pltpu.VMEM((80, 128), F32)],
        compiler_params=params(),
        name="across",
    )(*[near(x) for x in extra], near(got), near(own), near(mgot), near(mown))


def column_pass(block, cols, half, at):
    tile = [block[:, 128 * n : 128 * (n + 1)] for n in range(EC // 128)]
    join = lambda *which: jnp.concatenate([tile[n] for n in which], axis=1)
    half[at, :256] = dot(join(4, 0, 1, 2), cols[...]).astype(BF16)
    half[at, 256:512] = dot(join(1, 2, 3, 4), cols[...]).astype(BF16)
    if half.shape[1] > TC:
        half[at, 512:] = dot(join(3, 4, 0), cols[:384, :128]).astype(BF16)


def first_half_kernel(tile, lo, hi, cols_far, half_far, sides, half, cols, sems, csem):
    load = pltpu.make_async_copy(cols_far, cols, csem)
    load.start()
    stores = []
    for n in range(TR // SB):
        rows, begin = slice(n * SB, (n + 1) * SB), HALO + n * SB
        beside = side(lo[:, rows], hi[:, rows]).astype(BF16)
        sides[rows] = beside
        if n == 0:
            load.wait()
        column_pass(jnp.concatenate([tile[rows], beside], axis=1), cols, half, slice(PAD + begin, PAD + begin + SB))
        at = pl.ds(PAD + begin, SB)
        stores.append(pltpu.make_async_copy(half.at[at], half_far.at[at], sems.at[n]))
        stores[-1].start()
    for copy in stores:
        copy.wait()


def half_cost():
    return pl.CostEstimate(flops=4 * ER * EC * EC, bytes_accessed=6 * ER * EC, transcendentals=0)


def first_half(tile, lo, hi):
    return pl.pallas_call(
        first_half_kernel,
        in_specs=[VMEM] * 3 + [HBM],
        out_specs=[HBM, VMEM],
        out_shape=[pltpu.HBM((ER + 2 * PAD, EC), BF16), pltpu.HBM((TR, EC - TC), BF16)],
        scratch_shapes=[pltpu.VMEM((ER + 2 * PAD, EC), BF16), pltpu.VMEM((512, 256), BF16), DMA((TR // SB,)), DMA],
        compiler_params=params(),
        cost_estimate=half_cost(),
        name="first_half",
    )(near(tile), near(lo), near(hi), far(jnp.asarray(fine_columns())))


def half_kernel(dose, cols_far, half, cols, csem):
    load = pltpu.make_async_copy(cols_far, cols, csem)
    load.start()
    fill_pads(half)
    load.wait()
    for b in range(NB):
        column_pass(dose[b * BLK : (b + 1) * BLK], cols, half, slice(PAD + b * BLK, PAD + (b + 1) * BLK))


def half_of(dose, lanes):
    return pl.pallas_call(
        half_kernel,
        in_specs=[VMEM, HBM],
        out_specs=VMEM,
        out_shape=pltpu.VMEM((ER + 2 * PAD, lanes), BF16),
        scratch_shapes=[pltpu.VMEM((512, 256), BF16), DMA],
        compiler_params=params(),
        cost_estimate=half_cost(),
        name="half",
    )(near(dose), far(jnp.asarray(fine_columns())))


def spread(received, part, matrix, cols):
    y = dot(matrix[...], jnp.concatenate([received, part[...]], axis=0), precision=EXACT)
    lane = lax.broadcasted_iota(jnp.int32, (QM, 128), 1)
    fourth = jnp.where(lane < 120, y[2 * QM : 3 * QM], jnp.where(lane == 120, y[3 * QM : 3 * QM + 1], 0.0))
    a, b, c = pieces(jnp.where(lane < 40, y[:QM], jnp.where(lane < 80, y[QM : 2 * QM], fourth)))
    return dot(a, cols) + dot(b, cols) + dot(c, cols)


def short_range(b, rows, half):
    return dot(rows[...], half[b * BLK : (b + 1) * BLK + 2 * PAD])


def update(b, old_rows, short, grid, out, skip):
    count, lanes = out.shape
    t = (lax.broadcasted_iota(jnp.int32, (8, lanes), 0).astype(F32) + 0.5) / 16.0
    for n in range(BLK // 16):
        row = b * BLK + 16 * n
        if not skip <= row < skip + count:
            continue
        at = row // 16
        a, m, c = (grid[at + k : at + k + 1] for k in range(3))
        back = jnp.concatenate([a + (t + 0.5) * (m - a), m + t * (c - m)], axis=0)
        full = 1.0 + (short[16 * n : 16 * n + 16] + back)
        out[row - skip : row - skip + 16] = (old_rows(row).astype(F32) * 2.0 / full).astype(out.dtype)


def step_kernel(first, got, part, matrix, cols, rpool, dose, half, *refs):
    if first:
        sides_far, fcols_far, out, send, own, rows, cpool, grid, sums, hbuf, sides, fcols, lsem, ssem, fsem = refs
        loads = [pltpu.make_async_copy(fcols_far, fcols, fsem)]
        at = pl.ds(PAD + HALO, TR)
        loads.append(pltpu.make_async_copy(half.at[at], hbuf.at[at], lsem))
        loads.append(pltpu.make_async_copy(sides_far, sides, ssem))
        for copy in loads:
            copy.start()
    else:
        out, send, own, rows, cpool, grid, sums = refs
        hbuf = half
    edge = {}
    fill_rows(rows)
    fill_pool(cpool)
    if first:
        parts = got[:, :32].astype(F32)
        received = parts[:, :8] + (parts[:, 8:16] + parts[:, 16:24])
    else:
        received = got[...]
    received = received.reshape(NY * 8, 128)
    grid[...] = spread(received, part, matrix, cols[...])
    if first:
        py = lax.axis_index("gy")
        fill_pads(hbuf)
        loads[0].wait()
        for row, p, real in (
            (0, jnp.maximum(py - 1, 0), py > 0),
            (ER - HALO, jnp.minimum(py + 1, NY - 1), py < NY - 1),
        ):
            tiles = [got[p, 32 + HALO * n : 32 + HALO * (n + 1)].astype(F32) for n in range(EC // 128)]
            values = jnp.where(real, jnp.concatenate(tiles, axis=1), 0.0).astype(BF16)
            edge[row] = values
            column_pass(values, fcols, hbuf, slice(PAD + row, PAD + row + HALO))
        for copy in loads[1:]:
            copy.wait()

    def old_rows(row):
        if row in edge:
            return edge[row]
        if first:
            at = slice(row - HALO, row - HALO + 16)
            return jnp.concatenate([dose[at], sides[at]], axis=1)
        return dose[row : row + 16]

    for b in range(NB):
        update(b, old_rows, short_range(b, rows, hbuf), grid, out, 0)
        pooled = dot(out[b * BLK : (b + 1) * BLK, :TC], cpool[...])
        pooled = jnp.sum(pooled.reshape(BLK // 16, 16, 128), axis=1)
        sums[16 * b : 16 * b + 16] = jnp.concatenate([pooled, jnp.zeros((16 - BLK // 16, 128), F32)], axis=0)
    pooled_out(sums[...], rpool, lax.axis_index("gx"), send, own)


def step(got, part, dose, half, ops, sides=None):
    first = sides is not None
    scratch = [
        pltpu.VMEM((BLK, BLK + 2 * PAD), BF16),
        pltpu.VMEM((TC, 128), BF16),
        pltpu.VMEM((QM, EC), F32),
        pltpu.VMEM((NB * 16, 128), F32),
    ]
    if first:
        scratch += [pltpu.VMEM((ER + 2 * PAD, EC), BF16), pltpu.VMEM((TR, EC - TC), BF16), pltpu.VMEM((512, 256), BF16)]
        scratch += [DMA] * 3
    return pl.pallas_call(
        functools.partial(step_kernel, first),
        in_specs=[VMEM] * 6 + ([HBM] * 3 if first else [VMEM]),
        out_specs=[VMEM] * 3,
        out_shape=[
            pltpu.VMEM((ER, EC), BF16),
            pltpu.HBM((NX, 8, 128), F32),
            pltpu.VMEM((32, 128), F32),
        ],
        scratch_shapes=scratch,
        input_output_aliases={} if first else {5: 0},
        compiler_params=params(),
        name="first_step" if first else "step",
    )(
        near(got), near(part), *[near(x) for x in ops], near(dose), far(half) if first else near(half),
        *([far(sides), far(jnp.asarray(fine_columns()))] if first else []),
    )


def finish_kernel(got, part, matrix, cols, dose, half, out, rows, made, grid, ssem):
    fill_rows(rows)
    grid[...] = spread(got[...].reshape(NY * 8, 128), part, matrix, cols[:, :TC])
    stores = []
    for b in range(NB):
        update(b, lambda row: dose[row : row + 16, :TC], short_range(b, rows, half), grid, made, HALO)
        begin, end = max(b * BLK - HALO, 0), min((b + 1) * BLK - HALO, TR)
        at = pl.ds(begin, end - begin)
        stores.append(pltpu.make_async_copy(made.at[at], out.at[at], ssem.at[b]))
        stores[-1].start()
    for copy in stores:
        copy.wait()


def finish(got, part, dose, half, ops):
    return pl.pallas_call(
        finish_kernel,
        in_specs=[VMEM] * 6,
        out_specs=HBM,
        out_shape=pltpu.HBM((TR, TC), F32),
        scratch_shapes=[
            pltpu.VMEM((BLK, BLK + 2 * PAD), BF16),
            pltpu.VMEM((TR, TC), F32),
            pltpu.VMEM((QM, TC), F32),
            DMA((NB,)),
        ],
        compiler_params=params(),
        name="finish",
    )(near(got), near(part), near(ops[0]), near(ops[1]), near(dose), near(half))


def shifted(x, axis, by):
    n = lax.axis_size(axis)
    return lax.ppermute(x, axis, [(i, i + by) for i in range(n) if 0 <= i + by < n])


def exchanged(x, axis):
    return lax.all_to_all(x, axis, 0, 0, tiled=True)


def local(classes, exponents, gain_field, level_table, level_weights):
    tile, top, bottom, lo, hi, send, own, mgot, mown, *ops = start(
        level_table, exponents, level_weights, classes, gain_field
    )
    left, right = shifted(hi, "gx", 1), shifted(lo, "gx", -1)
    got = exchanged(send, "gx")
    send, part = across(True, (top, bottom, left, right), got, own, mgot, mown)
    got = exchanged(send, "gy")
    half, sides = first_half(tile, left, right)
    dose, send, own = step(got, part, tile, half, ops, sides)
    for sweep in range(2, ITERS + 1):
        got = exchanged(send, "gx")
        half = half_of(dose, EC if sweep < ITERS else TC)
        send, part = across(False, (half,), got, own, mgot, mown)
        got = exchanged(send, "gy")
        if sweep < ITERS:
            dose, send, own = step(got, part, dose, half, ops)
    return finish(got, part, dose, half, ops)


def solution(mesh):
    in_specs = (P("gy", "gx"), P("gy", "gx"), P("gy", "gx"), P(), P())
    return jax.shard_map(local, mesh=mesh, in_specs=in_specs, out_specs=P("gy", "gx"), check_vma=False)
```

```python
import functools

import jax
import jax.numpy as jnp
import ml_dtypes
import numpy as np
from jax import lax
from jax.experimental import pallas as pl
from jax.experimental.pallas import tpu as pltpu
from jax.sharding import PartitionSpec as P

HW = 4
CLASSES = 8
SB = 128
ITERS = 4
NX, NY = 32, 8
TR, TC = 1024, 512
HALO = HW * ITERS
ER = TR + 2 * HALO
EC = TC + 128
PAD = 16
BLK = 176
NB = ER // BLK
QC, QR = 36, 68
F32, BF16 = jnp.float32, jnp.bfloat16
EXACT = lax.Precision.HIGHEST


def gauss_taps():
    offsets = np.arange(-HW, HW + 1).astype(np.float32)
    weights = np.exp(-(offsets * offsets) / np.float32(HW * HW)).astype(np.float32)
    return weights / weights.sum(dtype=np.float32)


def blur_operator(n):
    taps = gauss_taps().astype(np.float64)
    out = np.zeros((n, n))
    for k in range(-HW, HW + 1):
        out += taps[k + HW] * np.eye(n, k=k)
    return out


def up_operator(n, factor):
    target = np.arange(n * factor)
    lower = (target - factor // 2) // factor
    t = (target - factor // 2 - factor * lower + 0.5) / factor
    out = np.zeros((n * factor, n))
    np.add.at(out, (target, np.clip(lower, 0, n - 1)), 1 - t)
    np.add.at(out, (target, np.clip(lower + 1, 0, n - 1)), t)
    return out


def level_operators(n_second):
    third, fourth = n_second // 4, n_second // 16
    return (
        blur_operator(n_second),
        up_operator(third, 4) @ blur_operator(third),
        up_operator(third, 4) @ up_operator(fourth, 4) @ blur_operator(fourth),
    )


@functools.cache
def column_matrices():
    second, third, fourth = level_operators(NX * 32)
    got = np.zeros((NX, 128, 256), np.float32)
    own = np.zeros((NX, 40, 32), np.float32)
    for px in range(NX):
        for q in range(QC):
            g = min(max(32 * px + q - 2, 0), NX * 32 - 1)
            for s in np.nonzero(second[g])[0]:
                p, j = divmod(int(s), 32)
                if p == px:
                    own[px, q, j] = second[g, s]
                else:
                    assert j >= 24 if p < px else j < 8
                    got[px, q, p * 8 + j % 8] = second[g, s]
            got[px, 40 + q] = third[g]
            for j in range(2):
                got[px, 80 + q, j::8] = fourth[g, j::2]
        got[px, 120, 0::8] = 1
        got[px, 120, 1::8] = 1
    return got, own


QM = QR + 4


def row_matrices():
    second, third, fourth = level_operators(NY * 64)
    out = np.zeros((NY, 3 * QM + 8, 144), np.float32)
    for py in range(NY):
        for q in range(QR):
            g = min(max(64 * py + q - 2, 0), NY * 64 - 1)
            for s in np.nonzero(second[g])[0]:
                p, j = divmod(int(s), 64)
                assert p == py or (j >= 56 if p < py else j < 8)
                out[py, q, 64 + j if p == py else p * 8 + j % 8] = second[g, s]
            for s in np.nonzero(third[g])[0]:
                p, j = divmod(int(s), 16)
                assert p == py or (j >= 8 if p < py else j < 8)
                out[py, QM + q, 128 + j if p == py else p * 8 + j % 8] = third[g, s]
            for s in np.nonzero(fourth[g])[0]:
                p, j = divmod(int(s), 4)
                out[py, 2 * QM + q, p * 8 + j] = fourth[g, s]
        out[py, 3 * QM, 4:64:8] = 1
    return out


@functools.cache
def column_spread():
    out = np.zeros((128, EC), np.float32)
    for lane in range(EC):
        cell = lane if lane < TC + HALO else lane - EC
        if cell < -HALO:
            continue
        lower = (cell - 8) // 16
        t = (cell - 8 - 16 * lower + 0.5) / 16
        for level in range(3):
            out[40 * level + lower + 2, lane] += 1 - t
            out[40 * level + lower + 3, lane] += t
        out[120, lane] = 1
    return out.astype(ml_dtypes.bfloat16)


@functools.cache
def row_pool(groups, stride, real, first):
    out = np.zeros((128, groups * stride), np.float32)
    for b in range(groups):
        for k in range(real):
            s = b * real + k - first
            if 0 <= s < TR // 16:
                at = b * stride + k
                out[s, at] = 2.0**-8
                out[64 + s // 4, at] = 2.0**-12
                out[80 + s // 16, at] = 2.0**-16
                out[84, at] = 1.0 / (TR * NY * TC * NX)
    return out.astype(ml_dtypes.bfloat16)


def fine_taps():
    return gauss_taps().astype(ml_dtypes.bfloat16)


@functools.cache
def fine_columns():
    out = np.zeros((512, 256), ml_dtypes.bfloat16)
    taps, lane = fine_taps(), np.arange(256)
    for k in range(-HW, HW + 1):
        out[lane + 128 + k, lane] = taps[k + HW]
    return out


VMEM = pl.BlockSpec(memory_space=pltpu.VMEM)
SMEM = pl.BlockSpec(memory_space=pltpu.SMEM)
HBM = pl.BlockSpec(memory_space=pl.ANY)
DMA = pltpu.SemaphoreType.DMA


def params(mib=24):
    return pltpu.CompilerParams(vmem_limit_bytes=mib * 2**20)


def near(x):
    return pltpu.with_memory_space_constraint(x, pltpu.VMEM)


def far(x):
    return pltpu.with_memory_space_constraint(x, pltpu.HBM)


def dot(a, b, **kw):
    return jnp.dot(a, b, preferred_element_type=F32, **kw)


def pieces(x):
    first = x.astype(BF16)
    rest = x - first.astype(F32)
    second = rest.astype(BF16)
    return first, second, (rest - second.astype(F32)).astype(BF16)


def fill_rows(rows):
    shift = lax.broadcasted_iota(jnp.int32, rows.shape, 1) - lax.broadcasted_iota(jnp.int32, rows.shape, 0)
    band = jnp.zeros(rows.shape, F32)
    for k in range(-HW, HW + 1):
        band = jnp.where(shift == PAD + k, float(fine_taps()[k + HW]), band)
    rows[...] = band.astype(BF16)


def fill_pads(half):
    for at in (slice(0, PAD), slice(PAD + ER, PAD + ER + PAD)):
        half[at] = jnp.zeros((PAD, half.shape[1]), BF16)


def fill_pool(cpool):
    col = lax.broadcasted_iota(jnp.int32, cpool.shape, 0)
    lane = lax.broadcasted_iota(jnp.int32, cpool.shape, 1)
    group = jnp.where(lane < 32, col >> 4, jnp.where(lane < 40, 32 + (col >> 6), 40 + (col >> 8)))
    cpool[...] = jnp.where((group == lane) & (col < TC), 1.0, 0.0).astype(BF16)


def pooled_out(sums, row_pool_ref, px, send_ref, own_ref):
    a, b, c = pieces(sums)
    rows = row_pool_ref[...]
    pooled = (dot(rows, a) + dot(rows, b) + dot(rows, c)).T
    own_ref[...] = pooled[:32]
    lane = lax.broadcasted_iota(jnp.int32, (8, 128), 1)
    coarse = jnp.where(lane < 80, pooled[32:40], pooled[40:48])
    left = jnp.where(lane < 64, pooled[0:8], coarse)
    right = jnp.where(lane < 64, pooled[24:32], coarse)
    for p in range(NX):
        send_ref[p] = jnp.where(p < px, left, right)


def start_kernel(table_far, exps_far, weights_far, classes, gain, *refs):
    fars, refs = refs[:6], refs[6:]
    dose, top, bottom, lo, hi, send, own, mgot, mown, matrix, spread_near, rpool_later = refs[:12]
    cbuf, gbuf, cpool, rpool, sums, table, exps, weights, csem, gsem, tsem, ssem = refs[12:]
    steps = TR // SB
    px, py = lax.axis_index("gx"), lax.axis_index("gy")
    scalars = [
        pltpu.make_async_copy(source, to, ssem.at[i])
        for i, (source, to) in enumerate(((table_far, table), (exps_far, exps), (weights_far, weights)))
    ]
    for copy in scalars:
        copy.start()
    loads = []
    for i in range(steps):
        rows = pl.ds(i * SB, SB)
        loads.append(
            (
                pltpu.make_async_copy(classes.at[rows], cbuf.at[rows], csem.at[i]),
                pltpu.make_async_copy(gain.at[rows], gbuf.at[rows], gsem.at[i]),
            )
        )
        for copy in loads[-1]:
            copy.start()
    nears = (rpool, mgot, mown, matrix, spread_near, rpool_later)
    index = (None, px, px, py, None, None)
    tables = []
    for i in range(6):
        source = fars[i] if index[i] is None else fars[i].at[index[i]]
        tables.append(pltpu.make_async_copy(source, nears[i], tsem.at[i]))
        tables[-1].start()
    fill_pool(cpool)
    for copy in scalars:
        copy.wait()

    def pool(i):
        across = dot(dose[i * SB : (i + 1) * SB], cpool[...])
        sums[8 * i : 8 * i + 8] = jnp.sum(across.reshape(8, 16, 128), axis=1)

    for i in range(steps):
        for copy in loads[i]:
            copy.wait()
        rows = slice(i * SB, (i + 1) * SB)
        for k in range(TC // SB):
            e = exps[k, i]
            scale = jnp.where(e > 0, 2.0, jnp.where(e < 0, 0.5, 1.0)).astype(F32)
            at = slice(k * SB, (k + 1) * SB)
            c = cbuf[rows, at]
            level = jnp.zeros((SB, SB), F32)
            for j in range(1, CLASSES):
                level = jnp.where(c == j, table[j] * scale, level)
            value = (level * gbuf[rows, at].astype(F32)).astype(BF16)
            dose[rows, at] = value
            if k == 0:
                lo[:, rows] = value.astype(F32).T[:HALO].astype(BF16)
            if k == TC // SB - 1:
                hi[:, rows] = value.astype(F32).T[SB - HALO :].astype(BF16)
        if i > 0:
            pool(i - 1)
    pool(steps - 1)
    top[...] = dose[:HALO]
    bottom[...] = dose[TR - HALO :]
    for copy in tables:
        copy.wait()
    for level in range(3):
        at = slice(QM * level, QM * (level + 1) if level < 2 else matrix.shape[0])
        matrix[at] = matrix[at] * weights[level]
    pooled_out(sums[...], rpool, px, send, own)


def start(table, exps, weights, classes, gain):
    steps = TR // SB
    mgot, mown = column_matrices()
    rows, cols, rpool = row_matrices(), column_spread(), row_pool(NB, 16, BLK // 16, 1)
    return pl.pallas_call(
        start_kernel,
        in_specs=[HBM] * 11,
        out_specs=[VMEM] * 12,
        out_shape=[
            pltpu.VMEM((TR, TC), BF16),
            pltpu.VMEM((HALO, TC), BF16),
            pltpu.VMEM((HALO, TC), BF16),
            pltpu.VMEM((HALO, TR), BF16),
            pltpu.VMEM((HALO, TR), BF16),
            pltpu.HBM((NX, 8, 128), F32),
            pltpu.VMEM((32, 128), F32),
            pltpu.VMEM(mgot.shape[1:], F32),
            pltpu.VMEM(mown.shape[1:], F32),
            pltpu.VMEM(rows.shape[1:], F32),
            pltpu.VMEM(cols.shape, BF16),
            pltpu.VMEM(rpool.shape, BF16),
        ],
        scratch_shapes=[
            pltpu.VMEM((TR, TC), jnp.int32),
            pltpu.VMEM((TR, TC), BF16),
            pltpu.VMEM((TC, 128), BF16),
            pltpu.VMEM((128, TR // 16), BF16),
            pltpu.VMEM((TR // 16, 128), F32),
            pltpu.SMEM((CLASSES,), F32),
            pltpu.SMEM((TC // SB, TR // SB), jnp.int32),
            pltpu.SMEM((3,), F32),
            DMA((steps,)),
            DMA((steps,)),
            DMA((6,)),
            DMA((3,)),
        ],
        compiler_params=params(),
        name="start",
    )(
        far(table), far(exps.T), far(weights), far(classes), far(gain),
        *[far(jnp.asarray(t)) for t in (row_pool(8, 8, 8, 0), mgot, mown, rows, cols, rpool)],
    )


def side(strip_lo, strip_hi):
    rows = strip_lo.shape[1]
    empty = jnp.zeros((rows, 128 - 2 * HALO), F32)
    return jnp.concatenate([strip_hi.astype(F32).T, empty, strip_lo.astype(F32).T], axis=1)


def across_kernel(first, *refs):
    if first:
        top, bottom, lo, hi, got, own, mgot, mown, send, part = refs
    else:
        _, got, own, mgot, mown, send, part = refs
    received = got[...].reshape(NX * 8, 128)
    z = dot(mgot[...], received, precision=EXACT)
    mine = dot(mown[...], own[...], precision=EXACT)
    z = jnp.concatenate([z[:40] + mine, z[40:]], axis=0).T
    part[...] = z[:80]
    lane = lax.broadcasted_iota(jnp.int32, (8, 128), 1)
    coarse = z[80:88]
    up = jnp.where(lane < 40, z[0:8], jnp.where(lane < 80, z[64:72], coarse))
    down = jnp.where(lane < 40, z[56:64], jnp.where(lane < 80, z[72:80], coarse))
    py = lax.axis_index("gy")
    if not first:
        for p in range(NY):
            send[p] = jnp.where(p < py, up, down)
        return
    above = side(lo[:, :128], hi[:, :128])[:HALO]
    below = side(lo[:, TR - 128 :], hi[:, TR - 128 :])[128 - HALO :]
    blocks = []
    for strip, coarse_part, beside in ((top, up, above), (bottom, down, below)):
        parts = [x.astype(F32) for x in pieces(coarse_part)] + [jnp.zeros((8, 128), F32)]
        parts += [strip[:, 128 * n : 128 * n + 128].astype(F32) for n in range(TC // 128)] + [beside]
        blocks.append(jnp.concatenate(parts, axis=0).astype(BF16))
    for p in range(NY):

        @pl.when(p < py)
        def _():
            send[p] = blocks[0]

        @pl.when(p >= py)
        def _():
            send[p] = blocks[1]


def across(first, extra, got, own, mgot, mown):
    rows, kind = (32 + HALO * (EC // 128), BF16) if first else (8, F32)
    return pl.pallas_call(
        functools.partial(across_kernel, first),
        in_specs=([VMEM] * 4 if first else [HBM]) + [VMEM] * 4,
        out_specs=[VMEM] * 2,
        out_shape=[pltpu.VMEM((NY, rows, 128), kind), pltpu.VMEM((80, 128), F32)],
        compiler_params=params(),
        name="across",
    )(*[near(x) for x in extra], near(got), near(own), near(mgot), near(mown))


def column_pass(block, cols, half, at):
    tile = [block[:, 128 * n : 128 * (n + 1)] for n in range(EC // 128)]
    join = lambda *which: jnp.concatenate([tile[n] for n in which], axis=1)
    half[at, :256] = dot(join(4, 0, 1, 2), cols[...]).astype(BF16)
    half[at, 256:512] = dot(join(1, 2, 3, 4), cols[...]).astype(BF16)
    if half.shape[1] > TC:
        half[at, 512:] = dot(join(3, 4, 0), cols[:384, :128]).astype(BF16)


def first_half_kernel(tile, lo, hi, cols_far, half_far, sides, half, cols, sems, csem):
    load = pltpu.make_async_copy(cols_far, cols, csem)
    load.start()
    stores = []
    for n in range(TR // SB):
        rows, begin = slice(n * SB, (n + 1) * SB), HALO + n * SB
        beside = side(lo[:, rows], hi[:, rows]).astype(BF16)
        sides[rows] = beside
        if n == 0:
            load.wait()
        column_pass(jnp.concatenate([tile[rows], beside], axis=1), cols, half, slice(PAD + begin, PAD + begin + SB))
        at = pl.ds(PAD + begin, SB)
        stores.append(pltpu.make_async_copy(half.at[at], half_far.at[at], sems.at[n]))
        stores[-1].start()
    for copy in stores:
        copy.wait()


def half_cost():
    return pl.CostEstimate(flops=4 * ER * EC * EC, bytes_accessed=6 * ER * EC, transcendentals=0)


def first_half(tile, lo, hi):
    return pl.pallas_call(
        first_half_kernel,
        in_specs=[VMEM] * 3 + [HBM],
        out_specs=[HBM, VMEM],
        out_shape=[pltpu.HBM((ER + 2 * PAD, EC), BF16), pltpu.HBM((TR, EC - TC), BF16)],
        scratch_shapes=[pltpu.VMEM((ER + 2 * PAD, EC), BF16), pltpu.VMEM((512, 256), BF16), DMA((TR // SB,)), DMA],
        compiler_params=params(),
        cost_estimate=half_cost(),
        name="first_half",
    )(near(tile), near(lo), near(hi), far(jnp.asarray(fine_columns())))


def half_kernel(dose, cols_far, half, cols, csem):
    load = pltpu.make_async_copy(cols_far, cols, csem)
    load.start()
    fill_pads(half)
    load.wait()
    for b in range(NB):
        column_pass(dose[b * BLK : (b + 1) * BLK], cols, half, slice(PAD + b * BLK, PAD + (b + 1) * BLK))


def half_of(dose, lanes):
    return pl.pallas_call(
        half_kernel,
        in_specs=[VMEM, HBM],
        out_specs=VMEM,
        out_shape=pltpu.VMEM((ER + 2 * PAD, lanes), BF16),
        scratch_shapes=[pltpu.VMEM((512, 256), BF16), DMA],
        compiler_params=params(),
        cost_estimate=half_cost(),
        name="half",
    )(near(dose), far(jnp.asarray(fine_columns())))


def spread(received, part, matrix, cols):
    y = dot(matrix[...], jnp.concatenate([received, part[...]], axis=0), precision=EXACT)
    lane = lax.broadcasted_iota(jnp.int32, (QM, 128), 1)
    fourth = jnp.where(lane < 120, y[2 * QM : 3 * QM], jnp.where(lane == 120, y[3 * QM : 3 * QM + 1], 0.0))
    a, b, c = pieces(jnp.where(lane < 40, y[:QM], jnp.where(lane < 80, y[QM : 2 * QM], fourth)))
    return dot(a, cols) + dot(b, cols) + dot(c, cols)


def short_range(b, rows, half):
    return dot(rows[...], half[b * BLK : (b + 1) * BLK + 2 * PAD])


def update(b, old_rows, short, grid, out, skip):
    count, lanes = out.shape
    t = (lax.broadcasted_iota(jnp.int32, (8, lanes), 0).astype(F32) + 0.5) / 16.0
    for n in range(BLK // 16):
        row = b * BLK + 16 * n
        if not skip <= row < skip + count:
            continue
        at = row // 16
        a, m, c = (grid[at + k : at + k + 1] for k in range(3))
        back = jnp.concatenate([a + (t + 0.5) * (m - a), m + t * (c - m)], axis=0)
        full = 1.0 + (short[16 * n : 16 * n + 16] + back)
        out[row - skip : row - skip + 16] = (old_rows(row).astype(F32) * 2.0 / full).astype(out.dtype)


def step_kernel(first, got, part, matrix, cols, rpool, dose, half, *refs):
    if first:
        sides_far, fcols_far, out, send, own, rows, cpool, grid, sums, hbuf, sides, fcols, lsem, ssem, fsem = refs
        loads = [pltpu.make_async_copy(fcols_far, fcols, fsem)]
        at = pl.ds(PAD + HALO, TR)
        loads.append(pltpu.make_async_copy(half.at[at], hbuf.at[at], lsem))
        loads.append(pltpu.make_async_copy(sides_far, sides, ssem))
        for copy in loads:
            copy.start()
    else:
        out, send, own, rows, cpool, grid, sums = refs
        hbuf = half
    edge = {}
    fill_rows(rows)
    fill_pool(cpool)
    if first:
        parts = got[:, :32].astype(F32)
        received = parts[:, :8] + (parts[:, 8:16] + parts[:, 16:24])
    else:
        received = got[...]
    received = received.reshape(NY * 8, 128)
    grid[...] = spread(received, part, matrix, cols[...])
    if first:
        py = lax.axis_index("gy")
        fill_pads(hbuf)
        loads[0].wait()
        for row, p, real in (
            (0, jnp.maximum(py - 1, 0), py > 0),
            (ER - HALO, jnp.minimum(py + 1, NY - 1), py < NY - 1),
        ):
            tiles = [got[p, 32 + HALO * n : 32 + HALO * (n + 1)].astype(F32) for n in range(EC // 128)]
            values = jnp.where(real, jnp.concatenate(tiles, axis=1), 0.0).astype(BF16)
            edge[row] = values
            column_pass(values, fcols, hbuf, slice(PAD + row, PAD + row + HALO))
        for copy in loads[1:]:
            copy.wait()

    def old_rows(row):
        if row in edge:
            return edge[row]
        if first:
            at = slice(row - HALO, row - HALO + 16)
            return jnp.concatenate([dose[at], sides[at]], axis=1)
        return dose[row : row + 16]

    for b in range(NB):
        update(b, old_rows, short_range(b, rows, hbuf), grid, out, 0)
        pooled = dot(out[b * BLK : (b + 1) * BLK, :TC], cpool[...])
        pooled = jnp.sum(pooled.reshape(BLK // 16, 16, 128), axis=1)
        sums[16 * b : 16 * b + 16] = jnp.concatenate([pooled, jnp.zeros((16 - BLK // 16, 128), F32)], axis=0)
    pooled_out(sums[...], rpool, lax.axis_index("gx"), send, own)


def step(got, part, dose, half, ops, sides=None):
    first = sides is not None
    scratch = [
        pltpu.VMEM((BLK, BLK + 2 * PAD), BF16),
        pltpu.VMEM((TC, 128), BF16),
        pltpu.VMEM((QM, EC), F32),
        pltpu.VMEM((NB * 16, 128), F32),
    ]
    if first:
        scratch += [pltpu.VMEM((ER + 2 * PAD, EC), BF16), pltpu.VMEM((TR, EC - TC), BF16), pltpu.VMEM((512, 256), BF16)]
        scratch += [DMA] * 3
    return pl.pallas_call(
        functools.partial(step_kernel, first),
        in_specs=[VMEM] * 6 + ([HBM] * 3 if first else [VMEM]),
        out_specs=[VMEM] * 3,
        out_shape=[
            pltpu.VMEM((ER, EC), BF16),
            pltpu.HBM((NX, 8, 128), F32),
            pltpu.VMEM((32, 128), F32),
        ],
        scratch_shapes=scratch,
        input_output_aliases={} if first else {5: 0},
        compiler_params=params(),
        name="first_step" if first else "step",
    )(
        near(got), near(part), *[near(x) for x in ops], near(dose), far(half) if first else near(half),
        *([far(sides), far(jnp.asarray(fine_columns()))] if first else []),
    )


def finish_kernel(got, part, matrix, cols, dose, half, out, rows, made, grid, ssem):
    fill_rows(rows)
    grid[...] = spread(got[...].reshape(NY * 8, 128), part, matrix, cols[:, :TC])
    stores = []
    for b in range(NB):
        update(b, lambda row: dose[row : row + 16, :TC], short_range(b, rows, half), grid, made, HALO)
        begin, end = max(b * BLK - HALO, 0), min((b + 1) * BLK - HALO, TR)
        at = pl.ds(begin, end - begin)
        stores.append(pltpu.make_async_copy(made.at[at], out.at[at], ssem.at[b]))
        stores[-1].start()
    for copy in stores:
        copy.wait()


def finish(got, part, dose, half, ops):
    return pl.pallas_call(
        finish_kernel,
        in_specs=[VMEM] * 6,
        out_specs=HBM,
        out_shape=pltpu.HBM((TR, TC), F32),
        scratch_shapes=[
            pltpu.VMEM((BLK, BLK + 2 * PAD), BF16),
            pltpu.VMEM((TR, TC), F32),
            pltpu.VMEM((QM, TC), F32),
            DMA((NB,)),
        ],
        compiler_params=params(),
        name="finish",
    )(near(got), near(part), near(ops[0]), near(ops[1]), near(dose), near(half))


def shifted(x, axis, by):
    n = lax.axis_size(axis)
    return lax.ppermute(x, axis, [(i, i + by) for i in range(n) if 0 <= i + by < n])


def exchanged(x, axis):
    return lax.all_to_all(x, axis, 0, 0, tiled=True)


def local(classes, exponents, gain_field, level_table, level_weights):
    tile, top, bottom, lo, hi, send, own, mgot, mown, *ops = start(
        level_table, exponents, level_weights, classes, gain_field
    )
    left, right = shifted(hi, "gx", 1), shifted(lo, "gx", -1)
    got = exchanged(send, "gx")
    send, part = across(True, (top, bottom, left, right), got, own, mgot, mown)
    got = exchanged(send, "gy")
    half, sides = first_half(tile, left, right)
    dose, send, own = step(got, part, tile, half, ops, sides)
    for sweep in range(2, ITERS + 1):
        got = exchanged(send, "gx")
        half = half_of(dose, EC if sweep < ITERS else TC)
        send, part = across(False, (half,), got, own, mgot, mown)
        got = exchanged(send, "gy")
        if sweep < ITERS:
            dose, send, own = step(got, part, dose, half, ops)
    return finish(got, part, dose, half, ops)


def solution(mesh):
    in_specs = (P("gy", "gx"), P("gy", "gx"), P("gy", "gx"), P(), P())
    return jax.shard_map(local, mesh=mesh, in_specs=in_specs, out_specs=P("gy", "gx"), check_vma=False)
```
